128 devices in a mesh: dp: 4 (over z), ctx: 4 (over y), tp: 8 (over x, core).
Axes of the slice: x: 4, y: 4, z: 4, core: 2. Of those that a mesh axis runs over, the one named last changes fastest.
Arguments:
- hidden_states: bfloat16 [4, 1024, 1536], P('dp', 'ctx'), may hold values from -32 to 32
- norm_gain: bfloat16 [1536], P(('dp', 'ctx')), may hold values from 0.5 to 1.5
- gate_weight: bfloat16 [1536, 3072], P(('dp', 'ctx'), 'tp'), may hold values from -0.15625 to 0.15625
- value_weight: bfloat16 [1536, 3072], P(('dp', 'ctx'), 'tp'), may hold values from -0.15625 to 0.15625
- state_proj: bfloat16 [1536, 256], P(('dp', 'ctx')), may hold values from -0.15625 to 0.15625
- step_proj: bfloat16 [1536, 48], P(('dp', 'ctx'), 'tp'), may hold values from -0.15625 to 0.15625
- value_filter: bfloat16 [4, 3072], P(None, 'tp'), may hold values from -3 to 3
- value_offset: bfloat16 [3072], P('tp'), may hold values from -0.5 to 0.5
- state_filter: bfloat16 [4, 256], replicated, may hold values from -3 to 3
- state_offset: bfloat16 [256], replicated, may hold values from -0.5 to 0.5
- step_bias: float32 [48], P('tp'), may hold values from -4 to -3
- decay_log: float32 [48], P('tp'), may hold values from -12 to 0
- skip_gain: float32 [48], P('tp'), may hold values from 0.5 to 1.5
- gate_norm_gain: bfloat16 [3072], P('tp'), may hold values from 0.5 to 1.5
- out_weight: bfloat16 [3072, 1536], P('tp', ('dp', 'ctx')), may hold values from -0.109375 to 0.109375
- out_grad: bfloat16 [4, 1024, 1536], P('dp', 'ctx'), may hold values from -6 to 6
Outputs:
- block_out: bfloat16 [4, 1024, 1536], P('dp', 'ctx')
- grad_hidden_states: float32 [4, 1024, 1536], P('dp', 'ctx')
- grad_norm_gain: float32 [1536], P(('dp', 'ctx'))
- grad_gate_weight: float32 [1536, 3072], P(('dp', 'ctx'), 'tp')
- grad_value_weight: float32 [1536, 3072], P(('dp', 'ctx'), 'tp')
- grad_state_proj: float32 [1536, 256], P(('dp', 'ctx'))
- grad_step_proj: float32 [1536, 48], P(('dp', 'ctx'), 'tp')
- grad_value_filter: float32 [4, 3072], P(None, 'tp')
- grad_value_offset: float32 [3072], P('tp')
- grad_state_filter: float32 [4, 256], replicated
- grad_state_offset: float32 [256], replicated
- grad_step_bias: float32 [48], P('tp')
- grad_decay_log: float32 [48], P('tp')
- grad_skip_gain: float32 [48], P('tp')
- grad_gate_norm_gain: float32 [3072], P('tp')
- grad_out_weight: float32 [3072, 1536], P('tp', ('dp', 'ctx'))
The draws below stay inside these ranges and needn't reach their ends.
All inputs are finite; a program needn't handle non-finite values.
Results may differ from the reference program's by a relative error of at most 0.011.
Values may be sent and summed in bfloat16 or wider, within the bound.
No kernel may reach another device: no remote copies, remote signals or barrier semaphores. Data moves between devices by JAX's collectives and lax.ppermute only.
A program may use at most 64 MiB of HBM per device.

```python
import math
import jax
import jax.numpy as jnp
from jax import lax

D = 1536
INNER = 3072
HEAD = 64
STATE = 128
KERNEL = 4
HEADS = 48
BLOCK = 256
LENGTH = 1024
BATCH = 4


def draw_hidden_states(key, part):
    key = jax.random.fold_in(key, 3)
    base_key, row_key, col_key = jax.random.split(key, 3)
    full_shape = (BATCH, LENGTH, D)
    standard = jnp.clip(jax.random.normal(base_key, full_shape, jnp.float32), -4.0, 4.0)
    row_scale = jnp.exp(jax.random.uniform(row_key, (BATCH, LENGTH, 1), jnp.float32, -1.2, 1.1))
    col_scale = jnp.exp(jax.random.uniform(col_key, (1, 1, D), jnp.float32, -0.92, 0.92))
    return (standard * row_scale * col_scale).astype(jnp.bfloat16)


def draw_decay_log(key, part):
    key = jax.random.fold_in(key, 5)
    lowest = math.log(0.1 / LENGTH)
    highest = math.log(1.0 / 30.0)
    decay_rates = jnp.exp(jax.random.uniform(key, (HEADS,), jnp.float32, lowest, highest))
    return jnp.log(20.0 * decay_rates)


def block_scale(stream_key, shape, cuts, smallest, largest):
    level = 1.0
    for position, parts in cuts:
        heights = jax.random.uniform(jax.random.fold_in(jax.random.fold_in(stream_key, 6), position), (parts,), jnp.float32, smallest / len(cuts), largest / len(cuts))
        level = level * jnp.repeat(jnp.exp(heights), shape[position] // parts).reshape((-1,) + (1,) * (len(shape) - 1 - position))
    return level


def centred(own_key, shape, scale, limit, shards=(), dtype=jnp.bfloat16):
    array = jax.random.normal(own_key, shape, jnp.float32) * scale
    if len(shards) > 0:
        array = block_scale(own_key, shape, shards, -0.22, 0.18) * array
    return jnp.clip(array, min=-limit, max=limit).astype(dtype)


def setup_inputs(seed: int = 0) -> dict:
    key_of = jax.random.split(jax.random.key(seed), 17)
    hidden_states = draw_hidden_states(jax.random.fold_in(key_of[16], 71), 0)
    norm_gain = jnp.clip(1.0 + 0.1 * jax.random.normal(key_of[1], (D,), jnp.float32), 0.5, 1.5).astype(jnp.bfloat16)
    gate_weight = centred(key_of[2], (D, INNER), D ** -0.5, 0.15625, ((0, 16), (1, 8)))
    value_weight = centred(key_of[3], (D, INNER), D ** -0.5, 0.15625, ((0, 16), (1, 8)))
    state_proj = centred(key_of[4], (D, 2 * STATE), D ** -0.5, 0.15625, ((0, 16),))
    step_proj = centred(key_of[5], (D, HEADS), D ** -0.5, 0.15625, ((0, 16), (1, 8)))
    value_filter = centred(key_of[6], (KERNEL, INNER), 0.5, 3.0, ((1, 8),))
    value_offset = jnp.clip(jax.random.uniform(key_of[7], (INNER,), jnp.float32, -0.5, 0.5) * block_scale(key_of[7], (INNER,), ((0, 8),), -0.4, 0.0), -0.5, 0.5).astype(jnp.bfloat16)
    state_filter = centred(key_of[8], (KERNEL, 2 * STATE), 0.5, 3.0)
    state_offset = jnp.clip(jax.random.uniform(key_of[9], (2 * STATE,), jnp.float32, -0.5, 0.5), -0.5, 0.5).astype(jnp.bfloat16)
    step_bias = jnp.clip(-4.0 + 1.0 * jax.random.uniform(key_of[10], (HEADS,), jnp.float32) ** block_scale(key_of[10], (HEADS,), ((0, 8),), -0.2, 0.2), -4.0, -3.0)
    decay_log = draw_decay_log(jax.random.fold_in(key_of[16], 71), 0)
    skip_gain = jnp.clip(0.5 + 1.0 * jax.random.uniform(key_of[12], (HEADS,), jnp.float32) ** block_scale(key_of[12], (HEADS,), ((0, 8),), -0.2, 0.2), 0.5, 1.5)
    gate_norm_gain = jnp.clip(1.0 + 0.1 * jax.random.normal(key_of[13], (INNER,), jnp.float32), 0.5, 1.5).astype(jnp.bfloat16)
    out_weight = centred(key_of[14], (INNER, D), INNER ** -0.5, 0.109375, ((0, 8), (1, 16)))
    out_grad = centred(key_of[15], (BATCH, LENGTH, D), 1.0, 6.0, ((0, 4), (1, 4)))
    return {"hidden_states": hidden_states, "norm_gain": norm_gain, "gate_weight": gate_weight, "value_weight": value_weight, "state_proj": state_proj, "step_proj": step_proj, "value_filter": value_filter, "value_offset": value_offset, "state_filter": state_filter, "state_offset": state_offset, "step_bias": step_bias, "decay_log": decay_log, "skip_gain": skip_gain, "gate_norm_gain": gate_norm_gain, "out_weight": out_weight, "out_grad": out_grad}


@jax.custom_vjp
def low(v):
    return lax.optimization_barrier(v.astype(jnp.bfloat16)).astype(jnp.float32)

@jax.custom_vjp
def low_back(v):
    return v

def low_keep(v):
    return (low(v), None)

def low_pass(kept, grad):
    return (grad,)

def back_keep(v):
    return (v, None)

def back_low(kept, grad):
    return (low(grad),)
low.defvjp(low_keep, low_pass)
low_back.defvjp(back_keep, back_low)
EPSILON = 1e-05
PRECISE = lax.Precision.HIGHEST

def precise_dot(former, latter):
    return jnp.dot(former, latter, precision=PRECISE, preferred_element_type=jnp.float32)

def block_local(values, bmatrix, cmatrix, step_size, decay_rates):
    length = step_size.shape[1]
    log_decay = jnp.cumsum(-step_size * decay_rates[None, None, :], axis=1)
    row_index = lax.broadcasted_iota(jnp.int32, (length, length), 0)
    col_index = lax.broadcasted_iota(jnp.int32, (length, length), 1)
    causal = (row_index >= col_index)[None, :, :, None]
    spread = log_decay[:, :, None, :] - log_decay[:, None, :, :]
    decay_mask = jnp.where(causal, jnp.exp(jnp.where(causal, spread, 0.0)), 0.0)
    scores = jnp.einsum('ctn,csn->cts', cmatrix, bmatrix, precision=PRECISE)
    weighted = values * step_size[:, :, :, None]
    within = jnp.einsum('ctsh,cshp->cthp', scores[:, :, :, None] * decay_mask, weighted, precision=PRECISE)
    to_end = jnp.exp(log_decay[:, -1:, :] - log_decay)
    local_states = jnp.einsum('cshp,csn->chpn', weighted * to_end[:, :, :, None], bmatrix, precision=PRECISE)
    return (log_decay, within, local_states)

def filter_apply(padded, filters, biases):
    length = padded.shape[0] - filters.shape[0] + 1
    summed = biases[None, :] + jnp.zeros((length, filters.shape[1]), jnp.float32)
    for offset in range(filters.shape[0]):
        summed = summed + filters[offset][None, :] * padded[offset:offset + length]
    return jax.nn.silu(summed)

def sequence_forward(hidden_states, norm_gain, gate_weight, value_weight, state_proj, step_proj, value_filter, value_offset, state_filter, state_offset, step_bias, decay_log, skip_gain, gate_norm_gain, out_weight):
    inv_rms = lax.rsqrt(lax.optimization_barrier(jnp.mean(hidden_states * hidden_states, axis=1, keepdims=True)) + EPSILON)
    hidden_in = low(hidden_states * inv_rms * norm_gain[None, :])
    projected = low_back(precise_dot(hidden_in, jnp.concatenate([gate_weight, value_weight, state_proj, step_proj], 1)))
    gate_pre = projected[:, :INNER]
    filter_input = low(projected[:, INNER:2 * INNER + 2 * STATE])
    step_pre = projected[:, 2 * INNER + 2 * STATE:]
    padded = jnp.concatenate([jnp.zeros((KERNEL - 1, filter_input.shape[1]), jnp.float32), filter_input], 0)
    activated = filter_apply(padded, jnp.concatenate([value_filter, state_filter], 1), jnp.concatenate([value_offset, state_offset], 0))
    blocks = LENGTH // BLOCK
    values = activated[:, :INNER].reshape(blocks, BLOCK, HEADS, HEAD)
    bmatrix = activated[:, INNER:INNER + STATE].reshape(blocks, BLOCK, STATE)
    cmatrix = activated[:, INNER + STATE:].reshape(blocks, BLOCK, STATE)
    step_size = jax.nn.softplus(step_pre + step_bias[None, :]).reshape(blocks, BLOCK, HEADS)
    decay_rates = jnp.exp(decay_log)

    def block_step(current, pieces):
        values_now, bmatrix_now, cmatrix_now, step_now = pieces
        log_decay, within, local_states = block_local(values_now[None], bmatrix_now[None], cmatrix_now[None], step_now[None], decay_rates)
        across = jnp.einsum('tn,hpn->thp', cmatrix_now, current, precision=PRECISE) * jnp.exp(log_decay[0])[:, :, None]
        following = current * jnp.exp(log_decay[0, -1])[:, None, None] + local_states[0]
        return (following, within[0] + across)
    start = jnp.zeros((HEADS, HEAD, STATE), jnp.float32)
    ignored, outputs = lax.scan(jax.checkpoint(block_step), start, (values, bmatrix, cmatrix, step_size))
    mixed_heads = outputs + values * skip_gain[None, None, :, None]
    gated = mixed_heads.reshape(LENGTH, INNER) * jax.nn.silu(gate_pre)
    inv_gate = lax.rsqrt(lax.optimization_barrier(jnp.mean(gated * gated, axis=1, keepdims=True)) + EPSILON)
    normed_out = low(gated * inv_gate * gate_norm_gain[None, :])
    return hidden_states + precise_dot(normed_out, out_weight)

def reference(hidden_states, norm_gain, gate_weight, value_weight, state_proj, step_proj, value_filter, value_offset, state_filter, state_offset, step_bias, decay_log, skip_gain, gate_norm_gain, out_weight, out_grad):
    floats = [arg.astype(jnp.float32) for arg in (hidden_states, norm_gain, gate_weight, value_weight, state_proj, step_proj, value_filter, value_offset, state_filter, state_offset, step_bias, decay_log, skip_gain, gate_norm_gain, out_weight)]

    def forward(*arrays):
        return jax.vmap(sequence_forward, in_axes=(0,) + (None,) * 14)(*arrays)
    block_out, pullback = jax.vjp(forward, *floats)
    grads = pullback(out_grad.astype(jnp.float32))
    return (block_out.astype(jnp.bfloat16), grads[0], grads[1], grads[2], grads[3], grads[4], grads[5], grads[6], grads[7], grads[8], grads[9], grads[10], grads[11], grads[12], grads[13], grads[14])
```

```python
import jax
import jax.numpy as jnp
from jax import lax
from jax.experimental import pallas as pl
from jax.experimental.pallas import tpu as pltpu
from jax.sharding import PartitionSpec as P

F32 = jnp.float32
BF16 = jnp.bfloat16
HIGH = lax.Precision.HIGHEST
EPSILON = 1e-05
INNER = 3072
D = 1536
T = 256
RIM = 16
EXT = T + RIM
KERNEL = 4
HEADS = 6
WIDE = 384
STATE = 128
MIX = WIDE + 2 * STATE
FIRST = MIX + 128
ROWS = 96
SHARES = 16
HALF = 640
RIM_SLOTS = ((0, ROWS), (0, ROWS + RIM), (1, ROWS))
SHARE = T // 8
REST = ROWS + 16
PART = 32
STEP_LANE = 32
GAIN_LANE = STEP_LANE + HEADS
STATE_LANE = 64
TURNED = 384
VMEM_LIMIT = 16 * 2**20
VMEM_WHOLE = 65_500_000

VALUES, SLOPE = slice(0, WIDE), slice(WIDE, WIDE + MIX)
STEP, STEP_SLOPE, LOG_DECAY = slice(1024, 1152), slice(1152, 1280), slice(1280, 1408)
BMAT, CMAT, WEIGHTED = slice(0, 128), slice(128, 256), slice(256, 640)
GATE_PRE, GRAD_NORMED, WITHIN = slice(0, 384), slice(384, 768), slice(768, 1152)
INSIDE, MIXED = slice(0, 384), slice(384, 768)
NORMED, LOW_GATE = slice(0, 384), slice(384, 768)


def fuse(function, outputs, ids, *arrays, scratch=(), fetch=False, rim=False):
    count = len(arrays)
    shapes = [array.shape for array in arrays]
    if rim:
        shapes[-1] = (RIM, D)

    def body(*refs):
        if not fetch:
            function(*refs)
            return
        given, rest = refs[1 : 1 + count], refs[1 + count : -1 - count]
        held, done = refs[-1 - count : -1], refs[-1]
        given = list(given)
        if rim:
            given[-1] = given[-1].at[pl.ds(T - RIM, RIM)]
        copies = [
            pltpu.make_async_copy(source, target, done.at[i])
            for i, (source, target) in enumerate(zip(given, held))
        ]
        for copy in copies:
            copy.start()
        for copy in copies:
            copy.wait()
        function(refs[0], *held, *rest)

    buffers = [pltpu.VMEM(shape, dtype) for shape, dtype in scratch]
    if fetch:
        buffers += [pltpu.VMEM(shape, array.dtype) for shape, array in zip(shapes, arrays)]
        buffers += [pltpu.SemaphoreType.DMA((count,))]
    space = pltpu.HBM if fetch else pltpu.VMEM
    call = pl.pallas_call(
        body,
        out_shape=[jax.ShapeDtypeStruct(shape, dtype) for shape, dtype in outputs],
        in_specs=[pl.BlockSpec(memory_space=pltpu.SMEM)]
        + [pl.BlockSpec(memory_space=space) for _ in arrays],
        out_specs=[pl.BlockSpec(memory_space=pltpu.VMEM) for _ in outputs],
        scratch_shapes=buffers,
        compiler_params=pltpu.CompilerParams(vmem_limit_bytes=VMEM_WHOLE if fetch else VMEM_LIMIT),
        name=function.__name__,
    )
    return list(call(ids, *arrays))


def roll(array, shift, axis):
    return pltpu.roll(array, shift % array.shape[axis], axis)


def product(a, b, left, right):
    return lax.dot_general(
        a.astype(BF16),
        b.astype(BF16),
        (((left,), (right,)), ((), ())),
        preferred_element_type=F32,
    )


def dot(a, b):
    return product(a, b, 1, 0)


def dot_last(a, b):
    return product(a, b, 1, 1)


def dot_first(a, b):
    return product(a, b, 0, 0)


def exact(a, b, left, right):
    return lax.dot_general(
        a, b, (((left,), (right,)), ((), ())), preferred_element_type=F32, precision=HIGH
    )


def iota(shape, axis):
    return lax.broadcasted_iota(jnp.int32, shape, axis)


def flag(condition):
    return jnp.where(condition, 1.0, 0.0)


def silu_parts(array):
    sig = jax.nn.sigmoid(array)
    return array * sig, sig * (1.0 + array * (1.0 - sig))


def spread_heads(array):
    rows = array.shape[0]
    lower = iota((rows, 128), 1) < 64
    pieces = [
        jnp.where(lower, array[:, h : h + 1], array[:, h + 1 : h + 2]) for h in range(0, HEADS, 2)
    ]
    return jnp.concatenate(pieces, axis=1)


def head_sums(array):
    chosen = flag((iota((128, WIDE), 1) >> 6) == iota((128, WIDE), 0))
    return exact(array, chosen, 1, 1)


def gain_row(tail):
    return dot_last(flag(iota((8, 128), 1) == GAIN_LANE), tail)[0:1]


def unit_rows(rows):
    tokens = rows.astype(F32)
    inv = lax.rsqrt(jnp.mean(tokens * tokens, axis=1, keepdims=True) + EPSILON)
    return tokens * inv


def aligned(start, size):
    return pl.ds(pl.multiple_of(start, size), size)


def prepare(
    ids, value_weight, gate_weight, state_proj, step_proj, norm_gain, out_weight, rim, left, longer, right
):
    left[0] = value_weight[...]
    left[1] = gate_weight[...]
    longer[0, :ROWS] = value_weight[...]
    longer[1, :ROWS] = gate_weight[...]
    for chunk in range(4):
        start = ROWS + RIM * (chunk % 2)
        longer[chunk // 2, start : start + RIM] = rim[:, WIDE * chunk : WIDE * chunk + WIDE]
    right[0, :, : 2 * STATE] = state_proj[...]
    place = iota((HEADS, 128), 1) == STEP_LANE + iota((HEADS, 128), 0)
    tail = dot_first(step_proj[...], flag(place))
    tail = tail + dot_first(norm_gain[...], flag(iota((1, 128), 1) == GAIN_LANE))
    right[0, :, 2 * STATE :] = tail.astype(BF16)
    right[1] = out_weight[...]


def tabulate(
    ids, value_filter, state_filter, value_offset, state_offset, gate_gain, step_bias, decay_log, skip_gain,
    rim, hidden, consts, units,
):
    units[:RIM] = unit_rows(rim[...])
    units[RIM:] = unit_rows(hidden[...])
    consts[...] = jnp.zeros(consts.shape, F32)
    consts[:KERNEL, :WIDE] = value_filter[...].astype(F32)
    consts[:KERNEL, WIDE:MIX] = state_filter[...].astype(F32)
    consts[KERNEL : KERNEL + 1, :WIDE] = value_offset[...].astype(F32)
    consts[KERNEL : KERNEL + 1, WIDE:MIX] = state_offset[...].astype(F32)
    consts[5:6, :WIDE] = gate_gain[...].astype(F32)
    consts[6:7, :HEADS] = step_bias[...]
    consts[7:8, :HEADS] = decay_log[...]
    consts[8:9, :HEADS] = skip_gain[...]


def place_blocks(ids, left, right, which, target):
    line, ctx = ids[0, 0], ids[0, 1]

    def piece(side, far, near):
        if far == 2:
            return side[2][near, which] if near < 2 else side[3][near - 2, which]
        return side[far + far // 3][near, which]

    for far in range(4):
        for near in range(4):
            block = ((line - far) & 3) * 4 + ((ctx - near) & 3)
            target[aligned(block * ROWS, ROWS), :WIDE] = piece(left, far, near)
            block = ((line - near) & 3) * 4 + ((ctx - far) & 3)
            target[aligned(block * ROWS, ROWS), WIDE:] = piece(right, far, near)


def enter(
    ids, l0, l1, l2, l3, l4, r0, r1, r2, r3, r4, units, consts,
    weights, hidden_in, taken, wide, narrow, message,
):
    place_blocks(ids, (l0, l1, l2, l3, l4), (r0, r1, r2, r3, r4), 0, weights)
    gain = gain_row(weights[:, MIX:])
    hidden_in[...] = (units[...] * gain).astype(BF16)
    projected = dot(hidden_in[...], weights[...])
    inputs = projected[:, :MIX].astype(BF16)
    taken[...] = inputs
    inputs = inputs.astype(F32)
    filter_pre = consts[KERNEL : KERNEL + 1, :MIX]
    for tap in range(KERNEL):
        filter_pre = filter_pre + consts[tap : tap + 1, :MIX] * roll(inputs, KERNEL - 1 - tap, 0)[RIM:]
    activated, wide[:, SLOPE] = silu_parts(filter_pre)
    lanes = iota((T, 128), 1) < HEADS
    step_in = roll(projected[RIM:, MIX:], 128 - STEP_LANE, 1) + consts[6:7, :128]
    step_in = jnp.where(lanes, step_in, -100.0)
    step = jnp.maximum(step_in, 0.0) + jnp.log1p(jnp.exp(-jnp.abs(step_in)))
    step = jnp.where(lanes, step, 0.0)
    rate = jnp.exp(consts[7:8, :128])
    log_decay = exact(flag(iota((T, T), 0) >= iota((T, T), 1)), -step * rate, 1, 0)
    values = activated[:, :WIDE]
    weighted = (values * spread_heads(step)).astype(BF16)
    wide[:, VALUES] = values
    wide[:, STEP] = step
    wide[:, STEP_SLOPE] = jax.nn.sigmoid(step_in)
    wide[:, LOG_DECAY] = log_decay
    narrow[:, BMAT] = activated[:, WIDE : WIDE + STATE].astype(BF16)
    narrow[:, CMAT] = activated[:, WIDE + STATE :].astype(BF16)
    narrow[:, WEIGHTED] = weighted
    last = log_decay[T - 1 :]
    to_end = spread_heads(jnp.exp(last - log_decay))
    message[:STATE] = dot_first(narrow[:, BMAT], weighted.astype(F32) * to_end).astype(BF16)
    span = spread_heads(last)
    high = span.astype(BF16).astype(F32)
    line = iota((16, WIDE), 0)
    tail = jnp.where(line == 0, high, jnp.where(line == 1, span - high, 0.0))
    message[STATE:] = tail.astype(BF16)


def decays(log_decay, turned, head):
    gap = log_decay[:, head : head + 1] - turned[head : head + 1, :]
    return jnp.exp(jnp.where(iota((T, T), 0) >= iota((T, T), 1), gap, -1e30))


def pair_columns(pair):
    return slice(128 * pair, 128 * pair + 128)


def project(
    ids, l0, l1, l2, l3, l4, r0, r1, r2, r3, r4, hidden_in, cotangent, wide, narrow, gate_out, before
):
    place_blocks(ids, (l0, l1, l2, l3, l4), (r0, r1, r2, r3, r4), 1, gate_out)
    before[:, GATE_PRE] = dot(hidden_in[RIM:], gate_out[:, :WIDE])
    before[:, GRAD_NORMED] = dot(cotangent[...], gate_out[:, WIDE:])
    scores = dot_last(narrow[:, CMAT], narrow[:, BMAT])
    log_decay = wide[:, LOG_DECAY]
    turned = log_decay.T
    lower = iota((T, 128), 1) < 64
    weighted = narrow[:, WEIGHTED]
    for pair in range(HEADS // 2):
        part = weighted[:, pair_columns(pair)]
        one = dot(scores * decays(log_decay, turned, 2 * pair), part)
        two = dot(scores * decays(log_decay, turned, 2 * pair + 1), part)
        start = WITHIN.start + 128 * pair
        before[:, start : start + 128] = jnp.where(lower, one, two)


def mix(ids, m1, m2, m3, wide, narrow, consts, before, state, after, sums):
    me = ids[0, 1]
    total = jnp.zeros((STATE, WIDE), F32)
    gap = jnp.zeros((1, WIDE), F32)
    for back, message in enumerate((m1, m2, m3)):
        tail = message[STATE:].astype(F32)
        log = tail[0:1] + tail[1:2]
        state[STATE + 8 * back : STATE + 8 * back + 8] = jnp.broadcast_to(log, (8, WIDE))
        scale = jnp.exp(gap) * jnp.where(me > back, 1.0, 0.0)
        total = total + scale * message[:STATE].astype(F32)
        gap = gap + log
    state[:STATE] = total
    grown = spread_heads(jnp.exp(wide[:, LOG_DECAY]))
    inside = before[:, WITHIN] + dot(narrow[:, CMAT], total) * grown
    after[:, INSIDE] = inside
    whole = inside + wide[:, VALUES] * spread_heads(consts[8:9, :128])
    after[:, MIXED] = whole
    gate = before[:, GATE_PRE]
    gated = whole * gate * jax.nn.sigmoid(gate)
    ones = jnp.ones((8, WIDE), F32)
    squares = exact(ones, gated * gated, 1, 1)
    crosses = exact(ones, before[:, GRAD_NORMED] * consts[5:6, :WIDE] * gated, 1, 1)
    sums[...] = jnp.where(iota((8, T), 0) < 4, squares, crosses)


def gate_back(
    ids, s0, s1, s2, s3, after, before, consts, wide, narrow, gated_low, grad_mixed, grad_gain, sensitivity
):
    total = s0[...] + s1[...] + s2[...] + s3[...]
    columns = exact(total, flag(iota((8, 128), 0) == 4 * iota((8, 128), 1)), 0, 0)
    inv = lax.rsqrt(columns[:, 0:1] / INNER + EPSILON)
    cross = columns[:, 1:2]
    act, slope = silu_parts(before[:, GATE_PRE])
    mixed = after[:, MIXED]
    normed = mixed * act * inv
    scaled = consts[5:6, :WIDE]
    gated_low[:, NORMED] = (normed * scaled).astype(BF16)
    grads = before[:, GRAD_NORMED]
    grad_gain[...] = jnp.broadcast_to(jnp.sum(grads * normed, axis=0, keepdims=True), (8, WIDE))
    grad_gated = inv * (grads * scaled) - normed * (inv * inv * cross / INNER)
    own = grad_gated * act
    grad_mixed[...] = own
    gated_low[:, LOW_GATE] = (grad_gated * mixed * slope).astype(BF16)
    grown = spread_heads(jnp.exp(wide[:, LOG_DECAY]))
    sensitivity[...] = dot_first(narrow[:, CMAT], own * grown).astype(BF16)


def share_out(ids, source, keep, send):
    chip, core = ids[0, 2] >> 1, ids[0, 2] & 1
    for ahead in range(4):
        start = ((chip + ahead) & 3) * 2
        keep[ahead] = source[aligned((start + core) * SHARE, SHARE)]
        send[ahead] = source[aligned((start + 1 - core) * SHARE, SHARE)]


def middle(
    ids, hidden_in, gated_low, cotangent, gate_out, wide, narrow, grad_mixed, gate, out, grads, branch
):
    gate[...] = dot_first(hidden_in[RIM:], gated_low[:, LOW_GATE]).astype(BF16)
    out[...] = dot_first(cotangent[...], gated_low[:, NORMED]).astype(BF16)
    branch[...] = dot_last(gated_low[:, NORMED], gate_out[:, WIDE:]).astype(BF16)
    bmat, cmat, weighted = narrow[:, BMAT], narrow[:, CMAT], narrow[:, WEIGHTED]
    scores = dot_last(cmat, bmat)
    log_decay = wide[:, LOG_DECAY]
    turned = log_decay.T
    lower = iota((T, 128), 1) < 64
    grad_scores = jnp.zeros((T, T), F32)
    for pair in range(HEADS // 2):
        part = weighted[:, pair_columns(pair)]
        grad = grad_mixed[:, pair_columns(pair)]
        got = []
        for side in range(2):
            weights = decays(log_decay, turned, 2 * pair + side)
            got.append(dot_first(scores * weights, grad))
            own = jnp.where(lower, grad, 0.0) if side == 0 else jnp.where(lower, 0.0, grad)
            grad_scores = grad_scores + dot_last(own, part) * weights
        grads[:, pair_columns(pair)] = jnp.where(lower, got[0], got[1])
    grads[:, WIDE : WIDE + STATE] = dot_first(grad_scores, cmat)
    grads[:, WIDE + STATE :] = dot(grad_scores, bmat)


def leave(
    ids, g1, g2, g3, state, after, grad_mixed, grads, wide, narrow, consts, taken, grad_gain,
    low, keep, send, small, turned,
):
    me = ids[0, 1]
    end = jnp.zeros((STATE, WIDE), F32)
    gap = jnp.zeros((1, WIDE), F32)
    for ahead, message in enumerate((g1, g2, g3)):
        scale = jnp.exp(gap) * jnp.where(me + ahead < 3, 1.0, 0.0)
        end = end + scale * message[...].astype(F32)
        start = STATE + 8 * (2 - ahead)
        gap = gap + state[start : start + 1]
    step, step_slope, log_decay = wide[:, STEP], wide[:, STEP_SLOPE], wide[:, LOG_DECAY]
    values = wide[:, VALUES]
    last = log_decay[T - 1 :]
    to_end = spread_heads(jnp.exp(last - log_decay))
    weighted = narrow[:, WEIGHTED].astype(F32)
    own = grad_mixed[...]
    from_end = dot(narrow[:, BMAT], end) * to_end
    inputs = grads[:, :WIDE] + from_end
    from_b = grads[:, WIDE : WIDE + STATE] + dot_last(weighted * to_end, end)
    grown = spread_heads(jnp.exp(log_decay))
    from_c = grads[:, WIDE + STATE :] + dot_last(own * grown, state[:STATE])
    grad_log = head_sums(own.astype(BF16).astype(F32) * after[:, INSIDE] - weighted * inputs)
    at_end = jnp.sum(weighted * from_end, axis=0, keepdims=True) + jnp.exp(
        spread_heads(last)
    ) * jnp.sum(end * state[:STATE], axis=0, keepdims=True)
    at_end = head_sums(jnp.broadcast_to(at_end, (8, WIDE)))[0:1]
    grad_decay = exact(flag(iota((T, T), 0) <= iota((T, T), 1)), grad_log, 1, 0) + at_end
    rate = jnp.exp(consts[7:8, :128])
    grad_step = head_sums(values * inputs) - rate * grad_decay
    grad_step_pre = grad_step * step_slope
    grad_values = own * spread_heads(consts[8:9, :128]) + inputs * spread_heads(step)
    grad_pre = jnp.concatenate([grad_values, from_b, from_c], axis=1) * wide[:, SLOPE]
    before = taken[...].astype(F32)
    padded = jnp.concatenate([jnp.zeros((RIM, MIX), F32), grad_pre], axis=0)
    grad_input = jnp.zeros((EXT, MIX), F32)
    line = iota((8, MIX), 0)
    taps = jnp.where(line == KERNEL, jnp.sum(grad_pre, axis=0, keepdims=True), 0.0)
    for tap in range(KERNEL):
        shift = KERNEL - 1 - tap
        found = jnp.sum(grad_pre * roll(before, shift, 0)[RIM:], axis=0, keepdims=True)
        taps = jnp.where(line == tap, found, taps)
        grad_input = grad_input + consts[tap : tap + 1, :MIX] * roll(padded, -shift, 0)
    low[:, :WIDE] = grad_input[:, :WIDE].astype(BF16)
    low_step = jnp.concatenate([jnp.zeros((RIM, 128), F32), grad_step_pre], axis=0)
    low[:, WIDE:] = roll(low_step, STEP_LANE, 1).astype(BF16)
    rest = jnp.zeros((TURNED - EXT - 8, 2 * STATE), F32)
    turned[...] = jnp.concatenate([grad_input[:, WIDE:], taps[:, WIDE:], rest], axis=0).T
    share_out(ids, turned, keep, send)
    heads = (
        jnp.sum(grad_step_pre, axis=0, keepdims=True),
        -rate * jnp.sum(grad_decay * step, axis=0, keepdims=True),
        head_sums(jnp.broadcast_to(jnp.sum(own * values, axis=0, keepdims=True), (8, WIDE)))[0:1],
    )
    none = jnp.zeros((1, 128), F32)
    heads = jnp.concatenate([heads[0] + roll(heads[1], 64, 1), heads[2], none], axis=1)
    line = iota((8, WIDE), 0)
    small[...] = jnp.where(line == 5, grad_gain[...], jnp.where(line == 6, heads, taps[:, :WIDE]))


def pair_sum(ids, keep, got, *shares):
    for ahead, share in enumerate(shares):
        share[...] = (keep[ahead].astype(F32) + got[ahead].astype(F32)).astype(share.dtype)


def value_grads(ids, low, gated_low, weights, gate_out, hidden_in, value, head):
    value[...] = dot_first(hidden_in[...], low[:, :WIDE]).astype(BF16)
    part = dot_last(low[:, :WIDE], weights[:, :WIDE]) + dot_last(low[:, WIDE:], weights[:, MIX:])
    head[:RIM] = part[:RIM]
    head[RIM:] = part[RIM:] + dot_last(gated_low[:, LOW_GATE], gate_out[:, :WIDE])


def fold(small):
    pieces = []
    for chunk in range(6):
        piece = small[:, pair_columns(chunk // 2)]
        pieces.append(piece if chunk % 2 else roll(piece, 64, 1))
    folded = jnp.concatenate(pieces, axis=0)
    high = folded.astype(BF16).astype(F32)
    return jnp.concatenate([high, folded - high], axis=0)


def unfold(block):
    folded = block[:48] + block[48:]
    lower = iota((8, 128), 1) < 64
    pairs = []
    for pair in range(3):
        one, two = folded[16 * pair : 16 * pair + 8], folded[16 * pair + 8 : 16 * pair + 16]
        pairs.append(jnp.where(lower, roll(one, 64, 1), two))
    return jnp.concatenate(pairs, axis=1)


def tidy(block):
    folded = block[:48] + block[48:]
    high = folded.astype(BF16).astype(F32)
    parts = jnp.concatenate([high, folded - high], axis=0)
    return jnp.where(iota((ROWS, 128), 1) < 64, block, parts)


def late_grads(
    ids, t0, t1, t2, t3, low, small, head, weights, units, hidden_in, gate, out, value,
    whole, *targets
):
    targets, tail = targets[:-1], targets[-1]
    total = t0[...] + t1[...] + t2[...] + t3[...]
    low_turned = total.astype(BF16).astype(F32)
    straight = jnp.concatenate([total, jnp.zeros((128 - PART, TURNED), F32)], axis=0).T
    low_tail = low[:, WIDE:].astype(F32) + straight[:EXT]
    tiles = jnp.concatenate([low_turned] * 8, axis=0)
    tiles = jnp.where((iota((8 * PART, TURNED), 0) >> 5) == ids[0, 2], tiles, 0.0)
    part = head[...] + product(tiles, weights[:, WIDE:MIX], 0, 1)[:EXT]
    behind = part[:RIM].astype(BF16)
    whole[...] = part[RIM:].astype(BF16)
    terms = part * units[...]
    grads = dot_first(hidden_in[...], low_tail)
    grads = grads + dot_first(terms, flag(iota((EXT, 128), 1) == GAIN_LANE))
    tail[...] = grads.astype(BF16)
    own = straight[EXT : EXT + 8]
    row = jnp.concatenate([own[0:1] + roll(own[1:2], 64, 1), own[2:3] + roll(own[3:4], 64, 1), own[4:5]], axis=1)
    folded = fold(jnp.where(iota((8, WIDE), 0) == 7, row, small[...]))
    arrange(ids, gate, out, value, tail, folded, targets)
    for chunk, (slot, start) in enumerate(RIM_SLOTS):
        piece = behind[:, HALF * chunk : HALF * chunk + HALF]
        targets[8][slot, start : start + RIM, : piece.shape[1]] = piece


def arrange(ids, gate, out, value, tail, folded, targets):
    line, ctx = ids[0, 0], ids[0, 1]
    lanes = iota((ROWS, 128), 1) < 64

    def left(block):
        rows = aligned(block * ROWS, ROWS)
        return gate[rows], value[rows, :256]

    def right(block):
        rows = aligned(block * ROWS, ROWS)
        end = jnp.where(lanes, tail[rows].astype(F32), folded).astype(BF16)
        return out[rows], value[rows, 256:], end

    for far in range(4):
        for near in range(4):
            slot = far + far // 3
            place = near
            if far == 2 and near >= 2:
                slot, place = 3, near - 2
            start = 0
            for part in left(((line + far) & 3) * 4 + ((ctx + near) & 3)):
                targets[slot][place, :, start : start + part.shape[1]] = part
                start += part.shape[1]
            start = 0
            for part in right(((line + near) & 3) * 4 + ((ctx + far) & 3)):
                targets[5 + slot][place, :ROWS, start : start + part.shape[1]] = part
                start += part.shape[1]


def put(target, total, tailed):
    if tailed:
        target[:, : HALF - 128] = total[:, : HALF - 128].astype(BF16)
        target[:, HALF - 128 :] = tidy(total[:, HALF - 128 :]).astype(BF16)
    else:
        target[...] = total.astype(BF16)


def relay(ids, *refs):
    for side in range(2):
        one, three, first, second = refs[4 * side : 4 * side + 4]
        to_one, to_three = refs[10 + 2 * side : 12 + 2 * side]
        for near in range(4):
            if near < 2:
                total = one[near].astype(F32) + first[near].astype(F32)
                put(to_one.at[near], total, side)
                to_three[near] = three[near]
            else:
                total = three[near].astype(F32) + second[near - 2, :ROWS].astype(F32)
                put(to_three.at[near], total, side)
                to_one[near] = one[near]
    head, branch = refs[8:10]
    keep, send, whole = refs[14:]
    inside = jnp.where(ids[0, 1] < 3, 1.0, 0.0)
    whole[: T - RIM] = head[: T - RIM]
    for chunk, (slot, start) in enumerate(RIM_SLOTS):
        columns = slice(HALF * chunk, min(HALF * chunk + HALF, D))
        behind = refs[7][slot, start : start + RIM, : columns.stop - columns.start]
        total = head[T - RIM :, columns].astype(F32) + behind.astype(F32) * inside
        whole[T - RIM :, columns] = total.astype(BF16)
    chip, core = ids[0, 2] >> 1, ids[0, 2] & 1
    for ahead in range(4):
        start = ((chip + ahead) & 3) * 2
        for half, source in enumerate((whole, branch)):
            rows = slice(half * SHARE, half * SHARE + SHARE)
            keep[ahead, rows] = source[aligned((start + core) * SHARE, SHARE)]
            send[ahead, rows] = source[aligned((start + 1 - core) * SHARE, SHARE)]


def halfway(ids, *refs):
    for side in range(2):
        own, one, three = refs[3 * side : 3 * side + 3]
        for near in range(4):
            total = own[near].astype(F32) + one[near].astype(F32) + three[near].astype(F32)
            put(refs[7 + 4 * side + near], total, side)


def collect(
    ids, a0, a1, a2, a3, b0, b1, b2, b3, settled,
    grad_gate, grad_value, grad_out, grad_step, taps, offset, gain, bias, decay, skip, message, rest,
):
    left = sum(part[...].astype(F32) for part in (a0, a1, a2, a3))
    right = sum(part[...].astype(F32) for part in (b0, b1, b2, b3))
    grad_gate[...] = left[:, :WIDE]
    grad_out[...] = right[:, :WIDE]
    grad_value[:, :256] = left[:, WIDE:]
    grad_value[:, 256:] = right[:, WIDE : HALF - 128]
    total = right[:, HALF - 128 :]
    rest[:ROWS] = total
    small = unfold(total)
    state = small[7:8]
    rest[ROWS:] = jnp.zeros((REST - ROWS, 128), F32)
    for tap in range(KERNEL + 1):
        piece = state[:, pair_columns(tap // 2)]
        rest[ROWS + tap : ROWS + tap + 1] = piece if tap % 2 else roll(piece, 64, 1)
    picked = flag(iota((8, 128), 1) == STEP_LANE + iota((8, 128), 0))
    grad_step[...] = exact(picked, total, 1, 1)[:HEADS]
    message[: 2 * SHARE] = settled[...]
    for block in range(REST // 16):
        message[2 * SHARE :, pair_columns(block)] = rest[16 * block : 16 * block + 16].astype(BF16)
    taps[...] = small[:KERNEL]
    offset[...] = small[KERNEL : KERNEL + 1]
    gain[...] = small[5:6]
    bias[...] = small[6:7, :HEADS]
    decay[...] = small[6:7, 64 : 64 + HEADS]
    skip[...] = small[6:7, 128 : 128 + HEADS]


def finish(
    ids, a0, a1, a2, a3, b0, b1, b2, b3, cotangent,
    grad_hidden, block_out, grad_state, grad_gain, taps, offset, rest,
):
    chip, core = ids[0, 2] >> 1, ids[0, 2] & 1
    for far, pair in enumerate(((a0, b0), (a1, b1), (a2, b2), (a3, b3))):
        start = ((chip - far) & 3) * 2
        for place, piece in zip((start + core, start + 1 - core), pair):
            rows = aligned(place * SHARE, SHARE)
            grad_hidden[rows] = cotangent[rows].astype(F32) + piece[:SHARE].astype(F32)
            block_out[rows] = piece[SHARE : 2 * SHARE]
            for block in range(REST // 16):
                part = piece[2 * SHARE :, pair_columns(block)]
                rest[place, 16 * block : 16 * block + 16] = part.astype(F32)
    lanes = iota((REST, 128), 1) >> 5
    total = rest[0]
    for half in range(2):
        state = jnp.zeros((REST, 128), F32)
        small = jnp.zeros((REST, 128), F32)
        for i in range(4):
            one = rest[4 * half + i]
            state = jnp.where(lanes == i, roll(one, PART * i, 1), state)
            small = jnp.where(lanes == i, roll(one, PART * i - STATE_LANE, 1), small)
            if half + i:
                total = total + one
        columns = pair_columns(half)
        grad_state[:, columns] = state[:ROWS]
        taps[:, columns] = small[ROWS : ROWS + KERNEL]
        offset[:, columns] = small[ROWS + KERNEL : ROWS + KERNEL + 1]
    grad_gain[...] = exact(flag(iota((8, 128), 1) == GAIN_LANE), total[:ROWS], 1, 1)[0:1]


def settle(ids, p0, p1, p2, p3, hidden, weights, settled):
    both = sum(part[...].astype(F32) for part in (p0, p1, p2, p3))
    mine = hidden[aligned(ids[0, 2] * SHARE, SHARE)].astype(F32)
    inv = lax.rsqrt(jnp.mean(mine * mine, axis=1, keepdims=True) + EPSILON)
    unit = mine * inv
    scaled = both[:SHARE] * gain_row(weights[:, MIX:])
    tokens = inv * (scaled - unit * jnp.mean(scaled * unit, axis=1, keepdims=True))
    settled[:SHARE] = tokens.astype(BF16)
    settled[SHARE:] = (mine + both[SHARE:]).astype(BF16)


def stack_blocks(ids, l0, l1, l2, l3, r0, r1, r2, r3, left, right, rim):
    for i, (one, two) in enumerate(((l0, r0), (l1, r1), (l2, r2), (l3, r3))):
        left[i] = one[:, :ROWS]
        right[i] = two[...]
    inside = jnp.where(ids[0, 1] > 0, 1.0, 0.0)
    for chunk in range(4):
        start = ROWS + RIM * (chunk % 2)
        piece = l1[chunk // 2, start : start + RIM].astype(F32) * inside
        rim[:, WIDE * chunk : WIDE * chunk + WIDE] = piece.astype(BF16)


def shift(array, axis, steps):
    return lax.ppermute(array, axis, [(i, (i + steps) % 4) for i in range(4)])


def from_chip(array, steps):
    return lax.ppermute(array, "tp", [(i, (i + 2 * steps) % 8) for i in range(8)])


def from_core(array):
    return lax.ppermute(array, "tp", [(i, i ^ 1) for i in range(8)])


def around(array, axis):
    return [array] + [shift(array, axis, steps) for steps in range(1, 4)]


def ring_sides(array, axis):
    return shift(array, axis, 1), shift(array, axis, 3)


def ring_rest(array, axis, one, three):
    return [array, one, shift(one[:2], axis, 1), shift(three[2:], axis, 3), three]


def chips_sum(ids, keep, send):
    outputs = [(keep.shape[1:], keep.dtype)] * 4
    pair = fuse(pair_sum, outputs, ids, keep, from_core(send))
    return [pair[0]] + [from_chip(pair[ahead], ahead) for ahead in range(1, 4)]


def chips_all(array):
    same = [array] + [from_chip(array, steps) for steps in range(1, 4)]
    return same + [from_core(one) for one in same]


def per_device(
    hidden_states,
    norm_gain,
    gate_weight,
    value_weight,
    state_proj,
    step_proj,
    value_filter,
    value_offset,
    state_filter,
    state_offset,
    step_bias,
    decay_log,
    skip_gain,
    gate_norm_gain,
    out_weight,
    out_grad,
):
    hidden = hidden_states[0]
    cotangent = out_grad[0]
    places = [lax.axis_index(axis).astype(jnp.int32) for axis in ("dp", "ctx", "tp")]
    ids = jnp.stack(places).reshape(1, 3)

    half = ((2, ROWS, WIDE), BF16)
    left, longer, right = fuse(
        prepare,
        [half, ((2, ROWS + 2 * RIM, WIDE), BF16), half],
        ids,
        value_weight,
        gate_weight,
        state_proj,
        step_proj.T,
        norm_gain[None],
        out_weight.T,
        hidden,
        fetch=True,
        rim=True,
    )
    near = [left, shift(longer, "ctx", 1), shift(left, "ctx", 2), shift(left, "ctx", 3)]
    left, right, rim = fuse(
        stack_blocks,
        [((4, 2, ROWS, WIDE), BF16)] * 2 + [((RIM, D), BF16)],
        ids,
        *near,
        *around(right, "dp"),
    )
    consts, units = fuse(
        tabulate,
        [((16, FIRST), F32), ((EXT, D), F32)],
        ids,
        value_filter,
        state_filter,
        value_offset[None],
        state_offset[None],
        gate_norm_gain[None],
        step_bias[None],
        decay_log[None],
        skip_gain[None],
        rim,
        hidden,
    )
    left = ring_rest(left, "dp", *ring_sides(left, "dp"))
    right = ring_rest(right, "ctx", *ring_sides(right, "ctx"))
    weights, hidden_in, taken, wide, narrow, message = fuse(
        enter,
        [
            ((D, FIRST), BF16),
            ((EXT, D), BF16),
            ((EXT, MIX), BF16),
            ((T, LOG_DECAY.stop), F32),
            ((T, WEIGHTED.stop), BF16),
            ((STATE + 16, WIDE), BF16),
        ],
        ids,
        *left,
        *right,
        units,
        consts,
    )
    messages = around(message, "ctx")[1:]
    gate_out, before = fuse(
        project,
        [((D, 2 * WIDE), BF16), ((T, WITHIN.stop), F32)],
        ids,
        *left,
        *right,
        hidden_in,
        cotangent,
        wide,
        narrow,
    )
    state, after, sums = fuse(
        mix,
        [((STATE + 24, WIDE), F32), ((T, MIXED.stop), F32), ((8, T), F32)],
        ids,
        *messages,
        wide,
        narrow,
        consts,
        before,
    )
    sums = sums + from_core(sums)
    gated_low, grad_mixed, grad_gain, sensitivity = fuse(
        gate_back,
        [
            ((T, LOW_GATE.stop), BF16),
            ((T, WIDE), F32),
            ((8, WIDE), F32),
            ((STATE, WIDE), BF16),
        ],
        ids,
        sums,
        *[from_chip(sums, steps) for steps in range(1, 4)],
        after,
        before,
        consts,
        wide,
        narrow,
    )
    later = [shift(sensitivity, "ctx", -steps) for steps in range(1, 4)]
    square = ((D, WIDE), BF16)
    gate, out, grads, branch = fuse(
        middle,
        [square, square, ((T, MIX), F32), ((T, D), BF16)],
        ids,
        hidden_in,
        gated_low,
        cotangent,
        gate_out,
        wide,
        narrow,
        grad_mixed,
    )
    low, turned_keep, turned_send, small = fuse(
        leave,
        [((EXT, WIDE + 128), BF16)] + [((4, PART, TURNED), F32)] * 2 + [((8, WIDE), F32)],
        ids,
        *later,
        state,
        after,
        grad_mixed,
        grads,
        wide,
        narrow,
        consts,
        taken,
        grad_gain,
        scratch=[((2 * STATE, TURNED), F32)],
    )
    value, head = fuse(
        value_grads,
        [square, ((EXT, D), F32)],
        ids,
        low,
        gated_low,
        weights,
        gate_out,
        hidden_in,
    )
    whole, part = ((4, ROWS, HALF), BF16), ((2, ROWS, HALF), BF16)
    longer = ((2, ROWS + 2 * RIM, HALF), BF16)
    head, *blocks = fuse(
        late_grads,
        [((T, D), BF16)] + [whole, whole, part, part, whole] + [whole, whole, part, longer, whole],
        ids,
        *chips_sum(ids, turned_keep, turned_send),
        low,
        small,
        head,
        weights,
        units,
        hidden_in,
        gate,
        out,
        value,
        scratch=[((D, 128), BF16)],
    )
    left, right = blocks[:5], blocks[5:]
    halves = []
    for side, axis in ((left, "dp"), (right, "ctx")):
        halves += [side[1], side[4], shift(side[2], axis, 1), shift(side[3], axis, 3)]
    *sides, head_keep, head_send = fuse(
        relay,
        [whole] * 4 + [((4, 2 * SHARE, D), BF16)] * 2,
        ids,
        *halves,
        head,
        branch,
        scratch=[((T, D), BF16)],
    )
    left = [left[0], shift(sides[0], "dp", 1), shift(sides[1], "dp", 3)]
    right = [right[0], shift(sides[2], "ctx", 1), shift(sides[3], "ctx", 3)]
    heads = chips_sum(ids, head_keep, head_send)
    sums = fuse(halfway, [((ROWS, HALF), BF16)] * 8, ids, *left, *right, heads[0])
    left = sums[:1] + [shift(sums[steps], "ctx", steps) for steps in range(1, 4)]
    right = sums[4:5] + [shift(sums[4 + steps], "dp", steps) for steps in range(1, 4)]
    (settled,) = fuse(settle, [((2 * SHARE, D), BF16)], ids, *heads, hidden, weights)
    few, line = ((1, HEADS), F32), ((1, WIDE), F32)
    grad_gate, grad_value, grad_out, grad_step, taps, offset, gain, bias, decay, skip, message = fuse(
        collect,
        [((ROWS, WIDE), F32)] * 3
        + [((HEADS, ROWS), F32), ((KERNEL, WIDE), F32)]
        + [line, line, few, few, few]
        + [((2 * SHARE + 16, D), BF16)],
        ids,
        *left,
        *right,
        settled,
        scratch=[((REST, 128), F32)],
    )
    grad_hidden, block_out, grad_state, grad_norm_gain, state_taps, state_offset = fuse(
        finish,
        [
            ((T, D), F32),
            ((T, D), BF16),
            ((ROWS, 2 * STATE), F32),
            ((1, ROWS), F32),
            ((KERNEL, 2 * STATE), F32),
            ((1, 2 * STATE), F32),
        ],
        ids,
        *chips_all(message),
        cotangent,
        scratch=[((8, REST, 128), F32)],
    )
    return (
        block_out[None],
        grad_hidden[None],
        grad_norm_gain[0],
        grad_gate,
        grad_value,
        grad_state,
        grad_step.T,
        taps,
        offset[0],
        state_taps,
        state_offset[0],
        bias[0],
        decay[0],
        skip[0],
        gain[0],
        grad_out.T,
    )


def solution(mesh):
    line = P(("dp", "ctx"))
    placed = (
        P("dp", "ctx", None),
        line,
        P(("dp", "ctx"), "tp"),
        P(("dp", "ctx"), "tp"),
        P(("dp", "ctx"), None),
        P(("dp", "ctx"), "tp"),
        P(None, "tp"),
        P("tp"),
        P(),
        P(),
        P("tp"),
        P("tp"),
        P("tp"),
        P("tp"),
        P("tp", ("dp", "ctx")),
        P("dp", "ctx", None),
    )
    given = (
        P("dp", "ctx", None),
        P("dp", "ctx", None),
        line,
        P(("dp", "ctx"), "tp"),
        P(("dp", "ctx"), "tp"),
        P(("dp", "ctx"), None),
        P(("dp", "ctx"), "tp"),
        P(None, "tp"),
        P("tp"),
        P(),
        P(),
        P("tp"),
        P("tp"),
        P("tp"),
        P("tp"),
        P("tp", ("dp", "ctx")),
    )
    return jax.shard_map(
        per_device, mesh=mesh, in_specs=placed, out_specs=given, check_vma=False
    )
```

```python
import jax
import jax.numpy as jnp
from jax import lax
from jax.experimental import pallas as pl
from jax.experimental.pallas import tpu as pltpu
from jax.sharding import PartitionSpec as P

F32 = jnp.float32
BF16 = jnp.bfloat16
HIGH = lax.Precision.HIGHEST
EPSILON = 1e-05
INNER = 3072
D = 1536
T = 256
RIM = 16
EXT = T + RIM
KERNEL = 4
HEADS = 6
WIDE = 384
STATE = 128
MIX = WIDE + 2 * STATE
FIRST = MIX + 128
ROWS = 96
SHARES = 16
NEAR = WIDE + WIDE + 128
FAR = MIX + 2 * WIDE - NEAR + 128
LEFT = 2 * WIDE
RIGHT = WIDE + 128
RIM_SLOTS = ((0, ROWS), (0, ROWS + RIM), (1, ROWS))
SHARE = T // 8
REST = ROWS + 16
PART = 32
STEP_LANE = 32
GAIN_LANE = STEP_LANE + HEADS
STATE_LANE = 64
TURNED = 384
VMEM_LIMIT = 16 * 2**20

VALUES, SLOPE = slice(0, WIDE), slice(WIDE, WIDE + MIX)
STEP, STEP_SLOPE, LOG_DECAY = slice(1024, 1152), slice(1152, 1280), slice(1280, 1408)
BMAT, CMAT, WEIGHTED = slice(0, 128), slice(128, 256), slice(256, 640)
GATE_PRE, GRAD_NORMED, WITHIN = slice(0, 384), slice(384, 768), slice(768, 1152)
INSIDE, MIXED = slice(0, 384), slice(384, 768)
NORMED, LOW_GATE = slice(0, 384), slice(384, 768)


def fuse(function, outputs, ids, *arrays, scratch=(), fetch=False, rim=False):
    count = len(arrays)
    shapes = [array.shape for array in arrays]
    if rim:
        shapes[-1] = (RIM, D)

    def body(*refs):
        if not fetch:
            function(*refs)
            return
        given, rest = refs[1 : 1 + count], refs[1 + count : -1 - count]
        held, done = refs[-1 - count : -1], refs[-1]
        given = list(given)
        if rim:
            given[-1] = given[-1].at[pl.ds(T - RIM, RIM)]
        copies = [
            pltpu.make_async_copy(source, target, done.at[i])
            for i, (source, target) in enumerate(zip(given, held))
        ]
        for copy in copies:
            copy.start()
        for copy in copies:
            copy.wait()
        function(refs[0], *held, *rest)

    buffers = [pltpu.VMEM(shape, dtype) for shape, dtype in scratch]
    if fetch:
        buffers += [pltpu.VMEM(shape, array.dtype) for shape, array in zip(shapes, arrays)]
        buffers += [pltpu.SemaphoreType.DMA((count,))]
    space = pltpu.HBM if fetch else pltpu.VMEM
    call = pl.pallas_call(
        body,
        out_shape=[jax.ShapeDtypeStruct(shape, dtype) for shape, dtype in outputs],
        in_specs=[pl.BlockSpec(memory_space=pltpu.SMEM)]
        + [pl.BlockSpec(memory_space=space) for _ in arrays],
        out_specs=[pl.BlockSpec(memory_space=pltpu.VMEM) for _ in outputs],
        scratch_shapes=buffers,
        compiler_params=pltpu.CompilerParams(vmem_limit_bytes=VMEM_LIMIT),
        name=function.__name__,
    )
    if fetch:
        arrays = [pltpu.with_memory_space_constraint(array, pltpu.HBM) for array in arrays]
    return list(call(ids, *arrays))


def roll(array, shift, axis):
    return pltpu.roll(array, shift % array.shape[axis], axis)


def product(a, b, left, right):
    return lax.dot_general(
        a.astype(BF16),
        b.astype(BF16),
        (((left,), (right,)), ((), ())),
        preferred_element_type=F32,
    )


def dot(a, b):
    return product(a, b, 1, 0)


def dot_last(a, b):
    return product(a, b, 1, 1)


def dot_first(a, b):
    return product(a, b, 0, 0)


def exact(a, b, left, right):
    return lax.dot_general(
        a, b, (((left,), (right,)), ((), ())), preferred_element_type=F32, precision=HIGH
    )


def iota(shape, axis):
    return lax.broadcasted_iota(jnp.int32, shape, axis)


def flag(condition):
    return jnp.where(condition, 1.0, 0.0)


def silu_parts(array):
    sig = jax.nn.sigmoid(array)
    return array * sig, sig * (1.0 + array * (1.0 - sig))


def spread_heads(array):
    rows = array.shape[0]
    lower = iota((rows, 128), 1) < 64
    pieces = [
        jnp.where(lower, array[:, h : h + 1], array[:, h + 1 : h + 2]) for h in range(0, HEADS, 2)
    ]
    return jnp.concatenate(pieces, axis=1)


def head_sums(array):
    chosen = flag((iota((128, WIDE), 1) >> 6) == iota((128, WIDE), 0))
    return exact(array, chosen, 1, 1)


def gain_row(tail):
    return dot_last(flag(iota((8, 128), 1) == GAIN_LANE), tail)[0:1]


def unit_rows(rows):
    tokens = rows.astype(F32)
    inv = lax.rsqrt(jnp.mean(tokens * tokens, axis=1, keepdims=True) + EPSILON)
    return tokens * inv


def aligned(start, size):
    return pl.ds(pl.multiple_of(start, size), size)


def prepare(
    ids, value_weight, gate_weight, state_proj, step_proj, norm_gain, out_weight, rim, left, longer, right
):
    for target in (left, longer):
        target[:ROWS, :WIDE] = value_weight[...]
        target[:ROWS, WIDE : 2 * WIDE] = gate_weight[...]
        target[:ROWS, 2 * WIDE :] = out_weight[:, :128]
    longer[ROWS : ROWS + RIM] = rim[:, :NEAR]
    longer[ROWS + RIM :, : D - NEAR] = rim[:, NEAR:]
    right[:, : 2 * STATE] = state_proj[...]
    place = iota((HEADS, 128), 1) == STEP_LANE + iota((HEADS, 128), 0)
    tail = dot_first(step_proj[...], flag(place))
    tail = tail + dot_first(norm_gain[...], flag(iota((1, 128), 1) == GAIN_LANE))
    right[:, 2 * STATE : WIDE] = tail.astype(BF16)
    right[:, WIDE:] = out_weight[:, 128:]


def tabulate(
    ids, value_filter, state_filter, value_offset, state_offset, gate_gain, heads, hidden, consts, units
):
    units[...] = unit_rows(hidden[...])
    consts[...] = jnp.zeros(consts.shape, F32)
    consts[:KERNEL, :WIDE] = value_filter[...].astype(F32)
    consts[:KERNEL, WIDE:MIX] = state_filter[...].astype(F32)
    consts[KERNEL : KERNEL + 1, :WIDE] = value_offset[...].astype(F32)
    consts[KERNEL : KERNEL + 1, WIDE:MIX] = state_offset[...].astype(F32)
    consts[5:6, :WIDE] = gate_gain[...].astype(F32)
    consts[6:9, :HEADS] = heads[...]


def place_blocks(ids, left, right, *moves):
    line, ctx = ids[0, 0], ids[0, 1]

    def piece(side, far, near):
        if far == 2:
            return (side[2], near) if near < 2 else (side[3], near - 2)
        return side[far + far // 3], near

    for far in range(4):
        for near in range(4):
            for target, side, start, source, size in moves:
                if side == 0:
                    block = ((line - far) & 3) * 4 + ((ctx - near) & 3)
                else:
                    block = ((line - near) & 3) * 4 + ((ctx - far) & 3)
                array, place = piece((left, right)[side], far, near)
                target[aligned(block * ROWS, ROWS), start : start + size] = array[
                    place, :, source : source + size
                ]


def enter(
    ids, l0, l1, l2, l3, l4, r0, r1, r2, r3, r4, rim, units, consts,
    weights, hidden_in, taken, wide, narrow, message,
):
    moves = (weights, 0, 0, 0, WIDE), (weights, 1, WIDE, 0, WIDE)
    place_blocks(ids, (l0, l1, l2, l3, l4), (r0, r1, r2, r3, r4), *moves)
    gain = gain_row(weights[:, MIX:])
    hidden_in[:RIM] = (unit_rows(rim[...]) * gain).astype(BF16)
    hidden_in[RIM:] = (units[...] * gain).astype(BF16)
    projected = dot(hidden_in[...], weights[...])
    inputs = projected[:, :MIX].astype(BF16)
    taken[...] = inputs
    inputs = inputs.astype(F32)
    filter_pre = consts[KERNEL : KERNEL + 1, :MIX]
    for tap in range(KERNEL):
        filter_pre = filter_pre + consts[tap : tap + 1, :MIX] * roll(inputs, KERNEL - 1 - tap, 0)[RIM:]
    activated, wide[:, SLOPE] = silu_parts(filter_pre)
    lanes = iota((T, 128), 1) < HEADS
    step_in = roll(projected[RIM:, MIX:], 128 - STEP_LANE, 1) + consts[6:7, :128]
    step_in = jnp.where(lanes, step_in, -100.0)
    step = jnp.maximum(step_in, 0.0) + jnp.log1p(jnp.exp(-jnp.abs(step_in)))
    step = jnp.where(lanes, step, 0.0)
    rate = jnp.exp(consts[7:8, :128])
    log_decay = exact(flag(iota((T, T), 0) >= iota((T, T), 1)), -step * rate, 1, 0)
    values = activated[:, :WIDE]
    weighted = (values * spread_heads(step)).astype(BF16)
    wide[:, VALUES] = values
    wide[:, STEP] = step
    wide[:, STEP_SLOPE] = jax.nn.sigmoid(step_in)
    wide[:, LOG_DECAY] = log_decay
    narrow[:, BMAT] = activated[:, WIDE : WIDE + STATE].astype(BF16)
    narrow[:, CMAT] = activated[:, WIDE + STATE :].astype(BF16)
    narrow[:, WEIGHTED] = weighted
    last = log_decay[T - 1 :]
    to_end = spread_heads(jnp.exp(last - log_decay))
    message[:STATE] = dot_first(narrow[:, BMAT], weighted.astype(F32) * to_end).astype(BF16)
    span = spread_heads(last)
    high = span.astype(BF16).astype(F32)
    line = iota((16, WIDE), 0)
    tail = jnp.where(line == 0, high, jnp.where(line == 1, span - high, 0.0))
    message[STATE:] = tail.astype(BF16)


def decays(log_decay, turned, head):
    gap = log_decay[:, head : head + 1] - turned[head : head + 1, :]
    return jnp.exp(jnp.where(iota((T, T), 0) >= iota((T, T), 1), gap, -1e30))


def pair_columns(pair):
    return slice(128 * pair, 128 * pair + 128)


def project(
    ids, l0, l1, l2, l3, l4, r0, r1, r2, r3, r4, hidden_in, cotangent, wide, narrow, gate_out, before
):
    moves = (gate_out, 0, 0, WIDE, WIDE + 128), (gate_out, 1, WIDE + 128, WIDE, WIDE - 128)
    place_blocks(ids, (l0, l1, l2, l3, l4), (r0, r1, r2, r3, r4), *moves)
    before[:, GATE_PRE] = dot(hidden_in[RIM:], gate_out[:, :WIDE])
    before[:, GRAD_NORMED] = dot(cotangent[...], gate_out[:, WIDE:])
    scores = dot_last(narrow[:, CMAT], narrow[:, BMAT])
    log_decay = wide[:, LOG_DECAY]
    turned = log_decay.T
    lower = iota((T, 128), 1) < 64
    weighted = narrow[:, WEIGHTED]
    for pair in range(HEADS // 2):
        part = weighted[:, pair_columns(pair)]
        one = dot(scores * decays(log_decay, turned, 2 * pair), part)
        two = dot(scores * decays(log_decay, turned, 2 * pair + 1), part)
        start = WITHIN.start + 128 * pair
        before[:, start : start + 128] = jnp.where(lower, one, two)


def mix(ids, m1, m2, m3, wide, narrow, consts, before, state, after, sums):
    me = ids[0, 1]
    total = jnp.zeros((STATE, WIDE), F32)
    gap = jnp.zeros((1, WIDE), F32)
    for back, message in enumerate((m1, m2, m3)):
        tail = message[STATE:].astype(F32)
        log = tail[0:1] + tail[1:2]
        state[STATE + 8 * back : STATE + 8 * back + 8] = jnp.broadcast_to(log, (8, WIDE))
        scale = jnp.exp(gap) * jnp.where(me > back, 1.0, 0.0)
        total = total + scale * message[:STATE].astype(F32)
        gap = gap + log
    state[:STATE] = total
    grown = spread_heads(jnp.exp(wide[:, LOG_DECAY]))
    inside = before[:, WITHIN] + dot(narrow[:, CMAT], total) * grown
    after[:, INSIDE] = inside
    whole = inside + wide[:, VALUES] * spread_heads(consts[8:9, :128])
    after[:, MIXED] = whole
    gate = before[:, GATE_PRE]
    gated = whole * gate * jax.nn.sigmoid(gate)
    ones = jnp.ones((8, WIDE), F32)
    squares = exact(ones, gated * gated, 1, 1)
    crosses = exact(ones, before[:, GRAD_NORMED] * consts[5:6, :WIDE] * gated, 1, 1)
    sums[...] = jnp.where(iota((8, T), 0) < 4, squares, crosses)


def gate_back(
    ids, s0, s1, s2, s3, after, before, consts, wide, narrow, gated_low, grad_mixed, grad_gain, sensitivity
):
    total = s0[...] + s1[...] + s2[...] + s3[...]
    columns = exact(total, flag(iota((8, 128), 0) == 4 * iota((8, 128), 1)), 0, 0)
    inv = lax.rsqrt(columns[:, 0:1] / INNER + EPSILON)
    cross = columns[:, 1:2]
    act, slope = silu_parts(before[:, GATE_PRE])
    mixed = after[:, MIXED]
    normed = mixed * act * inv
    scaled = consts[5:6, :WIDE]
    gated_low[:, NORMED] = (normed * scaled).astype(BF16)
    grads = before[:, GRAD_NORMED]
    grad_gain[...] = jnp.broadcast_to(jnp.sum(grads * normed, axis=0, keepdims=True), (8, WIDE))
    grad_gated = inv * (grads * scaled) - normed * (inv * inv * cross / INNER)
    own = grad_gated * act
    grad_mixed[...] = own
    gated_low[:, LOW_GATE] = (grad_gated * mixed * slope).astype(BF16)
    grown = spread_heads(jnp.exp(wide[:, LOG_DECAY]))
    sensitivity[...] = dot_first(narrow[:, CMAT], own * grown).astype(BF16)


def share_out(ids, source, keep, send):
    chip, core = ids[0, 2] >> 1, ids[0, 2] & 1
    for ahead in range(4):
        start = ((chip + ahead) & 3) * 2
        keep[ahead] = source[aligned((start + core) * SHARE, SHARE)]
        send[ahead] = source[aligned((start + 1 - core) * SHARE, SHARE)]


def middle(
    ids, hidden_in, gated_low, cotangent, gate_out, wide, narrow, grad_mixed, gate, out, grads, branch
):
    gate[...] = dot_first(hidden_in[RIM:], gated_low[:, LOW_GATE]).astype(BF16)
    out[...] = dot_first(cotangent[...], gated_low[:, NORMED]).astype(BF16)
    branch[...] = dot_last(gated_low[:, NORMED], gate_out[:, WIDE:]).astype(BF16)
    bmat, cmat, weighted = narrow[:, BMAT], narrow[:, CMAT], narrow[:, WEIGHTED]
    scores = dot_last(cmat, bmat)
    log_decay = wide[:, LOG_DECAY]
    turned = log_decay.T
    lower = iota((T, 128), 1) < 64
    grad_scores = jnp.zeros((T, T), F32)
    for pair in range(HEADS // 2):
        part = weighted[:, pair_columns(pair)]
        grad = grad_mixed[:, pair_columns(pair)]
        got = []
        for side in range(2):
            weights = decays(log_decay, turned, 2 * pair + side)
            got.append(dot_first(scores * weights, grad))
            own = jnp.where(lower, grad, 0.0) if side == 0 else jnp.where(lower, 0.0, grad)
            grad_scores = grad_scores + dot_last(own, part) * weights
        grads[:, pair_columns(pair)] = jnp.where(lower, got[0], got[1])
    grads[:, WIDE : WIDE + STATE] = dot_first(grad_scores, cmat)
    grads[:, WIDE + STATE :] = dot(grad_scores, bmat)


def leave(
    ids, g1, g2, g3, state, after, grad_mixed, grads, wide, narrow, consts, taken, grad_gain,
    low, state_low, keep, send, small, turned,
):
    me = ids[0, 1]
    end = jnp.zeros((STATE, WIDE), F32)
    gap = jnp.zeros((1, WIDE), F32)
    for ahead, message in enumerate((g1, g2, g3)):
        scale = jnp.exp(gap) * jnp.where(me + ahead < 3, 1.0, 0.0)
        end = end + scale * message[...].astype(F32)
        start = STATE + 8 * (2 - ahead)
        gap = gap + state[start : start + 1]
    step, step_slope, log_decay = wide[:, STEP], wide[:, STEP_SLOPE], wide[:, LOG_DECAY]
    values = wide[:, VALUES]
    last = log_decay[T - 1 :]
    to_end = spread_heads(jnp.exp(last - log_decay))
    weighted = narrow[:, WEIGHTED].astype(F32)
    own = grad_mixed[...]
    from_end = dot(narrow[:, BMAT], end) * to_end
    inputs = grads[:, :WIDE] + from_end
    from_b = grads[:, WIDE : WIDE + STATE] + dot_last(weighted * to_end, end)
    grown = spread_heads(jnp.exp(log_decay))
    from_c = grads[:, WIDE + STATE :] + dot_last(own * grown, state[:STATE])
    grad_log = head_sums(own.astype(BF16).astype(F32) * after[:, INSIDE] - weighted * inputs)
    at_end = jnp.sum(weighted * from_end, axis=0, keepdims=True) + jnp.exp(
        spread_heads(last)
    ) * jnp.sum(end * state[:STATE], axis=0, keepdims=True)
    at_end = head_sums(jnp.broadcast_to(at_end, (8, WIDE)))[0:1]
    grad_decay = exact(flag(iota((T, T), 0) <= iota((T, T), 1)), grad_log, 1, 0) + at_end
    rate = jnp.exp(consts[7:8, :128])
    grad_step = head_sums(values * inputs) - rate * grad_decay
    grad_step_pre = grad_step * step_slope
    grad_values = own * spread_heads(consts[8:9, :128]) + inputs * spread_heads(step)
    grad_pre = jnp.concatenate([grad_values, from_b, from_c], axis=1) * wide[:, SLOPE]
    before = taken[...].astype(F32)
    padded = jnp.concatenate([jnp.zeros((RIM, MIX), F32), grad_pre], axis=0)
    grad_input = jnp.zeros((EXT, MIX), F32)
    line = iota((8, MIX), 0)
    taps = jnp.where(line == KERNEL, jnp.sum(grad_pre, axis=0, keepdims=True), 0.0)
    for tap in range(KERNEL):
        shift = KERNEL - 1 - tap
        found = jnp.sum(grad_pre * roll(before, shift, 0)[RIM:], axis=0, keepdims=True)
        taps = jnp.where(line == tap, found, taps)
        grad_input = grad_input + consts[tap : tap + 1, :MIX] * roll(padded, -shift, 0)
    low[:, :WIDE] = grad_input[:, :WIDE].astype(BF16)
    state_low[...] = grad_input[:, WIDE:]
    low_step = jnp.concatenate([jnp.zeros((RIM, 128), F32), grad_step_pre], axis=0)
    low[:, WIDE:] = roll(low_step, STEP_LANE, 1).astype(BF16)
    rest = jnp.zeros((TURNED - EXT - 8, 2 * STATE), F32)
    turned[...] = jnp.concatenate([grad_input[:, WIDE:], taps[:, WIDE:], rest], axis=0).T
    share_out(ids, turned, keep, send)
    heads = (
        jnp.sum(grad_step_pre, axis=0, keepdims=True),
        -rate * jnp.sum(grad_decay * step, axis=0, keepdims=True),
        head_sums(jnp.broadcast_to(jnp.sum(own * values, axis=0, keepdims=True), (8, WIDE)))[0:1],
    )
    none = jnp.zeros((1, 128), F32)
    heads = jnp.concatenate([heads[0] + roll(heads[1], 64, 1), heads[2], none], axis=1)
    line = iota((8, WIDE), 0)
    small[...] = jnp.where(line == 5, grad_gain[...], jnp.where(line == 6, heads, taps[:, :WIDE]))


def two_parts(array):
    high = array.astype(BF16)
    return high, array - high.astype(F32)


def pair_sum(ids, keep, got, *shares):
    for ahead, share in enumerate(shares):
        share[...] = (keep[ahead].astype(F32) + got[ahead].astype(F32)).astype(share.dtype)


def value_grads(ids, low, state_low, gated_low, weights, gate_out, hidden_in, pair, value, head):
    value[...] = dot_first(hidden_in[...], low[:, :WIDE]).astype(BF16)
    part = dot_last(low[:, :WIDE], weights[:, :WIDE]) + dot_last(low[:, WIDE:], weights[:, MIX:])
    high, rest = two_parts(state_low[...])
    part = part + dot_last(high, weights[:, WIDE:MIX]) + dot_last(rest, weights[:, WIDE:MIX])
    head[:RIM] = part[:RIM]
    head[RIM:] = part[RIM:] + dot_last(gated_low[:, LOW_GATE], gate_out[:, :WIDE])


def fold(small):
    pieces = []
    for chunk in range(6):
        piece = small[:, pair_columns(chunk // 2)]
        pieces.append(piece if chunk % 2 else roll(piece, 64, 1))
    folded = jnp.concatenate(pieces, axis=0)
    high = folded.astype(BF16).astype(F32)
    return jnp.concatenate([high, folded - high], axis=0)


def unfold(block):
    folded = block[:48] + block[48:]
    lower = iota((8, 128), 1) < 64
    pairs = []
    for pair in range(3):
        one, two = folded[16 * pair : 16 * pair + 8], folded[16 * pair + 8 : 16 * pair + 16]
        pairs.append(jnp.where(lower, roll(one, 64, 1), two))
    return jnp.concatenate(pairs, axis=1)


def tidy(block):
    folded = block[:48] + block[48:]
    high = folded.astype(BF16).astype(F32)
    parts = jnp.concatenate([high, folded - high], axis=0)
    return jnp.where(iota((ROWS, 128), 1) < 64, block, parts)


def late_grads(
    ids, t0, t1, t2, t3, low, small, head, rim, units, hidden_in, gate, out, value, *targets
):
    targets, tail = targets[:-1], targets[-1]
    total = t0[...] + t1[...] + t2[...] + t3[...]
    straight = jnp.concatenate([total, jnp.zeros((128 - PART, TURNED), F32)], axis=0).T
    low_tail = low[:, WIDE:].astype(F32) + straight[:EXT]
    terms = jnp.concatenate([head[:RIM] * unit_rows(rim[...]), head[RIM:] * units[...]], axis=0)
    grads = dot_first(hidden_in[...], low_tail)
    grads = grads + dot_first(terms, flag(iota((EXT, 128), 1) == GAIN_LANE))
    tail[...] = grads.astype(BF16)
    own = straight[EXT : EXT + 8]
    row = jnp.concatenate([own[0:1] + roll(own[1:2], 64, 1), own[2:3] + roll(own[3:4], 64, 1), own[4:5]], axis=1)
    folded = fold(jnp.where(iota((8, WIDE), 0) == 7, row, small[...]))
    arrange(ids, gate, out, value, tail, folded, targets)
    for chunk, (slot, start) in enumerate(RIM_SLOTS):
        targets[8][slot, start : start + RIM] = head[:RIM, RIGHT * chunk : RIGHT * chunk + RIGHT].astype(
            BF16
        )

def arrange(ids, gate, out, value, tail, folded, targets):
    line, ctx = ids[0, 0], ids[0, 1]
    lanes = iota((ROWS, 128), 1) < 64
    for far in range(4):
        for near in range(4):
            slot, place = far + far // 3, near
            if far == 2 and near >= 2:
                slot, place = 3, near - 2
            block = ((line + far) & 3) * 4 + ((ctx + near) & 3)
            rows = aligned(block * ROWS, ROWS)
            targets[slot][place, :, :WIDE] = gate[rows]
            targets[slot][place, :, WIDE:] = value[rows]
            block = ((line + near) & 3) * 4 + ((ctx + far) & 3)
            rows = aligned(block * ROWS, ROWS)
            end = jnp.where(lanes, tail[rows].astype(F32), folded).astype(BF16)
            targets[5 + slot][place, :ROWS, :WIDE] = out[rows]
            targets[5 + slot][place, :ROWS, WIDE:] = end


def put(target, total, tailed):
    if tailed:
        target[:, :WIDE] = total[:, :WIDE].astype(BF16)
        target[:, WIDE:] = tidy(total[:, WIDE:]).astype(BF16)
    else:
        target[...] = total.astype(BF16)


def pair_halves(ids, keep, got, near, far):
    for other in range(4):
        target = far if other % 2 else near
        total = keep[other].astype(F32) + got[other].astype(F32)
        target[other // 2] = total.astype(BF16)


def pair_again(ids, near, got, own, second):
    for index, target in enumerate((own, second)):
        target[...] = (near[index].astype(F32) + got[index].astype(F32)).astype(BF16)


def relay(ids, *refs):
    for side in range(2):
        one, three, first, second = refs[4 * side : 4 * side + 4]
        to_one, to_three = refs[10 + 2 * side : 12 + 2 * side]
        for near in range(4):
            if near < 2:
                total = one[near].astype(F32) + first[near].astype(F32)
                put(to_one.at[near], total, side)
                to_three[near] = three[near]
            else:
                total = three[near].astype(F32) + second[near - 2, :ROWS].astype(F32)
                put(to_three.at[near], total, side)
                to_one[near] = one[near]
    head, branch = refs[8:10]
    keep, send, whole = refs[14:]
    inside = jnp.where(ids[0, 1] < 3, 1.0, 0.0)
    whole[: T - RIM] = head[RIM:T].astype(BF16)
    for chunk, (slot, start) in enumerate(RIM_SLOTS):
        columns = slice(RIGHT * chunk, RIGHT * chunk + RIGHT)
        behind = refs[7][slot, start : start + RIM].astype(F32) * inside
        whole[T - RIM :, columns] = (head[T:, columns] + behind).astype(BF16)
    chip, core = ids[0, 2] >> 1, ids[0, 2] & 1
    for other in range(4):
        start = (chip ^ other) * 2
        for half, source in enumerate((whole, branch)):
            rows = slice(half * SHARE, half * SHARE + SHARE)
            keep[other, rows] = source[aligned((start + core) * SHARE, SHARE)]
            send[other, rows] = source[aligned((start + 1 - core) * SHARE, SHARE)]


def halfway(ids, *refs):
    for side in range(2):
        own, one, three = refs[3 * side : 3 * side + 3]
        for near in range(4):
            total = own[near].astype(F32) + one[near].astype(F32) + three[near].astype(F32)
            put(refs[7 + 4 * side + near], total, side)


def collect(
    ids, a0, a1, a2, a3, b0, b1, b2, b3, settled,
    grad_gate, grad_value, grad_out, grad_step, taps, offset, gain, bias, decay, skip, message, rest,
):
    left = sum(part[...].astype(F32) for part in (a0, a1, a2, a3))
    right = sum(part[...].astype(F32) for part in (b0, b1, b2, b3))
    grad_gate[...] = left[:, :WIDE]
    grad_value[...] = left[:, WIDE:]
    grad_out[...] = right[:, :WIDE]
    total = right[:, WIDE:]
    rest[:ROWS] = total
    small = unfold(total)
    state = small[7:8]
    rest[ROWS:] = jnp.zeros((REST - ROWS, 128), F32)
    for tap in range(KERNEL + 1):
        piece = state[:, pair_columns(tap // 2)]
        rest[ROWS + tap : ROWS + tap + 1] = piece if tap % 2 else roll(piece, 64, 1)
    picked = flag(iota((8, 128), 1) == STEP_LANE + iota((8, 128), 0))
    grad_step[...] = exact(picked, total, 1, 1)[:HEADS]
    message[: 2 * SHARE] = settled[...]
    for block in range(REST // 16):
        message[2 * SHARE :, pair_columns(block)] = rest[16 * block : 16 * block + 16].astype(BF16)
    taps[...] = small[:KERNEL]
    offset[...] = small[KERNEL : KERNEL + 1]
    gain[...] = small[5:6]
    bias[...] = small[6:7, :HEADS]
    decay[...] = small[6:7, 64 : 64 + HEADS]
    skip[...] = small[6:7, 128 : 128 + HEADS]


def finish(
    ids, a0, a1, a2, a3, b0, b1, b2, b3, cotangent,
    grad_hidden, block_out, grad_state, grad_gain, taps, offset, rest,
):
    chip, core = ids[0, 2] >> 1, ids[0, 2] & 1
    for far, pair in enumerate(((a0, b0), (a1, b1), (a2, b2), (a3, b3))):
        start = ((chip - far) & 3) * 2
        for place, piece in zip((start + core, start + 1 - core), pair):
            rows = aligned(place * SHARE, SHARE)
            grad_hidden[rows] = cotangent[rows].astype(F32) + piece[:SHARE].astype(F32)
            block_out[rows] = piece[SHARE : 2 * SHARE]
            for block in range(REST // 16):
                part = piece[2 * SHARE :, pair_columns(block)]
                rest[place, 16 * block : 16 * block + 16] = part.astype(F32)
    lanes = iota((REST, 128), 1) >> 5
    total = rest[0]
    for half in range(2):
        state = jnp.zeros((REST, 128), F32)
        small = jnp.zeros((REST, 128), F32)
        for i in range(4):
            one = rest[4 * half + i]
            state = jnp.where(lanes == i, roll(one, PART * i, 1), state)
            small = jnp.where(lanes == i, roll(one, PART * i - STATE_LANE, 1), small)
            if half + i:
                total = total + one
        columns = pair_columns(half)
        grad_state[:, columns] = state[:ROWS]
        taps[:, columns] = small[ROWS : ROWS + KERNEL]
        offset[:, columns] = small[ROWS + KERNEL : ROWS + KERNEL + 1]
    grad_gain[...] = exact(flag(iota((8, 128), 1) == GAIN_LANE), total[:ROWS], 1, 1)[0:1]


def settle(ids, p0, p1, hidden, weights, settled):
    both = p0[...].astype(F32) + p1[...].astype(F32)
    mine = hidden[aligned(ids[0, 2] * SHARE, SHARE)].astype(F32)
    inv = lax.rsqrt(jnp.mean(mine * mine, axis=1, keepdims=True) + EPSILON)
    unit = mine * inv
    scaled = both[:SHARE] * gain_row(weights[:, MIX:])
    tokens = inv * (scaled - unit * jnp.mean(scaled * unit, axis=1, keepdims=True))
    settled[:SHARE] = tokens.astype(BF16)
    settled[SHARE:] = (mine + both[SHARE:]).astype(BF16)


def stack_blocks(ids, l0, l1, l2, l3, r0, r1, r2, r3, left, right, rim):
    for i, (one, two) in enumerate(((l0, r0), (l1, r1), (l2, r2), (l3, r3))):
        left[i] = one[:ROWS]
        right[i] = two[...]
    inside = jnp.where(ids[0, 1] > 0, 1.0, 0.0)
    rim[:, :NEAR] = (l1[ROWS : ROWS + RIM].astype(F32) * inside).astype(BF16)
    rim[:, NEAR:] = (l1[ROWS + RIM :, : D - NEAR].astype(F32) * inside).astype(BF16)


def shift(array, axis, steps):
    return lax.ppermute(array, axis, [(i, (i + steps) % 4) for i in range(4)])


def from_chip(array, steps):
    return lax.ppermute(array, "tp", [(i, (i + 2 * steps) % 8) for i in range(8)])


def across(array, bits):
    return lax.ppermute(array, "tp", [(i, i ^ bits) for i in range(8)])


def around(array, axis):
    return [array] + [shift(array, axis, steps) for steps in range(1, 4)]


def ring_sides(array, axis):
    return shift(array, axis, 1), shift(array, axis, 3)


def ring_rest(array, axis, one, three):
    return [array, one, shift(one[:2], axis, 1), shift(three[2:], axis, 3), three]


def chips_all(array):
    same = [array] + [from_chip(array, steps) for steps in range(1, 4)]
    return same + [across(one, 1) for one in same]


def per_device(
    hidden_states,
    norm_gain,
    gate_weight,
    value_weight,
    state_proj,
    step_proj,
    value_filter,
    value_offset,
    state_filter,
    state_offset,
    step_bias,
    decay_log,
    skip_gain,
    gate_norm_gain,
    out_weight,
    out_grad,
):
    hidden = hidden_states[0]
    cotangent = out_grad[0]
    places = [lax.axis_index(axis).astype(jnp.int32) for axis in ("dp", "ctx", "tp")]
    ids = jnp.stack(places).reshape(1, 3)

    left, longer, right = fuse(
        prepare,
        [((ROWS, NEAR), BF16), ((ROWS + 2 * RIM, NEAR), BF16), ((ROWS, FAR), BF16)],
        ids,
        value_weight,
        gate_weight,
        state_proj,
        step_proj.T,
        norm_gain[None],
        out_weight.T,
        hidden,
        fetch=True,
        rim=True,
    )
    near = [left, shift(longer, "ctx", 1), shift(left, "ctx", 2), shift(left, "ctx", 3)]
    left, right, rim = fuse(
        stack_blocks,
        [((4, ROWS, NEAR), BF16), ((4, ROWS, FAR), BF16), ((RIM, D), BF16)],
        ids,
        *near,
        *around(right, "dp"),
    )
    consts, units = fuse(
        tabulate,
        [((16, FIRST), F32), ((T, D), F32)],
        ids,
        value_filter,
        state_filter,
        value_offset[None],
        state_offset[None],
        gate_norm_gain[None],
        jnp.stack([step_bias, decay_log, skip_gain]),
        hidden,
        fetch=True,
    )
    left = ring_rest(left, "dp", *ring_sides(left, "dp"))
    right = ring_rest(right, "ctx", *ring_sides(right, "ctx"))
    weights, hidden_in, taken, wide, narrow, message = fuse(
        enter,
        [
            ((D, FIRST), BF16),
            ((EXT, D), BF16),
            ((EXT, MIX), BF16),
            ((T, LOG_DECAY.stop), F32),
            ((T, WEIGHTED.stop), BF16),
            ((STATE + 16, WIDE), BF16),
        ],
        ids,
        *left,
        *right,
        rim,
        units,
        consts,
    )
    messages = around(message, "ctx")[1:]
    gate_out, before = fuse(
        project,
        [((D, 2 * WIDE), BF16), ((T, WITHIN.stop), F32)],
        ids,
        *left,
        *right,
        hidden_in,
        cotangent,
        wide,
        narrow,
    )
    state, after, sums = fuse(
        mix,
        [((STATE + 24, WIDE), F32), ((T, MIXED.stop), F32), ((8, T), F32)],
        ids,
        *messages,
        wide,
        narrow,
        consts,
        before,
    )
    sums = sums + across(sums, 1)
    gated_low, grad_mixed, grad_gain, sensitivity = fuse(
        gate_back,
        [
            ((T, LOW_GATE.stop), BF16),
            ((T, WIDE), F32),
            ((8, WIDE), F32),
            ((STATE, WIDE), BF16),
        ],
        ids,
        sums,
        *[from_chip(sums, steps) for steps in range(1, 4)],
        after,
        before,
        consts,
        wide,
        narrow,
    )
    later = [shift(sensitivity, "ctx", -steps) for steps in range(1, 4)]
    square = ((D, WIDE), BF16)
    gate, out, grads, branch = fuse(
        middle,
        [square, square, ((T, MIX), F32), ((T, D), BF16)],
        ids,
        hidden_in,
        gated_low,
        cotangent,
        gate_out,
        wide,
        narrow,
        grad_mixed,
    )
    low, state_low, keep, send, small = fuse(
        leave,
        [((EXT, WIDE + 128), BF16), ((EXT, 2 * STATE), F32)] + [((4, PART, TURNED), F32)] * 2 + [((8, WIDE), F32)],
        ids,
        *later,
        state,
        after,
        grad_mixed,
        grads,
        wide,
        narrow,
        consts,
        taken,
        grad_gain,
        scratch=[((2 * STATE, TURNED), F32)],
    )
    pair = fuse(pair_sum, [((PART, TURNED), F32)] * 4, ids, keep, across(send, 1))
    turned = pair[:1] + [from_chip(pair[steps], steps) for steps in range(1, 4)]
    value, head = fuse(
        value_grads,
        [square, ((EXT, D), F32)],
        ids,
        low,
        state_low,
        gated_low,
        weights,
        gate_out,
        hidden_in,
        pair[0],
    )
    both = ((2 * SHARE, D), BF16)
    two = ((2, 2 * SHARE, D), BF16)

    def stage(count, rows, columns):
        return (count, rows, columns), BF16

    outputs = []
    for columns, rows in ((LEFT, ROWS), (RIGHT, ROWS + 2 * RIM)):
        whole = stage(4, ROWS, columns)
        outputs += [whole, whole, stage(2, ROWS, columns), stage(2, rows, columns), whole]
    blocks = fuse(
        late_grads,
        outputs,
        ids,
        *turned,
        low,
        small,
        head,
        rim,
        units,
        hidden_in,
        gate,
        out,
        value,
        scratch=[((D, 128), BF16)],
    )
    left, right = blocks[:5], blocks[5:]
    halves = []
    for side, axis in ((left, "dp"), (right, "ctx")):
        halves += [side[1], side[4], shift(side[2], axis, 1), shift(side[3], axis, 3)]
    *sides, keep, send = fuse(
        relay,
        [stage(4, ROWS, LEFT)] * 2 + [stage(4, ROWS, RIGHT)] * 2 + [((4, 2 * SHARE, D), BF16)] * 2,
        ids,
        *halves,
        head,
        branch,
        scratch=[((T, D), BF16)],
    )
    left = [left[0], shift(sides[0], "dp", 1), shift(sides[1], "dp", 3)]
    right = [right[0], shift(sides[2], "ctx", 1), shift(sides[3], "ctx", 3)]
    near, far = fuse(pair_halves, [two] * 2, ids, keep, across(send, 1))
    own, second = fuse(pair_again, [both] * 2, ids, near, across(far, 2))
    outputs = [((ROWS, LEFT), BF16)] * 4 + [((ROWS, RIGHT), BF16)] * 4
    sums = fuse(halfway, outputs, ids, *left, *right, own)
    left = sums[:1] + [shift(sums[steps], "ctx", steps) for steps in range(1, 4)]
    right = sums[4:5] + [shift(sums[4 + steps], "dp", steps) for steps in range(1, 4)]
    (settled,) = fuse(settle, [both], ids, own, across(second, 4), hidden, weights)
    few, line = ((1, HEADS), F32), ((1, WIDE), F32)
    grad_gate, grad_value, grad_out, grad_step, taps, offset, gain, bias, decay, skip, message = fuse(
        collect,
        [((ROWS, WIDE), F32)] * 3
        + [((HEADS, ROWS), F32), ((KERNEL, WIDE), F32)]
        + [line, line, few, few, few]
        + [((2 * SHARE + 16, D), BF16)],
        ids,
        *left,
        *right,
        settled,
        scratch=[((REST, 128), F32)],
    )
    grad_hidden, block_out, grad_state, grad_norm_gain, state_taps, state_offset = fuse(
        finish,
        [
            ((T, D), F32),
            ((T, D), BF16),
            ((ROWS, 2 * STATE), F32),
            ((1, ROWS), F32),
            ((KERNEL, 2 * STATE), F32),
            ((1, 2 * STATE), F32),
        ],
        ids,
        *chips_all(message),
        cotangent,
        scratch=[((8, REST, 128), F32)],
    )
    return (
        block_out[None],
        grad_hidden[None],
        grad_norm_gain[0],
        grad_gate,
        grad_value,
        grad_state,
        grad_step.T,
        taps,
        offset[0],
        state_taps,
        state_offset[0],
        bias[0],
        decay[0],
        skip[0],
        gain[0],
        grad_out.T,
    )


def solution(mesh):
    line = P(("dp", "ctx"))
    placed = (
        P("dp", "ctx", None),
        line,
        P(("dp", "ctx"), "tp"),
        P(("dp", "ctx"), "tp"),
        P(("dp", "ctx"), None),
        P(("dp", "ctx"), "tp"),
        P(None, "tp"),
        P("tp"),
        P(),
        P(),
        P("tp"),
        P("tp"),
        P("tp"),
        P("tp"),
        P("tp", ("dp", "ctx")),
        P("dp", "ctx", None),
    )
    given = (
        P("dp", "ctx", None),
        P("dp", "ctx", None),
        line,
        P(("dp", "ctx"), "tp"),
        P(("dp", "ctx"), "tp"),
        P(("dp", "ctx"), None),
        P(("dp", "ctx"), "tp"),
        P(None, "tp"),
        P("tp"),
        P(),
        P(),
        P("tp"),
        P("tp"),
        P("tp"),
        P("tp"),
        P("tp", ("dp", "ctx")),
    )
    return jax.shard_map(
        per_device, mesh=mesh, in_specs=placed, out_specs=given, check_vma=False
    )
```

```python
import jax
import jax.numpy as jnp
from jax import lax
from jax.experimental import pallas as pl
from jax.experimental.pallas import tpu as pltpu
from jax.sharding import PartitionSpec as P

F32 = jnp.float32
BF16 = jnp.bfloat16
EPSILON = 1e-05
INNER = 3072
D = 1536
T = 256
RIM = 16
EXT = T + RIM
KERNEL = 4
HEADS = 6
WIDE = 384
STATE = 128
MIX = WIDE + 2 * STATE
FIRST = MIX + 128
ROWS = 96
SHARES = 16
PAIR = 2 * WIDE
RIGHT = 512
OUT_RIGHT = RIGHT - 128
LEFT = 3 * WIDE - OUT_RIGHT
SHARE = T // 8
PART = 32
STEP_LANE = 32
GAIN_LANE = STEP_LANE + HEADS
STATE_LANE = 64
TURNED = 384
VMEM_LIMIT = 8 * 2**20

VALUES, SLOPE = slice(0, WIDE), slice(WIDE, WIDE + MIX)
STEP, STEP_SLOPE, LOG_DECAY = slice(1024, 1152), slice(1152, 1280), slice(1280, 1408)
BMAT, CMAT, WEIGHTED = slice(0, 128), slice(128, 256), slice(256, 640)
GATE_PRE, GRAD_NORMED, WITHIN = slice(0, 384), slice(384, 768), slice(768, 1152)
INSIDE, MIXED = slice(0, 384), slice(384, 768)
NORMED, LOW_GATE = slice(0, 384), slice(384, 768)
GROWN, TO_END, STEPS = slice(0, 384), slice(384, 768), slice(768, 1152)


WORK = {"pair_again": 2 * 10**9, "collect_left": 5 * 10**9}


def fuse(function, outputs, ids, *arrays, scratch=(), fetch=0, rim=False):
    count = len(arrays)
    plain = count - fetch
    shapes = [array.shape for array in arrays]
    if rim:
        shapes[-1] = (RIM, D)

    def body(*refs):
        if not fetch:
            function(*refs)
            return
        given = list(refs[1 + plain : 1 + count])
        held, done = refs[-1 - fetch : -1], refs[-1]
        if rim:
            given[-1] = given[-1].at[pl.ds(T - RIM, RIM)]
        copies = [
            pltpu.make_async_copy(source, target, done.at[i])
            for i, (source, target) in enumerate(zip(given, held))
        ]
        for copy in copies:
            copy.start()

        def ready():
            for copy in copies:
                copy.wait()

        function(*refs[: 1 + plain], *held, *refs[1 + count : -1 - fetch], ready=ready)

    buffers = [pltpu.VMEM(shape, dtype) for shape, dtype in scratch]
    spaces = [pltpu.SMEM] + [pltpu.VMEM] * plain + [pltpu.HBM] * fetch
    if fetch:
        buffers += [pltpu.VMEM(shapes[i], arrays[i].dtype) for i in range(plain, count)]
        buffers += [pltpu.SemaphoreType.DMA((fetch,))]
        held = [pltpu.with_memory_space_constraint(array, pltpu.HBM) for array in arrays[plain:]]
        arrays = (*arrays[:plain], *held)
    cost = None
    if function.__name__ in WORK:
        cost = pl.CostEstimate(
            flops=WORK[function.__name__], bytes_accessed=10**6, transcendentals=1
        )
    call = pl.pallas_call(
        body,
        out_shape=[jax.ShapeDtypeStruct(shape, dtype) for shape, dtype in outputs],
        in_specs=[pl.BlockSpec(memory_space=space) for space in spaces],
        out_specs=[pl.BlockSpec(memory_space=pltpu.VMEM) for _ in outputs],
        scratch_shapes=buffers,
        compiler_params=pltpu.CompilerParams(vmem_limit_bytes=VMEM_LIMIT),
        cost_estimate=cost,
        name=function.__name__,
    )
    return list(call(ids, *arrays))


def roll(array, shift, axis):
    return pltpu.roll(array, shift % array.shape[axis], axis)


def product(a, b, left, right):
    return lax.dot_general(
        a.astype(BF16),
        b.astype(BF16),
        (((left,), (right,)), ((), ())),
        preferred_element_type=F32,
    )


def dot(a, b):
    return product(a, b, 1, 0)


def dot_last(a, b):
    return product(a, b, 1, 1)


def dot_first(a, b):
    return product(a, b, 0, 0)


def split(array, count):
    parts = []
    for _ in range(count):
        part = array.astype(BF16)
        parts.append(part)
        array = array - part.astype(F32)
    return parts


def pick(chosen, array, left, right, parts=2):
    return sum(product(chosen, part, left, right) for part in split(array, parts))


def iota(shape, axis):
    return lax.broadcasted_iota(jnp.int32, shape, axis)


def flag(condition):
    return jnp.where(condition, 1.0, 0.0)


def silu_parts(array):
    sig = jax.nn.sigmoid(array)
    return array * sig, sig * (1.0 + array * (1.0 - sig))


def spread_heads(array):
    rows = array.shape[0]
    lower = iota((rows, 128), 1) < 64
    pieces = [
        jnp.where(lower, array[:, h : h + 1], array[:, h + 1 : h + 2]) for h in range(0, HEADS, 2)
    ]
    return jnp.concatenate(pieces, axis=1)


def head_sums(array):
    chosen = flag((iota((128, WIDE), 1) >> 6) == iota((128, WIDE), 0))
    return sum(dot_last(part, chosen) for part in split(array, 2))


def gain_row(tail):
    return dot_last(flag(iota((8, 128), 1) == GAIN_LANE), tail)[0:1]


def unit_rows(rows):
    tokens = rows.astype(F32)
    inv = lax.rsqrt(jnp.mean(tokens * tokens, axis=1, keepdims=True) + EPSILON)
    return tokens * inv


def aligned(start, size):
    return pl.ds(pl.multiple_of(start, size), size)


def prepare(
    ids, value_weight, gate_weight, state_proj, step_proj, norm_gain, out_weight, rim, left, longer, right, ready
):
    ready()
    for target in (left, longer):
        target[:ROWS, :WIDE] = value_weight[...]
        target[:ROWS, WIDE:] = gate_weight[...]
    last = rim[...].astype(F32)[8:]
    longer[ROWS:] = jnp.concatenate([last[:, :PAIR], last[:, PAIR:]], axis=0).astype(BF16)
    right[:, : 2 * STATE] = state_proj[...]
    place = iota((HEADS, 128), 1) == STEP_LANE + iota((HEADS, 128), 0)
    tail = dot_first(step_proj[...], flag(place))
    tail = tail + dot_first(norm_gain[...], flag(iota((1, 128), 1) == GAIN_LANE))
    right[:, 2 * STATE : WIDE] = tail.astype(BF16)
    right[:, WIDE:] = out_weight[...]


def tabulate(
    ids, value_filter, state_filter, value_offset, state_offset, gate_gain, heads, hidden, consts, units, ready
):
    ready()
    units[...] = unit_rows(hidden[...])
    consts[...] = jnp.zeros(consts.shape, F32)
    consts[:KERNEL, :WIDE] = value_filter[...].astype(F32)
    consts[:KERNEL, WIDE:MIX] = state_filter[...].astype(F32)
    consts[KERNEL : KERNEL + 1, :WIDE] = value_offset[...].astype(F32)
    consts[KERNEL : KERNEL + 1, WIDE:MIX] = state_offset[...].astype(F32)
    consts[5:6, :WIDE] = gate_gain[...].astype(F32)
    consts[6:9, :HEADS] = heads[...]


def place_blocks(ids, left, right, *moves):
    line, ctx = ids[0, 0], ids[0, 1]

    def piece(side, far, near):
        if far == 2:
            return (side[2], near) if near < 2 else (side[3], near - 2)
        return side[far + far // 3], near

    for far in range(4):
        for near in range(4):
            for target, side, start, source, size in moves:
                if side == 0:
                    block = ((line - far) & 3) * 4 + ((ctx - near) & 3)
                else:
                    block = ((line - near) & 3) * 4 + ((ctx - far) & 3)
                array, place = piece((left, right)[side], far, near)
                target[aligned(block * ROWS, ROWS), start : start + size] = array[
                    place, :, source : source + size
                ]


def enter(
    ids, l0, l1, l2, l3, l4, r0, r1, r2, r3, r4, rim, units, consts,
    weights, hidden_in, taken, wide, narrow, message,
):
    moves = (weights, 0, 0, 0, WIDE), (weights, 1, WIDE, 0, WIDE)
    place_blocks(ids, (l0, l1, l2, l3, l4), (r0, r1, r2, r3, r4), *moves)
    gain = gain_row(weights[:, MIX:])
    hidden_in[:RIM] = (unit_rows(rim[...]) * gain).astype(BF16)
    hidden_in[RIM:] = (units[...] * gain).astype(BF16)
    projected = dot(hidden_in[...], weights[...])
    inputs = projected[:, :MIX].astype(BF16)
    taken[...] = inputs
    inputs = inputs.astype(F32)
    filter_pre = consts[KERNEL : KERNEL + 1, :MIX]
    for tap in range(KERNEL):
        filter_pre = filter_pre + consts[tap : tap + 1, :MIX] * roll(inputs, KERNEL - 1 - tap, 0)[RIM:]
    wide[:, SLOPE] = filter_pre
    activated = filter_pre * jax.nn.sigmoid(filter_pre)
    lanes = iota((T, 128), 1) < HEADS
    step_in = roll(projected[RIM:, MIX:], 128 - STEP_LANE, 1) + consts[6:7, :128]
    step_in = jnp.where(lanes, step_in, -100.0)
    step = jnp.maximum(step_in, 0.0) + jnp.log1p(jnp.exp(-jnp.abs(step_in)))
    step = jnp.where(lanes, step, 0.0)
    rate = jnp.exp(consts[7:8, :128])
    log_decay = pick(flag(iota((T, T), 0) >= iota((T, T), 1)), -step * rate, 1, 0, 3)
    values = activated[:, :WIDE]
    weighted = (values * spread_heads(step)).astype(BF16)
    wide[:, VALUES] = values
    wide[:, STEP] = step
    wide[:, STEP_SLOPE] = jax.nn.sigmoid(step_in)
    wide[:, LOG_DECAY] = log_decay
    narrow[:, BMAT] = activated[:, WIDE : WIDE + STATE].astype(BF16)
    narrow[:, CMAT] = activated[:, WIDE + STATE :].astype(BF16)
    narrow[:, WEIGHTED] = weighted
    last = log_decay[T - 1 :]
    to_end = spread_heads(jnp.exp(last - log_decay))
    message[:STATE] = dot_first(narrow[:, BMAT], weighted.astype(F32) * to_end).astype(BF16)
    span = spread_heads(last)
    high = span.astype(BF16).astype(F32)
    line = iota((16, WIDE), 0)
    tail = jnp.where(line == 0, high, jnp.where(line == 1, span - high, 0.0))
    message[STATE:] = tail.astype(BF16)


def decays(log_decay, turned, head):
    gap = log_decay[:, head : head + 1] - turned[head : head + 1, :]
    return jnp.exp(jnp.where(iota((T, T), 0) >= iota((T, T), 1), gap, -1e30))


def pair_columns(pair):
    return slice(128 * pair, 128 * pair + 128)


def project(
    ids, l0, l1, l2, l3, l4, r0, r1, r2, r3, r4, hidden_in, cotangent, wide, narrow,
    gate_out, before, slope, spread,
):
    moves = (gate_out, 0, 0, WIDE, WIDE), (gate_out, 1, WIDE, WIDE, WIDE)
    place_blocks(ids, (l0, l1, l2, l3, l4), (r0, r1, r2, r3, r4), *moves)
    _, slope[...] = silu_parts(wide[:, SLOPE])
    last = wide[T - 1 :, LOG_DECAY]
    spread[:, GROWN] = spread_heads(jnp.exp(wide[:, LOG_DECAY]))
    spread[:, TO_END] = spread_heads(jnp.exp(last - wide[:, LOG_DECAY]))
    spread[:, STEPS] = spread_heads(wide[:, STEP])
    before[:, GATE_PRE] = dot(hidden_in[RIM:], gate_out[:, :WIDE])
    before[:, GRAD_NORMED] = dot(cotangent[...], gate_out[:, WIDE:])
    scores = dot_last(narrow[:, CMAT], narrow[:, BMAT])
    log_decay = wide[:, LOG_DECAY]
    turned = log_decay.T
    lower = iota((T, 128), 1) < 64
    weighted = narrow[:, WEIGHTED]
    for pair in range(HEADS // 2):
        part = weighted[:, pair_columns(pair)]
        one = dot(scores * decays(log_decay, turned, 2 * pair), part)
        two = dot(scores * decays(log_decay, turned, 2 * pair + 1), part)
        start = WITHIN.start + 128 * pair
        before[:, start : start + 128] = jnp.where(lower, one, two)


def mix(ids, m1, m2, m3, wide, spread, narrow, consts, before, state, after, sums):
    me = ids[0, 1]
    total = jnp.zeros((STATE, WIDE), F32)
    gap = jnp.zeros((1, WIDE), F32)
    for back, message in enumerate((m1, m2, m3)):
        tail = message[STATE:].astype(F32)
        log = tail[0:1] + tail[1:2]
        state[STATE + 8 * back : STATE + 8 * back + 8] = jnp.broadcast_to(log, (8, WIDE))
        scale = jnp.exp(gap) * jnp.where(me > back, 1.0, 0.0)
        total = total + scale * message[:STATE].astype(F32)
        gap = gap + log
    state[:STATE] = total
    inside = before[:, WITHIN] + dot(narrow[:, CMAT], total) * spread[:, GROWN]
    after[:, INSIDE] = inside
    whole = inside + wide[:, VALUES] * spread_heads(consts[8:9, :128])
    after[:, MIXED] = whole
    gate = before[:, GATE_PRE]
    gated = whole * gate * jax.nn.sigmoid(gate)
    ones = jnp.ones((8, WIDE), F32)
    squares = pick(ones, gated * gated, 1, 1)
    crosses = pick(ones, before[:, GRAD_NORMED] * consts[5:6, :WIDE] * gated, 1, 1)
    sums[...] = jnp.where(iota((8, T), 0) < 4, squares, crosses)


def gate_back(
    ids, s0, s1, s2, s3, after, before, consts, spread, narrow, gated_low, grad_mixed, grad_gain, sensitivity
):
    total = s0[...] + s1[...] + s2[...] + s3[...]
    chosen = flag(iota((8, 128), 0) == 4 * iota((8, 128), 1))
    columns = sum(dot_first(part, chosen) for part in split(total, 3))
    inv = lax.rsqrt(columns[:, 0:1] / INNER + EPSILON)
    cross = columns[:, 1:2]
    act, slope = silu_parts(before[:, GATE_PRE])
    mixed = after[:, MIXED]
    normed = mixed * act * inv
    scaled = consts[5:6, :WIDE]
    gated_low[:, NORMED] = (normed * scaled).astype(BF16)
    grads = before[:, GRAD_NORMED]
    grad_gain[...] = jnp.broadcast_to(jnp.sum(grads * normed, axis=0, keepdims=True), (8, WIDE))
    grad_gated = inv * (grads * scaled) - normed * (inv * inv * cross / INNER)
    own = grad_gated * act
    grad_mixed[...] = own
    gated_low[:, LOW_GATE] = (grad_gated * mixed * slope).astype(BF16)
    sensitivity[...] = dot_first(narrow[:, CMAT], own * spread[:, GROWN]).astype(BF16)


def turn_out(ids, source, keep, send):
    chip, core = ids[0, 2] >> 1, ids[0, 2] & 1
    for ahead in range(4):
        start = ((chip + ahead) & 3) * 2
        keep[ahead] = source[aligned((start + core) * SHARE, SHARE)]
        send[ahead] = source[aligned((start + 1 - core) * SHARE, SHARE)]


def middle(
    ids, hidden_in, gated_low, cotangent, gate_out, wide, narrow, grad_mixed, gate, out, grads, branch
):
    gate[...] = dot_first(hidden_in[RIM:], gated_low[:, LOW_GATE]).astype(BF16)
    out[...] = dot_first(cotangent[...], gated_low[:, NORMED]).astype(BF16)
    branch[...] = dot_last(gated_low[:, NORMED], gate_out[:, WIDE:]).astype(BF16)
    bmat, cmat, weighted = narrow[:, BMAT], narrow[:, CMAT], narrow[:, WEIGHTED]
    scores = dot_last(cmat, bmat)
    log_decay = wide[:, LOG_DECAY]
    turned = log_decay.T
    lower = iota((T, 128), 1) < 64
    grad_scores = jnp.zeros((T, T), F32)
    for pair in range(HEADS // 2):
        part = weighted[:, pair_columns(pair)]
        grad = grad_mixed[:, pair_columns(pair)]
        got = []
        for side in range(2):
            weights = decays(log_decay, turned, 2 * pair + side)
            got.append(dot_first(scores * weights, grad))
            own = jnp.where(lower, grad, 0.0) if side == 0 else jnp.where(lower, 0.0, grad)
            grad_scores = grad_scores + dot_last(own, part) * weights
        grads[:, pair_columns(pair)] = jnp.where(lower, got[0], got[1])
    grads[:, WIDE : WIDE + STATE] = dot_first(grad_scores, cmat)
    grads[:, WIDE + STATE :] = dot(grad_scores, bmat)


def leave(
    ids, g1, g2, g3, state, after, grad_mixed, grads, wide, spread, slope, narrow, consts, taken, grad_gain,
    low, state_low, keep, send, small, turned,
):
    me = ids[0, 1]
    end = jnp.zeros((STATE, WIDE), F32)
    gap = jnp.zeros((1, WIDE), F32)
    for ahead, message in enumerate((g1, g2, g3)):
        scale = jnp.exp(gap) * jnp.where(me + ahead < 3, 1.0, 0.0)
        end = end + scale * message[...].astype(F32)
        start = STATE + 8 * (2 - ahead)
        gap = gap + state[start : start + 1]
    step, step_slope = wide[:, STEP], wide[:, STEP_SLOPE]
    values = wide[:, VALUES]
    last = wide[T - 1 :, LOG_DECAY]
    to_end = spread[:, TO_END]
    weighted = narrow[:, WEIGHTED].astype(F32)
    own = grad_mixed[...]
    from_end = dot(narrow[:, BMAT], end) * to_end
    inputs = grads[:, :WIDE] + from_end
    from_b = grads[:, WIDE : WIDE + STATE] + dot_last(weighted * to_end, end)
    from_c = grads[:, WIDE + STATE :] + dot_last(own * spread[:, GROWN], state[:STATE])
    grad_log = head_sums(own.astype(BF16).astype(F32) * after[:, INSIDE] - weighted * inputs)
    at_end = jnp.sum(weighted * from_end, axis=0, keepdims=True) + jnp.exp(
        spread_heads(last)
    ) * jnp.sum(end * state[:STATE], axis=0, keepdims=True)
    at_end = head_sums(jnp.broadcast_to(at_end, (8, WIDE)))[0:1]
    grad_decay = pick(flag(iota((T, T), 0) <= iota((T, T), 1)), grad_log, 1, 0) + at_end
    rate = jnp.exp(consts[7:8, :128])
    grad_step = head_sums(values * inputs) - rate * grad_decay
    grad_step_pre = grad_step * step_slope
    grad_values = own * spread_heads(consts[8:9, :128]) + inputs * spread[:, STEPS]
    grad_pre = jnp.concatenate([grad_values, from_b, from_c], axis=1) * slope[...]
    before = taken[...].astype(F32)
    padded = jnp.concatenate([jnp.zeros((RIM, MIX), F32), grad_pre], axis=0)
    grad_input = jnp.zeros((EXT, MIX), F32)
    line = iota((8, MIX), 0)
    taps = jnp.where(line == KERNEL, jnp.sum(grad_pre, axis=0, keepdims=True), 0.0)
    for tap in range(KERNEL):
        later = roll(padded, tap + 1 - KERNEL, 0)
        taps = jnp.where(line == tap, jnp.sum(before * later, axis=0, keepdims=True), taps)
        grad_input = grad_input + consts[tap : tap + 1, :MIX] * later
    low[:, :WIDE] = grad_input[:, :WIDE].astype(BF16)
    state_low[...] = grad_input[:, WIDE:]
    low_step = jnp.concatenate([jnp.zeros((RIM, 128), F32), grad_step_pre], axis=0)
    low[:, WIDE:] = roll(low_step, STEP_LANE, 1).astype(BF16)
    rest = jnp.zeros((TURNED - EXT - 8, 2 * STATE), F32)
    turned[...] = jnp.concatenate([grad_input[:, WIDE:], taps[:, WIDE:], rest], axis=0).T
    turn_out(ids, turned, keep, send)
    heads = (
        jnp.sum(grad_step_pre, axis=0, keepdims=True),
        -rate * jnp.sum(grad_decay * step, axis=0, keepdims=True),
        head_sums(jnp.broadcast_to(jnp.sum(own * values, axis=0, keepdims=True), (8, WIDE)))[0:1],
    )
    none = jnp.zeros((1, 128), F32)
    heads = jnp.concatenate([heads[0] + roll(heads[1], 64, 1), heads[2], none], axis=1)
    line = iota((8, WIDE), 0)
    small[...] = jnp.where(line == 5, grad_gain[...], jnp.where(line == 6, heads, taps[:, :WIDE]))


def pair_sum(ids, keep, got, *shares):
    for ahead, share in enumerate(shares):
        share[...] = (keep[ahead].astype(F32) + got[ahead].astype(F32)).astype(share.dtype)


def value_grads(
    ids, low, state_low, gated_low, weights, gate_out, hidden_in, pair, value, head
):
    value[...] = dot_first(hidden_in[...], low[:, :WIDE]).astype(BF16)
    part = dot_last(low[:, :WIDE], weights[:, :WIDE]) + dot_last(low[:, WIDE:], weights[:, MIX:])
    high, rest = split(state_low[...], 2)
    part = part + dot_last(high, weights[:, WIDE:MIX]) + dot_last(rest, weights[:, WIDE:MIX])
    head[:RIM] = part[:RIM]
    head[RIM:] = part[RIM:] + dot_last(gated_low[:, LOW_GATE], gate_out[:, :WIDE])


def share_out(ids, head, branch, keep, send, whole):
    whole[...] = head[RIM:].astype(BF16)
    chip, core = ids[0, 2] >> 1, ids[0, 2] & 1
    for other in range(4):
        start = (chip ^ other) * 2
        for half, source in enumerate((whole, branch)):
            rows = slice(half * SHARE, half * SHARE + SHARE)
            keep[other, rows] = source[aligned((start + core) * SHARE, SHARE)]
            send[other, rows] = source[aligned((start + 1 - core) * SHARE, SHARE)]


def fold(small):
    pieces = []
    for chunk in range(6):
        piece = small[:, pair_columns(chunk // 2)]
        pieces.append(piece if chunk % 2 else roll(piece, 64, 1))
    folded = jnp.concatenate(pieces, axis=0)
    high = folded.astype(BF16).astype(F32)
    return jnp.concatenate([high, folded - high], axis=0)


def unfold(block):
    folded = block[:48] + block[48:]
    lower = iota((8, 128), 1) < 64
    pairs = []
    for pair in range(3):
        one, two = folded[16 * pair : 16 * pair + 8], folded[16 * pair + 8 : 16 * pair + 16]
        pairs.append(jnp.where(lower, roll(one, 64, 1), two))
    return jnp.concatenate(pairs, axis=1)


def tidy(block):
    folded = block[:48] + block[48:]
    high = folded.astype(BF16).astype(F32)
    parts = jnp.concatenate([high, folded - high], axis=0)
    return jnp.where(iota((ROWS, 128), 1) < 64, block, parts)


def late_grads(
    ids, t0, t1, t2, t3, low, small, head, rim, units, hidden_in, gate, out, value, branch, keep, send, *targets
):
    targets, tail, whole = targets[:-2], targets[-2], targets[-1]
    total = t0[...] + t1[...] + t2[...] + t3[...]
    straight = jnp.concatenate([total, jnp.zeros((128 - PART, TURNED), F32)], axis=0).T
    low_tail = low[:, WIDE:].astype(F32) + straight[:EXT]
    terms = jnp.sum(head[:RIM] * unit_rows(rim[...]), axis=0, keepdims=True)
    terms = terms + jnp.sum(head[RIM:] * units[...], axis=0, keepdims=True)
    grads = dot_first(hidden_in[...], low_tail)
    row = jnp.where(iota((8, D), 0) == 0, terms, 0.0)
    chosen = flag(iota((8, 128), 1) == GAIN_LANE)
    grads = grads + sum(dot_first(part, chosen) for part in split(row, 2))
    tail[...] = grads.astype(BF16)
    own = straight[EXT : EXT + 8]
    row = jnp.concatenate([own[0:1] + roll(own[1:2], 64, 1), own[2:3] + roll(own[3:4], 64, 1), own[4:5]], axis=1)
    folded = fold(jnp.where(iota((8, WIDE), 0) == 7, row, small[...]))
    lanes = iota((ROWS, 128), 1) < 64
    for target, place, block in places(ids, 0, targets[:5]):
        rows = aligned(block * ROWS, ROWS)
        target[place, :, :WIDE] = gate[rows]
        target[place, :, WIDE:] = value[rows]
    for target, place, block in places(ids, 1, targets[5:]):
        rows = aligned(block * ROWS, ROWS)
        target[place, :ROWS, :OUT_RIGHT] = out[rows]
        end = jnp.where(lanes, tail[rows].astype(F32), folded)
        target[place, :ROWS, OUT_RIGHT:] = end.astype(BF16)
    share_out(ids, head, branch, keep, send, whole)
    last = head[:RIM][8:]
    pieces = [last[:, RIGHT * chunk : RIGHT * chunk + RIGHT] for chunk in range(D // RIGHT)]
    pieces.append(jnp.zeros((8, RIGHT), F32))
    for slot in range(2):
        targets[8][slot, ROWS:] = jnp.concatenate(pieces[2 * slot : 2 * slot + 2], axis=0).astype(BF16)


def places(ids, side, targets):
    line, ctx = ids[0, 0], ids[0, 1]
    for far in range(4):
        for near in range(4):
            slot, place = far + far // 3, near
            if far == 2 and near >= 2:
                slot, place = 3, near - 2
            one, two = (near, far) if side else (far, near)
            yield targets[slot], place, ((line + one) & 3) * 4 + ((ctx + two) & 3)


def put(target, total, tailed):
    if tailed:
        target[:, :OUT_RIGHT] = total[:, :OUT_RIGHT].astype(BF16)
        target[:, OUT_RIGHT:] = tidy(total[:, OUT_RIGHT:]).astype(BF16)
    else:
        target[...] = total.astype(BF16)


def pair_halves(ids, keep, got, near, far):
    for other in range(4):
        target = far if other % 2 else near
        total = keep[other].astype(F32) + got[other].astype(F32)
        target[other // 2] = total.astype(BF16)


def relay(side, one, three, first, second, to_one, to_three):
    for near in range(4):
        if near < 2:
            total = one[near].astype(F32) + first[near].astype(F32)
            put(to_one.at[near], total, side)
            to_three[near] = three[near]
        else:
            total = three[near].astype(F32) + second[near - 2, :ROWS].astype(F32)
            put(to_three.at[near], total, side)
            to_one[near] = one[near]


def relay_both(ids, *refs):
    relay(0, *refs[:4], *refs[9:11])
    relay(1, *refs[4:8], *refs[11:13])
    second, behind = refs[7], refs[13]
    inside = jnp.where(ids[0, 1] < 3, 1.0, 0.0)
    for chunk in range(D // RIGHT):
        got = second[chunk // 2, ROWS:].astype(F32) * inside
        start = 8 * (chunk % 2)
        behind[:, RIGHT * chunk : RIGHT * chunk + RIGHT] = got[start : start + 8]


def halfway(side, own, one, three, *targets):
    for near, target in enumerate(targets):
        total = own[near].astype(F32) + one[near].astype(F32) + three[near].astype(F32)
        put(target, total, side)


def halfway_both(ids, l0, l1, l3, r0, r1, r3, own, *targets):
    halfway(0, l0, l1, l3, *targets[:4])
    halfway(1, r0, r1, r3, *targets[4:])


def pair_again(ids, near, got, cotangent, hidden, own, second, held, mine, last):
    for index, target in enumerate((own, second)):
        target[...] = (near[index].astype(F32) + got[index].astype(F32)).astype(BF16)
    held[...] = cotangent[...]
    mine[...] = hidden[aligned(ids[0, 2] * SHARE, SHARE)]
    last[...] = hidden[T - RIM :].astype(F32)[8:]


def collect_left(ids, a0, a1, a2, a3, b0, b1, b2, b3, grad_gate, grad_value, grad_out):
    total = sum(part[...].astype(F32) for part in (a0, a1, a2, a3))
    grad_gate[...] = total[:, :WIDE]
    grad_value[...] = total[:, WIDE:]
    grad_out[...] = sum(part[:, :OUT_RIGHT].astype(F32) for part in (b0, b1, b2, b3))


def hidden_back(grads, rows, gain):
    tokens = rows.astype(F32)
    inv = lax.rsqrt(jnp.mean(tokens * tokens, axis=1, keepdims=True) + EPSILON)
    unit = tokens * inv
    scaled = grads * gain
    return inv * (scaled - unit * jnp.mean(scaled * unit, axis=1, keepdims=True)), tokens


def gather_up(
    ids, b0, b1, b2, b3, p0, p1, mine, weights, behind,
    message, gain_out, grad_step, taps, offset, gain, bias, decay, skip, rest,
):
    both = p0[...].astype(F32) + p1[...].astype(F32)
    row = gain_row(weights[:, MIX:])
    gain_out[...] = jnp.broadcast_to(row, (8, D))
    grads, tokens = hidden_back(both[:SHARE], mine[...], row)
    message[:SHARE] = grads.astype(BF16)
    message[SHARE : 2 * SHARE] = (tokens + both[SHARE:]).astype(BF16)
    total = sum(part[:, OUT_RIGHT:].astype(F32) for part in (b0, b1, b2, b3))
    rest[...] = total
    small = unfold(total)
    state = small[7:8]
    lanes = iota((8, 128), 1)
    for tap in range(KERNEL + 1):
        piece = state[:, pair_columns(tap // 2)]
        piece = piece if tap % 2 == 0 else roll(piece, 64, 1)
        if tap == 0:
            rows = jnp.where(iota((8, 128), 0) == 0, roll(piece, STATE_LANE, 1), 0.0)
        else:
            rows = jnp.where(iota((8, 128), 0) == tap, roll(piece, STATE_LANE, 1), rows)
    rest[:8] = jnp.where(lanes < 64, rest[:8], rows)
    for block in range(ROWS // 16):
        message[2 * SHARE :, pair_columns(block)] = rest[16 * block : 16 * block + 16].astype(BF16)
    for block in range(6):
        pair = [behind[:, pair_columns(2 * block + i)] for i in range(2)]
        message[2 * SHARE :, pair_columns(6 + block)] = jnp.concatenate(pair, axis=0).astype(BF16)
    picked = flag(iota((8, 128), 1) == STEP_LANE + iota((8, 128), 0))
    grad_step[...] = pick(picked, total, 1, 1, 3)[:HEADS]
    taps[...] = small[:KERNEL]
    offset[...] = small[KERNEL : KERNEL + 1]
    gain[...] = small[5:6]
    bias[...] = small[6:7, :HEADS]
    decay[...] = small[6:7, 64 : 64 + HEADS]
    skip[...] = small[6:7, 128 : 128 + HEADS]


def finish(ids, *refs):
    pieces, row, cotangent, last = refs[:8], refs[8], refs[9], refs[10]
    grad_hidden, block_out, grad_state, grad_gain, taps, offset, rest, rims = refs[11:]
    chip, core = ids[0, 2] >> 1, ids[0, 2] & 1
    order = []
    for far in range(4):
        start = ((chip - far) & 3) * 2
        order += [(start + core, pieces[far]), (start + 1 - core, pieces[4 + far])]
    for place, piece in order:
        block_out[aligned(place * SHARE, SHARE)] = piece[SHARE : 2 * SHARE]
        for block in range(6):
            part = piece[2 * SHARE :, pair_columns(block)]
            rest[place, 16 * block : 16 * block + 16] = part.astype(F32)
            part = piece[2 * SHARE :, pair_columns(6 + block)].astype(F32)
            rims[place, :, pair_columns(2 * block)] = part[:8]
            rims[place, :, pair_columns(2 * block + 1)] = part[8:]
    total, behind = rest[0], rims[0]
    for i in range(1, 8):
        total = total + rest[i]
        behind = behind + rims[i]
    for place, piece in order:
        rows = aligned(place * SHARE, SHARE)
        grad_hidden[rows] = cotangent[rows].astype(F32) + piece[:SHARE].astype(F32)
    grads, _ = hidden_back(behind, last[...], row[0:1])
    grad_hidden[T - 8 :] = grad_hidden[T - 8 :] + grads
    lanes = iota((ROWS, 128), 1) >> 5
    for half in range(2):
        state = jnp.zeros((ROWS, 128), F32)
        small = jnp.zeros((8, 128), F32)
        for i in range(4):
            one = rest[4 * half + i]
            state = jnp.where(lanes == i, roll(one, PART * i, 1), state)
            small = jnp.where(lanes[:8] == i, roll(one[:8], PART * i - STATE_LANE, 1), small)
        columns = pair_columns(half)
        grad_state[:, columns] = state
        taps[:, columns] = small[:KERNEL]
        offset[:, columns] = small[KERNEL : KERNEL + 1]
    grad_gain[...] = pick(flag(iota((8, 128), 1) == GAIN_LANE), total, 1, 1, 3)[0:1]


def stack_blocks(ids, l0, l1, l2, l3, r0, r1, r2, r3, left, right, rim):
    for i, (one, two) in enumerate(((l0, r0), (l1, r1), (l2, r2), (l3, r3))):
        left[i] = one[:ROWS]
        right[i] = two[...]
    inside = jnp.where(ids[0, 1] > 0, 1.0, 0.0)
    got = l1[ROWS:].astype(F32) * inside
    none = jnp.zeros((8, PAIR), F32)
    rim[:, :PAIR] = jnp.concatenate([none, got[:8]], axis=0).astype(BF16)
    rim[:, PAIR:] = jnp.concatenate([none, got[8:]], axis=0).astype(BF16)


def shift(array, axis, steps):
    return lax.ppermute(array, axis, [(i, (i + steps) % 4) for i in range(4)])


def from_chip(array, steps):
    return lax.ppermute(array, "tp", [(i, (i + 2 * steps) % 8) for i in range(8)])


def across(array, bits):
    return lax.ppermute(array, "tp", [(i, i ^ bits) for i in range(8)])


def around(array, axis):
    return [array] + [shift(array, axis, steps) for steps in range(1, 4)]


def ring_sides(array, axis):
    return shift(array, axis, 1), shift(array, axis, 3)


def ring_rest(array, axis, one, three):
    return [array, one, shift(one[:2], axis, 1), shift(three[2:], axis, 3), three]


def chips_all(array):
    same = [array] + [from_chip(array, steps) for steps in range(1, 4)]
    return same + [across(one, 1) for one in same]


def per_device(
    hidden_states,
    norm_gain,
    gate_weight,
    value_weight,
    state_proj,
    step_proj,
    value_filter,
    value_offset,
    state_filter,
    state_offset,
    step_bias,
    decay_log,
    skip_gain,
    gate_norm_gain,
    out_weight,
    out_grad,
):
    hidden = hidden_states[0]
    cotangent = out_grad[0]
    places = [lax.axis_index(axis).astype(jnp.int32) for axis in ("dp", "ctx", "tp")]
    ids = jnp.stack(places).reshape(1, 3)

    left, longer, right = fuse(
        prepare,
        [((ROWS, PAIR), BF16), ((ROWS + RIM, PAIR), BF16), ((ROWS, PAIR), BF16)],
        ids,
        value_weight,
        gate_weight,
        state_proj,
        step_proj.T,
        norm_gain[None],
        out_weight.T,
        hidden,
        fetch=7,
        rim=True,
    )
    near = [left, shift(longer, "ctx", 1), shift(left, "ctx", 2), shift(left, "ctx", 3)]
    left, right, rim = fuse(
        stack_blocks,
        [((4, ROWS, PAIR), BF16)] * 2 + [((RIM, D), BF16)],
        ids,
        *near,
        *around(right, "dp"),
    )
    consts, units = fuse(
        tabulate,
        [((16, FIRST), F32), ((T, D), F32)],
        ids,
        value_filter,
        state_filter,
        value_offset[None],
        state_offset[None],
        gate_norm_gain[None],
        jnp.stack([step_bias, decay_log, skip_gain]),
        hidden,
        fetch=7,
    )
    left = ring_rest(left, "dp", *ring_sides(left, "dp"))
    right = ring_rest(right, "ctx", *ring_sides(right, "ctx"))
    weights, hidden_in, taken, wide, narrow, message = fuse(
        enter,
        [
            ((D, FIRST), BF16),
            ((EXT, D), BF16),
            ((EXT, MIX), BF16),
            ((T, LOG_DECAY.stop), F32),
            ((T, WEIGHTED.stop), BF16),
            ((STATE + 16, WIDE), BF16),
        ],
        ids,
        *left,
        *right,
        rim,
        units,
        consts,
    )
    messages = around(message, "ctx")[1:]
    gate_out, before, slope, spread = fuse(
        project,
        [((D, 2 * WIDE), BF16), ((T, WITHIN.stop), F32), ((T, MIX), F32), ((T, STEPS.stop), F32)],
        ids,
        *left,
        *right,
        hidden_in,
        cotangent,
        wide,
        narrow,
    )
    state, after, sums = fuse(
        mix,
        [((STATE + 24, WIDE), F32), ((T, MIXED.stop), F32), ((8, T), F32)],
        ids,
        *messages,
        wide,
        spread,
        narrow,
        consts,
        before,
    )
    sums = sums + across(sums, 1)
    gated_low, grad_mixed, grad_gain, sensitivity = fuse(
        gate_back,
        [
            ((T, LOW_GATE.stop), BF16),
            ((T, WIDE), F32),
            ((8, WIDE), F32),
            ((STATE, WIDE), BF16),
        ],
        ids,
        sums,
        *[from_chip(sums, steps) for steps in range(1, 4)],
        after,
        before,
        consts,
        spread,
        narrow,
    )
    later = [shift(sensitivity, "ctx", -steps) for steps in range(1, 4)]
    square = ((D, WIDE), BF16)
    gate, out, grads, branch = fuse(
        middle,
        [square, square, ((T, MIX), F32), ((T, D), BF16)],
        ids,
        hidden_in,
        gated_low,
        cotangent,
        gate_out,
        wide,
        narrow,
        grad_mixed,
    )
    low, state_low, keep, send, small = fuse(
        leave,
        [((EXT, WIDE + 128), BF16), ((EXT, 2 * STATE), F32)] + [((4, PART, TURNED), F32)] * 2 + [((8, WIDE), F32)],
        ids,
        *later,
        state,
        after,
        grad_mixed,
        grads,
        wide,
        spread,
        slope,
        narrow,
        consts,
        taken,
        grad_gain,
        scratch=[((2 * STATE, TURNED), F32)],
    )
    pair = fuse(pair_sum, [((PART, TURNED), F32)] * 4, ids, keep, across(send, 1))
    turned = pair[:1] + [from_chip(pair[steps], steps) for steps in range(1, 4)]
    value, head = fuse(
        value_grads,
        [square, ((EXT, D), F32)],
        ids,
        low,
        state_low,
        gated_low,
        weights,
        gate_out,
        hidden_in,
        pair[0],
    )
    both = ((2 * SHARE, D), BF16)
    two = ((2, 2 * SHARE, D), BF16)

    def stage(count, rows, columns):
        return (count, rows, columns), BF16

    def stages(columns, rows):
        whole = stage(4, ROWS, columns)
        return [whole, whole, stage(2, ROWS, columns), stage(2, rows, columns), whole]

    keep, send, *blocks = fuse(
        late_grads,
        [((4, 2 * SHARE, D), BF16)] * 2 + stages(LEFT, ROWS) + stages(RIGHT, ROWS + RIM),
        ids,
        *turned,
        low,
        small,
        head,
        rim,
        units,
        hidden_in,
        gate,
        out,
        value,
        branch,
        scratch=[((D, 128), BF16), ((T, D), BF16)],
    )
    left, right = blocks[:5], blocks[5:]
    near, far = fuse(pair_halves, [two] * 2, ids, keep, across(send, 1))
    *sides, behind = fuse(
        relay_both,
        [stage(4, ROWS, LEFT)] * 2 + [stage(4, ROWS, RIGHT)] * 2 + [((8, D), F32)],
        ids,
        *(left[1], left[4], shift(left[2], "dp", 1), shift(left[3], "dp", 3)),
        *(right[1], right[4], shift(right[2], "ctx", 1), shift(right[3], "ctx", 3)),
        near,
    )
    left = [left[0], shift(sides[0], "dp", 1), shift(sides[1], "dp", 3)]
    right = [right[0], shift(sides[2], "ctx", 1), shift(sides[3], "ctx", 3)]
    own, second, held, mine, last = fuse(
        pair_again,
        [both, both, ((T, D), BF16), ((SHARE, D), BF16), ((8, D), F32)],
        ids,
        near,
        across(far, 2),
        cotangent,
        hidden,
    )
    sums = fuse(
        halfway_both,
        [((ROWS, LEFT), BF16)] * 4 + [((ROWS, RIGHT), BF16)] * 4,
        ids,
        *left,
        *right,
        own,
    )
    left = sums[:1] + [shift(sums[steps], "ctx", steps) for steps in range(1, 4)]
    right = sums[4:5] + [shift(sums[4 + steps], "dp", steps) for steps in range(1, 4)]
    few, line = ((1, HEADS), F32), ((1, WIDE), F32)
    message, gain_full, *few_grads = fuse(
        gather_up,
        [((2 * SHARE + 16, D), BF16), ((8, D), F32), ((HEADS, ROWS), F32), ((KERNEL, WIDE), F32)]
        + [line, line, few, few, few],
        ids,
        *right,
        own,
        across(second, 4),
        mine,
        weights,
        behind,
        scratch=[((ROWS, 128), F32)],
    )
    grad_step, taps, offset, gain, bias, decay, skip = few_grads
    grad_gate, grad_value, grad_out = fuse(
        collect_left, [((ROWS, WIDE), F32)] * 3, ids, *left, *right
    )
    grad_hidden, block_out, grad_state, grad_norm_gain, state_taps, state_offset = fuse(
        finish,
        [
            ((T, D), F32),
            ((T, D), BF16),
            ((ROWS, 2 * STATE), F32),
            ((1, ROWS), F32),
            ((KERNEL, 2 * STATE), F32),
            ((1, 2 * STATE), F32),
        ],
        ids,
        *chips_all(message),
        gain_full,
        held,
        last,
        scratch=[((8, ROWS, 128), F32), ((8, 8, D), F32)],
    )
    return (
        block_out[None],
        grad_hidden[None],
        grad_norm_gain[0],
        grad_gate,
        grad_value,
        grad_state,
        grad_step.T,
        taps,
        offset[0],
        state_taps,
        state_offset[0],
        bias[0],
        decay[0],
        skip[0],
        gain[0],
        grad_out.T,
    )


def solution(mesh):
    line = P(("dp", "ctx"))
    placed = (
        P("dp", "ctx", None),
        line,
        P(("dp", "ctx"), "tp"),
        P(("dp", "ctx"), "tp"),
        P(("dp", "ctx"), None),
        P(("dp", "ctx"), "tp"),
        P(None, "tp"),
        P("tp"),
        P(),
        P(),
        P("tp"),
        P("tp"),
        P("tp"),
        P("tp"),
        P("tp", ("dp", "ctx")),
        P("dp", "ctx", None),
    )
    given = (
        P("dp", "ctx", None),
        P("dp", "ctx", None),
        line,
        P(("dp", "ctx"), "tp"),
        P(("dp", "ctx"), "tp"),
        P(("dp", "ctx"), None),
        P(("dp", "ctx"), "tp"),
        P(None, "tp"),
        P("tp"),
        P(),
        P(),
        P("tp"),
        P("tp"),
        P("tp"),
        P("tp"),
        P("tp", ("dp", "ctx")),
    )
    return jax.shard_map(
        per_device, mesh=mesh, in_specs=placed, out_specs=given, check_vma=False
    )
```

```python
import jax
import jax.numpy as jnp
from jax import lax
from jax.experimental import pallas as pl
from jax.experimental.pallas import tpu as pltpu
from jax.sharding import PartitionSpec as P

F32 = jnp.float32
BF16 = jnp.bfloat16
EPSILON = 1e-05
INNER = 3072
D = 1536
T = 256
RIM = 16
EXT = T + RIM
KERNEL = 4
HEADS = 6
WIDE = 384
STATE = 128
MIX = WIDE + 2 * STATE
FIRST = MIX + 128
ROWS = 96
SHARES = 16
PAIR = 2 * WIDE
RIGHT = 512
OUT_RIGHT = RIGHT - 128
LEFT = 3 * WIDE - OUT_RIGHT
SHARE = T // 8
PART = 32
STEP_LANE = 32
GAIN_LANE = STEP_LANE + HEADS
STATE_LANE = 64
TURNED = 384
VMEM_LIMIT = 8 * 2**20

VALUES, SLOPE = slice(0, WIDE), slice(WIDE, WIDE + MIX)
STEP, STEP_SLOPE, LOG_DECAY = slice(1024, 1152), slice(1152, 1280), slice(1280, 1408)
BMAT, CMAT, WEIGHTED = slice(0, 128), slice(128, 256), slice(256, 640)
GATE_PRE, GRAD_NORMED, WITHIN = slice(0, 384), slice(384, 768), slice(768, 1152)
INSIDE, MIXED = slice(0, 384), slice(384, 768)
NORMED, LOW_GATE = slice(0, 384), slice(384, 768)
GROWN, TO_END, STEPS = slice(0, 384), slice(384, 768), slice(768, 1152)


WORK = {"pair_again": 2 * 10**9, "collect_left": 5 * 10**9}


def fuse(function, outputs, ids, *arrays, scratch=(), fetch=0, rim=False):
    count = len(arrays)
    plain = count - fetch
    shapes = [array.shape for array in arrays]
    if rim:
        shapes[-1] = (RIM, D)

    def body(*refs):
        if not fetch:
            function(*refs)
            return
        given = list(refs[1 + plain : 1 + count])
        held, done = refs[-1 - fetch : -1], refs[-1]
        if rim:
            given[-1] = given[-1].at[pl.ds(T - RIM, RIM)]
        copies = [
            pltpu.make_async_copy(source, target, done.at[i])
            for i, (source, target) in enumerate(zip(given, held))
        ]
        for copy in copies:
            copy.start()

        def ready():
            for copy in copies:
                copy.wait()

        function(*refs[: 1 + plain], *held, *refs[1 + count : -1 - fetch], ready=ready)

    buffers = [pltpu.VMEM(shape, dtype) for shape, dtype in scratch]
    spaces = [pltpu.SMEM] + [pltpu.VMEM] * plain + [pltpu.HBM] * fetch
    if fetch:
        buffers += [pltpu.VMEM(shapes[i], arrays[i].dtype) for i in range(plain, count)]
        buffers += [pltpu.SemaphoreType.DMA((fetch,))]
        held = [pltpu.with_memory_space_constraint(array, pltpu.HBM) for array in arrays[plain:]]
        arrays = (*arrays[:plain], *held)
    cost = None
    if function.__name__ in WORK:
        cost = pl.CostEstimate(
            flops=WORK[function.__name__], bytes_accessed=10**6, transcendentals=1
        )
    call = pl.pallas_call(
        body,
        out_shape=[jax.ShapeDtypeStruct(shape, dtype) for shape, dtype in outputs],
        in_specs=[pl.BlockSpec(memory_space=space) for space in spaces],
        out_specs=[pl.BlockSpec(memory_space=pltpu.VMEM) for _ in outputs],
        scratch_shapes=buffers,
        compiler_params=pltpu.CompilerParams(vmem_limit_bytes=VMEM_LIMIT),
        cost_estimate=cost,
        name=function.__name__,
    )
    return list(call(ids, *arrays))


def roll(array, shift, axis):
    return pltpu.roll(array, shift % array.shape[axis], axis)


def product(a, b, left, right):
    return lax.dot_general(
        a.astype(BF16),
        b.astype(BF16),
        (((left,), (right,)), ((), ())),
        preferred_element_type=F32,
    )


def dot(a, b):
    return product(a, b, 1, 0)


def dot_last(a, b):
    return product(a, b, 1, 1)


def dot_first(a, b):
    return product(a, b, 0, 0)


def split(array, count):
    parts = []
    for _ in range(count):
        part = array.astype(BF16)
        parts.append(part)
        array = array - part.astype(F32)
    return parts


def twice(a, b, left, right):
    return sum(product(part, b, left, right) for part in split(a, 2))


def pick(chosen, array, left, right, parts=2):
    return sum(product(chosen, part, left, right) for part in split(array, parts))


def iota(shape, axis):
    return lax.broadcasted_iota(jnp.int32, shape, axis)


def flag(condition):
    return jnp.where(condition, 1.0, 0.0)


def silu_parts(array):
    sig = jax.nn.sigmoid(array)
    return array * sig, sig * (1.0 + array * (1.0 - sig))


def spread_heads(array):
    rows = array.shape[0]
    lower = iota((rows, 128), 1) < 64
    pieces = [
        jnp.where(lower, array[:, h : h + 1], array[:, h + 1 : h + 2]) for h in range(0, HEADS, 2)
    ]
    return jnp.concatenate(pieces, axis=1)


def head_sums(array):
    chosen = flag((iota((128, WIDE), 1) >> 6) == iota((128, WIDE), 0))
    return sum(dot_last(part, chosen) for part in split(array, 2))


def gain_row(tail):
    return dot_last(flag(iota((8, 128), 1) == GAIN_LANE), tail)[0:1]


def unit_rows(rows):
    tokens = rows.astype(F32)
    inv = lax.rsqrt(jnp.mean(tokens * tokens, axis=1, keepdims=True) + EPSILON)
    return tokens * inv


def aligned(start, size):
    return pl.ds(pl.multiple_of(start, size), size)


def prepare(
    ids, value_weight, gate_weight, state_proj, step_proj, norm_gain, out_weight, rim, left, longer, right, ready
):
    ready()
    for target in (left, longer):
        target[:ROWS, :WIDE] = value_weight[...]
        target[:ROWS, WIDE:] = gate_weight[...]
    last = rim[...].astype(F32)[8:]
    longer[ROWS:] = jnp.concatenate([last[:, :PAIR], last[:, PAIR:]], axis=0).astype(BF16)
    right[:, : 2 * STATE] = state_proj[...]
    place = iota((HEADS, 128), 1) == STEP_LANE + iota((HEADS, 128), 0)
    tail = dot_first(step_proj[...], flag(place))
    tail = tail + dot_first(norm_gain[...], flag(iota((1, 128), 1) == GAIN_LANE))
    right[:, 2 * STATE : WIDE] = tail.astype(BF16)
    right[:, WIDE:] = out_weight[...]


def tabulate(
    ids, value_filter, state_filter, value_offset, state_offset, gate_gain, heads, hidden, consts, units, ready
):
    ready()
    units[...] = unit_rows(hidden[...])
    consts[...] = jnp.zeros(consts.shape, F32)
    consts[:KERNEL, :WIDE] = value_filter[...].astype(F32)
    consts[:KERNEL, WIDE:MIX] = state_filter[...].astype(F32)
    consts[KERNEL : KERNEL + 1, :WIDE] = value_offset[...].astype(F32)
    consts[KERNEL : KERNEL + 1, WIDE:MIX] = state_offset[...].astype(F32)
    consts[5:6, :WIDE] = gate_gain[...].astype(F32)
    consts[6:9, :HEADS] = heads[...]


def place_blocks(ids, left, right, *moves):
    line, ctx = ids[0, 0], ids[0, 1]

    def piece(side, far, near):
        if far == 2:
            return (side[2], near) if near < 2 else (side[3], near - 2)
        return side[far + far // 3], near

    for far in range(4):
        for near in range(4):
            for target, side, start, source, size in moves:
                if side == 0:
                    block = ((line - far) & 3) * 4 + ((ctx - near) & 3)
                else:
                    block = ((line - near) & 3) * 4 + ((ctx - far) & 3)
                array, place = piece((left, right)[side], far, near)
                target[aligned(block * ROWS, ROWS), start : start + size] = array[
                    place, :, source : source + size
                ]


def enter(
    ids, l0, l1, l2, l3, l4, r0, r1, r2, r3, r4, rim, units, consts,
    weights, hidden_in, taken, wide, narrow, message,
):
    moves = (weights, 0, 0, 0, WIDE), (weights, 1, WIDE, 0, WIDE)
    place_blocks(ids, (l0, l1, l2, l3, l4), (r0, r1, r2, r3, r4), *moves)
    gain = gain_row(weights[:, MIX:])
    hidden_in[:RIM] = (unit_rows(rim[...]) * gain).astype(BF16)
    hidden_in[RIM:] = (units[...] * gain).astype(BF16)
    projected = dot(hidden_in[...], weights[...])
    inputs = projected[:, :MIX].astype(BF16)
    taken[...] = inputs
    inputs = inputs.astype(F32)
    filter_pre = consts[KERNEL : KERNEL + 1, :MIX]
    for tap in range(KERNEL):
        filter_pre = filter_pre + consts[tap : tap + 1, :MIX] * roll(inputs, KERNEL - 1 - tap, 0)[RIM:]
    wide[:, SLOPE] = filter_pre
    activated = filter_pre * jax.nn.sigmoid(filter_pre)
    lanes = iota((T, 128), 1) < HEADS
    step_in = roll(projected[RIM:, MIX:], 128 - STEP_LANE, 1) + consts[6:7, :128]
    step_in = jnp.where(lanes, step_in, -100.0)
    step = jnp.maximum(step_in, 0.0) + jnp.log1p(jnp.exp(-jnp.abs(step_in)))
    step = jnp.where(lanes, step, 0.0)
    rate = jnp.exp(consts[7:8, :128])
    log_decay = pick(flag(iota((T, T), 0) >= iota((T, T), 1)), -step * rate, 1, 0, 3)
    values = activated[:, :WIDE]
    weighted = (values * spread_heads(step)).astype(BF16)
    wide[:, VALUES] = values
    wide[:, STEP] = step
    wide[:, STEP_SLOPE] = jax.nn.sigmoid(step_in)
    wide[:, LOG_DECAY] = log_decay
    narrow[:, BMAT] = activated[:, WIDE : WIDE + STATE].astype(BF16)
    narrow[:, CMAT] = activated[:, WIDE + STATE :].astype(BF16)
    narrow[:, WEIGHTED] = weighted
    last = log_decay[T - 1 :]
    to_end = spread_heads(jnp.exp(last - log_decay))
    message[:STATE] = dot_first(narrow[:, BMAT], weighted.astype(F32) * to_end).astype(BF16)
    span = spread_heads(last)
    high = span.astype(BF16).astype(F32)
    line = iota((16, WIDE), 0)
    tail = jnp.where(line == 0, high, jnp.where(line == 1, span - high, 0.0))
    message[STATE:] = tail.astype(BF16)


def decays(log_decay, turned, head):
    gap = log_decay[:, head : head + 1] - turned[head : head + 1, :]
    return jnp.exp(jnp.where(iota((T, T), 0) >= iota((T, T), 1), gap, -1e30))


def pair_columns(pair):
    return slice(128 * pair, 128 * pair + 128)


def project(
    ids, l0, l1, l2, l3, l4, r0, r1, r2, r3, r4, hidden_in, cotangent, wide, narrow,
    gate_out, before, slope, spread,
):
    moves = (gate_out, 0, 0, WIDE, WIDE), (gate_out, 1, WIDE, WIDE, WIDE)
    place_blocks(ids, (l0, l1, l2, l3, l4), (r0, r1, r2, r3, r4), *moves)
    _, slope[...] = silu_parts(wide[:, SLOPE])
    last = wide[T - 1 :, LOG_DECAY]
    spread[:, GROWN] = spread_heads(jnp.exp(wide[:, LOG_DECAY]))
    spread[:, TO_END] = spread_heads(jnp.exp(last - wide[:, LOG_DECAY]))
    spread[:, STEPS] = spread_heads(wide[:, STEP])
    before[:, GATE_PRE] = dot(hidden_in[RIM:], gate_out[:, :WIDE])
    before[:, GRAD_NORMED] = dot(cotangent[...], gate_out[:, WIDE:])
    scores = dot_last(narrow[:, CMAT], narrow[:, BMAT])
    log_decay = wide[:, LOG_DECAY]
    turned = log_decay.T
    lower = iota((T, 128), 1) < 64
    weighted = narrow[:, WEIGHTED]
    for pair in range(HEADS // 2):
        part = weighted[:, pair_columns(pair)]
        one = dot(scores * decays(log_decay, turned, 2 * pair), part)
        two = dot(scores * decays(log_decay, turned, 2 * pair + 1), part)
        start = WITHIN.start + 128 * pair
        before[:, start : start + 128] = jnp.where(lower, one, two)


def mix(ids, m1, m2, m3, wide, spread, narrow, consts, before, state, after, sums):
    me = ids[0, 1]
    total = jnp.zeros((STATE, WIDE), F32)
    gap = jnp.zeros((1, WIDE), F32)
    for back, message in enumerate((m1, m2, m3)):
        tail = message[STATE:].astype(F32)
        log = tail[0:1] + tail[1:2]
        state[STATE + 8 * back : STATE + 8 * back + 8] = jnp.broadcast_to(log, (8, WIDE))
        scale = jnp.exp(gap) * jnp.where(me > back, 1.0, 0.0)
        total = total + scale * message[:STATE].astype(F32)
        gap = gap + log
    state[:STATE] = total
    inside = before[:, WITHIN] + dot(narrow[:, CMAT], total) * spread[:, GROWN]
    after[:, INSIDE] = inside
    whole = inside + wide[:, VALUES] * spread_heads(consts[8:9, :128])
    after[:, MIXED] = whole
    gate = before[:, GATE_PRE]
    gated = whole * gate * jax.nn.sigmoid(gate)
    ones = jnp.ones((8, WIDE), F32)
    squares = pick(ones, gated * gated, 1, 1)
    crosses = pick(ones, before[:, GRAD_NORMED] * consts[5:6, :WIDE] * gated, 1, 1)
    sums[...] = jnp.where(iota((8, T), 0) < 4, squares, crosses)


def gate_back(
    ids, s0, s1, s2, s3, after, before, consts, spread, narrow, gated_low, grad_mixed, grad_gain, sensitivity
):
    total = s0[...] + s1[...] + s2[...] + s3[...]
    chosen = flag(iota((8, 128), 0) == 4 * iota((8, 128), 1))
    columns = sum(dot_first(part, chosen) for part in split(total, 3))
    inv = lax.rsqrt(columns[:, 0:1] / INNER + EPSILON)
    cross = columns[:, 1:2]
    act, slope = silu_parts(before[:, GATE_PRE])
    mixed = after[:, MIXED]
    normed = mixed * act * inv
    scaled = consts[5:6, :WIDE]
    gated_low[:, NORMED] = (normed * scaled).astype(BF16)
    grads = before[:, GRAD_NORMED]
    grad_gain[...] = jnp.broadcast_to(jnp.sum(grads * normed, axis=0, keepdims=True), (8, WIDE))
    grad_gated = inv * (grads * scaled) - normed * (inv * inv * cross / INNER)
    own = grad_gated * act
    grad_mixed[...] = own
    gated_low[:, LOW_GATE] = (grad_gated * mixed * slope).astype(BF16)
    sensitivity[...] = dot_first(narrow[:, CMAT], own * spread[:, GROWN]).astype(BF16)


def turn_out(ids, source, keep, send):
    chip, core = ids[0, 2] >> 1, ids[0, 2] & 1
    for ahead in range(4):
        start = ((chip + ahead) & 3) * 2
        keep[ahead] = source[aligned((start + core) * SHARE, SHARE)]
        send[ahead] = source[aligned((start + 1 - core) * SHARE, SHARE)]


def middle(
    ids, hidden_in, gated_low, cotangent, gate_out, wide, narrow, grad_mixed, gate, out, grads, branch
):
    gate[...] = dot_first(hidden_in[RIM:], gated_low[:, LOW_GATE]).astype(BF16)
    out[...] = dot_first(cotangent[...], gated_low[:, NORMED]).astype(BF16)
    branch[...] = dot_last(gated_low[:, NORMED], gate_out[:, WIDE:]).astype(BF16)
    bmat, cmat, weighted = narrow[:, BMAT], narrow[:, CMAT], narrow[:, WEIGHTED]
    scores = dot_last(cmat, bmat)
    log_decay = wide[:, LOG_DECAY]
    turned = log_decay.T
    lower = iota((T, 128), 1) < 64
    grad_scores = jnp.zeros((T, T), F32)
    for pair in range(HEADS // 2):
        part = weighted[:, pair_columns(pair)]
        grad = grad_mixed[:, pair_columns(pair)]
        got = []
        for side in range(2):
            weights = decays(log_decay, turned, 2 * pair + side)
            got.append(dot_first(scores * weights, grad))
            own = jnp.where(lower, grad, 0.0) if side == 0 else jnp.where(lower, 0.0, grad)
            grad_scores = grad_scores + twice(own, part, 1, 1) * weights
        grads[:, pair_columns(pair)] = jnp.where(lower, got[0], got[1])
    grads[:, WIDE : WIDE + STATE] = twice(grad_scores, cmat, 0, 0)
    grads[:, WIDE + STATE :] = twice(grad_scores, bmat, 1, 0)


def leave(
    ids, g1, g2, g3, state, after, grad_mixed, grads, wide, spread, slope, narrow, consts, taken, grad_gain,
    low, state_low, keep, send, small, turned,
):
    me = ids[0, 1]
    end = jnp.zeros((STATE, WIDE), F32)
    gap = jnp.zeros((1, WIDE), F32)
    for ahead, message in enumerate((g1, g2, g3)):
        scale = jnp.exp(gap) * jnp.where(me + ahead < 3, 1.0, 0.0)
        end = end + scale * message[...].astype(F32)
        start = STATE + 8 * (2 - ahead)
        gap = gap + state[start : start + 1]
    step, step_slope = wide[:, STEP], wide[:, STEP_SLOPE]
    values = wide[:, VALUES]
    last = wide[T - 1 :, LOG_DECAY]
    to_end = spread[:, TO_END]
    weighted = narrow[:, WEIGHTED].astype(F32)
    own = grad_mixed[...]
    from_end = dot(narrow[:, BMAT], end) * to_end
    inputs = grads[:, :WIDE] + from_end
    from_b = grads[:, WIDE : WIDE + STATE]
    from_b = from_b + sum(dot_last(weighted * to_end, part) for part in split(end, 2))
    from_c = grads[:, WIDE + STATE :]
    from_c = from_c + sum(
        dot_last(own * spread[:, GROWN], part) for part in split(state[:STATE], 2)
    )
    grad_log = head_sums(own.astype(BF16).astype(F32) * after[:, INSIDE] - weighted * inputs)
    at_end = jnp.sum(weighted * from_end, axis=0, keepdims=True) + jnp.exp(
        spread_heads(last)
    ) * jnp.sum(end * state[:STATE], axis=0, keepdims=True)
    at_end = head_sums(jnp.broadcast_to(at_end, (8, WIDE)))[0:1]
    grad_decay = pick(flag(iota((T, T), 0) <= iota((T, T), 1)), grad_log, 1, 0) + at_end
    rate = jnp.exp(consts[7:8, :128])
    grad_step = head_sums(values * inputs) - rate * grad_decay
    grad_step_pre = grad_step * step_slope
    grad_values = own * spread_heads(consts[8:9, :128]) + inputs * spread[:, STEPS]
    grad_pre = jnp.concatenate([grad_values, from_b, from_c], axis=1) * slope[...]
    before = taken[...].astype(F32)
    padded = jnp.concatenate([jnp.zeros((RIM, MIX), F32), grad_pre], axis=0)
    grad_input = jnp.zeros((EXT, MIX), F32)
    line = iota((8, MIX), 0)
    taps = jnp.where(line == KERNEL, jnp.sum(grad_pre, axis=0, keepdims=True), 0.0)
    for tap in range(KERNEL):
        later = roll(padded, tap + 1 - KERNEL, 0)
        taps = jnp.where(line == tap, jnp.sum(before * later, axis=0, keepdims=True), taps)
        grad_input = grad_input + consts[tap : tap + 1, :MIX] * later
    low[:, :WIDE] = grad_input[:, :WIDE].astype(BF16)
    state_low[...] = grad_input[:, WIDE:]
    low_step = jnp.concatenate([jnp.zeros((RIM, 128), F32), grad_step_pre], axis=0)
    low[:, WIDE:] = roll(low_step, STEP_LANE, 1).astype(BF16)
    rest = jnp.zeros((TURNED - EXT - 8, 2 * STATE), F32)
    turned[...] = jnp.concatenate([grad_input[:, WIDE:], taps[:, WIDE:], rest], axis=0).T
    turn_out(ids, turned, keep, send)
    heads = (
        jnp.sum(grad_step_pre, axis=0, keepdims=True),
        -rate * jnp.sum(grad_decay * step, axis=0, keepdims=True),
        head_sums(jnp.broadcast_to(jnp.sum(own * values, axis=0, keepdims=True), (8, WIDE)))[0:1],
    )
    none = jnp.zeros((1, 128), F32)
    heads = jnp.concatenate([heads[0] + roll(heads[1], 64, 1), heads[2], none], axis=1)
    line = iota((8, WIDE), 0)
    small[...] = jnp.where(line == 5, grad_gain[...], jnp.where(line == 6, heads, taps[:, :WIDE]))


def pair_sum(ids, keep, got, *shares):
    for ahead, share in enumerate(shares):
        share[...] = (keep[ahead].astype(F32) + got[ahead].astype(F32)).astype(share.dtype)


def value_grads(
    ids, low, state_low, gated_low, weights, gate_out, hidden_in, pair, value, head
):
    value[...] = dot_first(hidden_in[...], low[:, :WIDE]).astype(BF16)
    part = dot_last(low[:, :WIDE], weights[:, :WIDE]) + dot_last(low[:, WIDE:], weights[:, MIX:])
    high, rest = split(state_low[...], 2)
    part = part + dot_last(high, weights[:, WIDE:MIX]) + dot_last(rest, weights[:, WIDE:MIX])
    head[:RIM] = part[:RIM]
    head[RIM:] = part[RIM:] + dot_last(gated_low[:, LOW_GATE], gate_out[:, :WIDE])


def share_out(ids, head, branch, keep, send, whole):
    whole[...] = head[RIM:].astype(BF16)
    chip, core = ids[0, 2] >> 1, ids[0, 2] & 1
    for other in range(4):
        start = (chip ^ other) * 2
        for half, source in enumerate((whole, branch)):
            rows = slice(half * SHARE, half * SHARE + SHARE)
            keep[other, rows] = source[aligned((start + core) * SHARE, SHARE)]
            send[other, rows] = source[aligned((start + 1 - core) * SHARE, SHARE)]


def fold(small):
    pieces = []
    for chunk in range(6):
        piece = small[:, pair_columns(chunk // 2)]
        pieces.append(piece if chunk % 2 else roll(piece, 64, 1))
    folded = jnp.concatenate(pieces, axis=0)
    high = folded.astype(BF16).astype(F32)
    return jnp.concatenate([high, folded - high], axis=0)


def unfold(block):
    folded = block[:48] + block[48:]
    lower = iota((8, 128), 1) < 64
    pairs = []
    for pair in range(3):
        one, two = folded[16 * pair : 16 * pair + 8], folded[16 * pair + 8 : 16 * pair + 16]
        pairs.append(jnp.where(lower, roll(one, 64, 1), two))
    return jnp.concatenate(pairs, axis=1)


def tidy(block):
    folded = block[:48] + block[48:]
    high = folded.astype(BF16).astype(F32)
    parts = jnp.concatenate([high, folded - high], axis=0)
    return jnp.where(iota((ROWS, 128), 1) < 64, block, parts)


def late_grads(
    ids, t0, t1, t2, t3, low, small, head, rim, units, hidden_in, gate, out, value, branch, keep, send, *targets
):
    targets, tail, whole = targets[:-2], targets[-2], targets[-1]
    total = t0[...] + t1[...] + t2[...] + t3[...]
    straight = jnp.concatenate([total, jnp.zeros((128 - PART, TURNED), F32)], axis=0).T
    low_tail = low[:, WIDE:].astype(F32) + straight[:EXT]
    terms = jnp.sum(head[:RIM] * unit_rows(rim[...]), axis=0, keepdims=True)
    terms = terms + jnp.sum(head[RIM:] * units[...], axis=0, keepdims=True)
    grads = dot_first(hidden_in[...], low_tail)
    row = jnp.where(iota((8, D), 0) == 0, terms, 0.0)
    chosen = flag(iota((8, 128), 1) == GAIN_LANE)
    grads = grads + sum(dot_first(part, chosen) for part in split(row, 2))
    tail[...] = grads.astype(BF16)
    own = straight[EXT : EXT + 8]
    row = jnp.concatenate([own[0:1] + roll(own[1:2], 64, 1), own[2:3] + roll(own[3:4], 64, 1), own[4:5]], axis=1)
    folded = fold(jnp.where(iota((8, WIDE), 0) == 7, row, small[...]))
    lanes = iota((ROWS, 128), 1) < 64
    for target, place, block in places(ids, 0, targets[:5]):
        rows = aligned(block * ROWS, ROWS)
        target[place, :, :WIDE] = gate[rows]
        target[place, :, WIDE:] = value[rows]
    for target, place, block in places(ids, 1, targets[5:]):
        rows = aligned(block * ROWS, ROWS)
        target[place, :ROWS, :OUT_RIGHT] = out[rows]
        end = jnp.where(lanes, tail[rows].astype(F32), folded)
        target[place, :ROWS, OUT_RIGHT:] = end.astype(BF16)
    share_out(ids, head, branch, keep, send, whole)
    last = head[:RIM][8:]
    pieces = [last[:, RIGHT * chunk : RIGHT * chunk + RIGHT] for chunk in range(D // RIGHT)]
    pieces.append(jnp.zeros((8, RIGHT), F32))
    for slot in range(2):
        targets[8][slot, ROWS:] = jnp.concatenate(pieces[2 * slot : 2 * slot + 2], axis=0).astype(BF16)


def places(ids, side, targets):
    line, ctx = ids[0, 0], ids[0, 1]
    for far in range(4):
        for near in range(4):
            slot, place = far + far // 3, near
            if far == 2 and near >= 2:
                slot, place = 3, near - 2
            one, two = (near, far) if side else (far, near)
            yield targets[slot], place, ((line + one) & 3) * 4 + ((ctx + two) & 3)


def put(target, total, tailed):
    if tailed:
        target[:, :OUT_RIGHT] = total[:, :OUT_RIGHT].astype(BF16)
        target[:, OUT_RIGHT:] = tidy(total[:, OUT_RIGHT:]).astype(BF16)
    else:
        target[...] = total.astype(BF16)


def pair_halves(ids, keep, got, near, far):
    for other in range(4):
        target = far if other % 2 else near
        total = keep[other].astype(F32) + got[other].astype(F32)
        target[other // 2] = total.astype(BF16)


def relay(side, one, three, first, second, to_one, to_three):
    for near in range(4):
        if near < 2:
            total = one[near].astype(F32) + first[near].astype(F32)
            put(to_one.at[near], total, side)
            to_three[near] = three[near]
        else:
            total = three[near].astype(F32) + second[near - 2, :ROWS].astype(F32)
            put(to_three.at[near], total, side)
            to_one[near] = one[near]


def relay_both(ids, *refs):
    relay(0, *refs[:4], *refs[9:11])
    relay(1, *refs[4:8], *refs[11:13])
    second, behind = refs[7], refs[13]
    inside = jnp.where(ids[0, 1] < 3, 1.0, 0.0)
    for chunk in range(D // RIGHT):
        got = second[chunk // 2, ROWS:].astype(F32) * inside
        start = 8 * (chunk % 2)
        behind[:, RIGHT * chunk : RIGHT * chunk + RIGHT] = got[start : start + 8]


def halfway(side, own, one, three, *targets):
    for near, target in enumerate(targets):
        total = own[near].astype(F32) + one[near].astype(F32) + three[near].astype(F32)
        put(target, total, side)


def halfway_both(ids, l0, l1, l3, r0, r1, r3, own, *targets):
    halfway(0, l0, l1, l3, *targets[:4])
    halfway(1, r0, r1, r3, *targets[4:])


def pair_again(ids, near, got, cotangent, hidden, own, second, held, mine, last):
    for index, target in enumerate((own, second)):
        target[...] = (near[index].astype(F32) + got[index].astype(F32)).astype(BF16)
    held[...] = cotangent[...]
    mine[...] = hidden[aligned(ids[0, 2] * SHARE, SHARE)]
    last[...] = hidden[T - RIM :].astype(F32)[8:]


def collect_left(ids, a0, a1, a2, a3, b0, b1, b2, b3, grad_gate, grad_value, grad_out):
    total = sum(part[...].astype(F32) for part in (a0, a1, a2, a3))
    grad_gate[...] = total[:, :WIDE]
    grad_value[...] = total[:, WIDE:]
    grad_out[...] = sum(part[:, :OUT_RIGHT].astype(F32) for part in (b0, b1, b2, b3))


def hidden_back(grads, rows, gain):
    tokens = rows.astype(F32)
    inv = lax.rsqrt(jnp.mean(tokens * tokens, axis=1, keepdims=True) + EPSILON)
    unit = tokens * inv
    scaled = grads * gain
    return inv * (scaled - unit * jnp.mean(scaled * unit, axis=1, keepdims=True)), tokens


def gather_up(
    ids, b0, b1, b2, b3, p0, p1, mine, weights, behind,
    message, gain_out, grad_step, taps, offset, gain, bias, decay, skip, rest,
):
    both = p0[...].astype(F32) + p1[...].astype(F32)
    row = gain_row(weights[:, MIX:])
    gain_out[...] = jnp.broadcast_to(row, (8, D))
    grads, tokens = hidden_back(both[:SHARE], mine[...], row)
    message[:SHARE] = grads.astype(BF16)
    message[SHARE : 2 * SHARE] = (tokens + both[SHARE:]).astype(BF16)
    total = sum(part[:, OUT_RIGHT:].astype(F32) for part in (b0, b1, b2, b3))
    rest[...] = total
    small = unfold(total)
    state = small[7:8]
    lanes = iota((8, 128), 1)
    for tap in range(KERNEL + 1):
        piece = state[:, pair_columns(tap // 2)]
        piece = piece if tap % 2 == 0 else roll(piece, 64, 1)
        if tap == 0:
            rows = jnp.where(iota((8, 128), 0) == 0, roll(piece, STATE_LANE, 1), 0.0)
        else:
            rows = jnp.where(iota((8, 128), 0) == tap, roll(piece, STATE_LANE, 1), rows)
    rest[:8] = jnp.where(lanes < 64, rest[:8], rows)
    for block in range(ROWS // 16):
        message[2 * SHARE :, pair_columns(block)] = rest[16 * block : 16 * block + 16].astype(BF16)
    for block in range(6):
        pair = [behind[:, pair_columns(2 * block + i)] for i in range(2)]
        message[2 * SHARE :, pair_columns(6 + block)] = jnp.concatenate(pair, axis=0).astype(BF16)
    picked = flag(iota((8, 128), 1) == STEP_LANE + iota((8, 128), 0))
    grad_step[...] = pick(picked, total, 1, 1, 3)[:HEADS]
    taps[...] = small[:KERNEL]
    offset[...] = small[KERNEL : KERNEL + 1]
    gain[...] = small[5:6]
    bias[...] = small[6:7, :HEADS]
    decay[...] = small[6:7, 64 : 64 + HEADS]
    skip[...] = small[6:7, 128 : 128 + HEADS]


def finish(ids, *refs):
    pieces, row, cotangent, last = refs[:8], refs[8], refs[9], refs[10]
    grad_hidden, block_out, grad_state, grad_gain, taps, offset, rest, rims = refs[11:]
    chip, core = ids[0, 2] >> 1, ids[0, 2] & 1
    order = []
    for far in range(4):
        start = ((chip - far) & 3) * 2
        order += [(start + core, pieces[far]), (start + 1 - core, pieces[4 + far])]
    for place, piece in order:
        block_out[aligned(place * SHARE, SHARE)] = piece[SHARE : 2 * SHARE]
        for block in range(6):
            part = piece[2 * SHARE :, pair_columns(block)]
            rest[place, 16 * block : 16 * block + 16] = part.astype(F32)
            part = piece[2 * SHARE :, pair_columns(6 + block)].astype(F32)
            rims[place, :, pair_columns(2 * block)] = part[:8]
            rims[place, :, pair_columns(2 * block + 1)] = part[8:]
    total, behind = rest[0], rims[0]
    for i in range(1, 8):
        total = total + rest[i]
        behind = behind + rims[i]
    for place, piece in order:
        rows = aligned(place * SHARE, SHARE)
        grad_hidden[rows] = cotangent[rows].astype(F32) + piece[:SHARE].astype(F32)
    grads, _ = hidden_back(behind, last[...], row[0:1])
    grad_hidden[T - 8 :] = grad_hidden[T - 8 :] + grads
    lanes = iota((ROWS, 128), 1) >> 5
    for half in range(2):
        state = jnp.zeros((ROWS, 128), F32)
        small = jnp.zeros((8, 128), F32)
        for i in range(4):
            one = rest[4 * half + i]
            state = jnp.where(lanes == i, roll(one, PART * i, 1), state)
            small = jnp.where(lanes[:8] == i, roll(one[:8], PART * i - STATE_LANE, 1), small)
        columns = pair_columns(half)
        grad_state[:, columns] = state
        taps[:, columns] = small[:KERNEL]
        offset[:, columns] = small[KERNEL : KERNEL + 1]
    grad_gain[...] = pick(flag(iota((8, 128), 1) == GAIN_LANE), total, 1, 1, 3)[0:1]


def stack_blocks(ids, l0, l1, l2, l3, r0, r1, r2, r3, left, right, rim):
    for i, (one, two) in enumerate(((l0, r0), (l1, r1), (l2, r2), (l3, r3))):
        left[i] = one[:ROWS]
        right[i] = two[...]
    inside = jnp.where(ids[0, 1] > 0, 1.0, 0.0)
    got = l1[ROWS:].astype(F32) * inside
    none = jnp.zeros((8, PAIR), F32)
    rim[:, :PAIR] = jnp.concatenate([none, got[:8]], axis=0).astype(BF16)
    rim[:, PAIR:] = jnp.concatenate([none, got[8:]], axis=0).astype(BF16)


def shift(array, axis, steps):
    return lax.ppermute(array, axis, [(i, (i + steps) % 4) for i in range(4)])


def from_chip(array, steps):
    return lax.ppermute(array, "tp", [(i, (i + 2 * steps) % 8) for i in range(8)])


def across(array, bits):
    return lax.ppermute(array, "tp", [(i, i ^ bits) for i in range(8)])


def around(array, axis):
    return [array] + [shift(array, axis, steps) for steps in range(1, 4)]


def ring_sides(array, axis):
    return shift(array, axis, 1), shift(array, axis, 3)


def ring_rest(array, axis, one, three):
    return [array, one, shift(one[:2], axis, 1), shift(three[2:], axis, 3), three]


def chips_all(array):
    same = [array] + [from_chip(array, steps) for steps in range(1, 4)]
    return same + [across(one, 1) for one in same]


def per_device(
    hidden_states,
    norm_gain,
    gate_weight,
    value_weight,
    state_proj,
    step_proj,
    value_filter,
    value_offset,
    state_filter,
    state_offset,
    step_bias,
    decay_log,
    skip_gain,
    gate_norm_gain,
    out_weight,
    out_grad,
):
    hidden = hidden_states[0]
    cotangent = out_grad[0]
    places = [lax.axis_index(axis).astype(jnp.int32) for axis in ("dp", "ctx", "tp")]
    ids = jnp.stack(places).reshape(1, 3)

    left, longer, right = fuse(
        prepare,
        [((ROWS, PAIR), BF16), ((ROWS + RIM, PAIR), BF16), ((ROWS, PAIR), BF16)],
        ids,
        value_weight,
        gate_weight,
        state_proj,
        step_proj.T,
        norm_gain[None],
        out_weight.T,
        hidden,
        fetch=7,
        rim=True,
    )
    near = [left, shift(longer, "ctx", 1), shift(left, "ctx", 2), shift(left, "ctx", 3)]
    left, right, rim = fuse(
        stack_blocks,
        [((4, ROWS, PAIR), BF16)] * 2 + [((RIM, D), BF16)],
        ids,
        *near,
        *around(right, "dp"),
    )
    consts, units = fuse(
        tabulate,
        [((16, FIRST), F32), ((T, D), F32)],
        ids,
        value_filter,
        state_filter,
        value_offset[None],
        state_offset[None],
        gate_norm_gain[None],
        jnp.stack([step_bias, decay_log, skip_gain]),
        hidden,
        fetch=7,
    )
    left = ring_rest(left, "dp", *ring_sides(left, "dp"))
    right = ring_rest(right, "ctx", *ring_sides(right, "ctx"))
    weights, hidden_in, taken, wide, narrow, message = fuse(
        enter,
        [
            ((D, FIRST), BF16),
            ((EXT, D), BF16),
            ((EXT, MIX), BF16),
            ((T, LOG_DECAY.stop), F32),
            ((T, WEIGHTED.stop), BF16),
            ((STATE + 16, WIDE), BF16),
        ],
        ids,
        *left,
        *right,
        rim,
        units,
        consts,
    )
    messages = around(message, "ctx")[1:]
    gate_out, before, slope, spread = fuse(
        project,
        [((D, 2 * WIDE), BF16), ((T, WITHIN.stop), F32), ((T, MIX), F32), ((T, STEPS.stop), F32)],
        ids,
        *left,
        *right,
        hidden_in,
        cotangent,
        wide,
        narrow,
    )
    state, after, sums = fuse(
        mix,
        [((STATE + 24, WIDE), F32), ((T, MIXED.stop), F32), ((8, T), F32)],
        ids,
        *messages,
        wide,
        spread,
        narrow,
        consts,
        before,
    )
    sums = sums + across(sums, 1)
    gated_low, grad_mixed, grad_gain, sensitivity = fuse(
        gate_back,
        [
            ((T, LOW_GATE.stop), BF16),
            ((T, WIDE), F32),
            ((8, WIDE), F32),
            ((STATE, WIDE), BF16),
        ],
        ids,
        sums,
        *[from_chip(sums, steps) for steps in range(1, 4)],
        after,
        before,
        consts,
        spread,
        narrow,
    )
    later = [shift(sensitivity, "ctx", -steps) for steps in range(1, 4)]
    square = ((D, WIDE), BF16)
    gate, out, grads, branch = fuse(
        middle,
        [square, square, ((T, MIX), F32), ((T, D), BF16)],
        ids,
        hidden_in,
        gated_low,
        cotangent,
        gate_out,
        wide,
        narrow,
        grad_mixed,
    )
    low, state_low, keep, send, small = fuse(
        leave,
        [((EXT, WIDE + 128), BF16), ((EXT, 2 * STATE), F32)] + [((4, PART, TURNED), F32)] * 2 + [((8, WIDE), F32)],
        ids,
        *later,
        state,
        after,
        grad_mixed,
        grads,
        wide,
        spread,
        slope,
        narrow,
        consts,
        taken,
        grad_gain,
        scratch=[((2 * STATE, TURNED), F32)],
    )
    pair = fuse(pair_sum, [((PART, TURNED), F32)] * 4, ids, keep, across(send, 1))
    turned = pair[:1] + [from_chip(pair[steps], steps) for steps in range(1, 4)]
    value, head = fuse(
        value_grads,
        [square, ((EXT, D), F32)],
        ids,
        low,
        state_low,
        gated_low,
        weights,
        gate_out,
        hidden_in,
        pair[0],
    )
    both = ((2 * SHARE, D), BF16)
    two = ((2, 2 * SHARE, D), BF16)

    def stage(count, rows, columns):
        return (count, rows, columns), BF16

    def stages(columns, rows):
        whole = stage(4, ROWS, columns)
        return [whole, whole, stage(2, ROWS, columns), stage(2, rows, columns), whole]

    keep, send, *blocks = fuse(
        late_grads,
        [((4, 2 * SHARE, D), BF16)] * 2 + stages(LEFT, ROWS) + stages(RIGHT, ROWS + RIM),
        ids,
        *turned,
        low,
        small,
        head,
        rim,
        units,
        hidden_in,
        gate,
        out,
        value,
        branch,
        scratch=[((D, 128), BF16), ((T, D), BF16)],
    )
    left, right = blocks[:5], blocks[5:]
    near, far = fuse(pair_halves, [two] * 2, ids, keep, across(send, 1))
    *sides, behind = fuse(
        relay_both,
        [stage(4, ROWS, LEFT)] * 2 + [stage(4, ROWS, RIGHT)] * 2 + [((8, D), F32)],
        ids,
        *(left[1], left[4], shift(left[2], "dp", 1), shift(left[3], "dp", 3)),
        *(right[1], right[4], shift(right[2], "ctx", 1), shift(right[3], "ctx", 3)),
        near,
    )
    left = [left[0], shift(sides[0], "dp", 1), shift(sides[1], "dp", 3)]
    right = [right[0], shift(sides[2], "ctx", 1), shift(sides[3], "ctx", 3)]
    own, second, held, mine, last = fuse(
        pair_again,
        [both, both, ((T, D), BF16), ((SHARE, D), BF16), ((8, D), F32)],
        ids,
        near,
        across(far, 2),
        cotangent,
        hidden,
    )
    sums = fuse(
        halfway_both,
        [((ROWS, LEFT), BF16)] * 4 + [((ROWS, RIGHT), BF16)] * 4,
        ids,
        *left,
        *right,
        own,
    )
    left = sums[:1] + [shift(sums[steps], "ctx", steps) for steps in range(1, 4)]
    right = sums[4:5] + [shift(sums[4 + steps], "dp", steps) for steps in range(1, 4)]
    few, line = ((1, HEADS), F32), ((1, WIDE), F32)
    message, gain_full, *few_grads = fuse(
        gather_up,
        [((2 * SHARE + 16, D), BF16), ((8, D), F32), ((HEADS, ROWS), F32), ((KERNEL, WIDE), F32)]
        + [line, line, few, few, few],
        ids,
        *right,
        own,
        across(second, 4),
        mine,
        weights,
        behind,
        scratch=[((ROWS, 128), F32)],
    )
    grad_step, taps, offset, gain, bias, decay, skip = few_grads
    grad_gate, grad_value, grad_out = fuse(
        collect_left, [((ROWS, WIDE), F32)] * 3, ids, *left, *right
    )
    grad_hidden, block_out, grad_state, grad_norm_gain, state_taps, state_offset = fuse(
        finish,
        [
            ((T, D), F32),
            ((T, D), BF16),
            ((ROWS, 2 * STATE), F32),
            ((1, ROWS), F32),
            ((KERNEL, 2 * STATE), F32),
            ((1, 2 * STATE), F32),
        ],
        ids,
        *chips_all(message),
        gain_full,
        held,
        last,
        scratch=[((8, ROWS, 128), F32), ((8, 8, D), F32)],
    )
    return (
        block_out[None],
        grad_hidden[None],
        grad_norm_gain[0],
        grad_gate,
        grad_value,
        grad_state,
        grad_step.T,
        taps,
        offset[0],
        state_taps,
        state_offset[0],
        bias[0],
        decay[0],
        skip[0],
        gain[0],
        grad_out.T,
    )


def solution(mesh):
    line = P(("dp", "ctx"))
    placed = (
        P("dp", "ctx", None),
        line,
        P(("dp", "ctx"), "tp"),
        P(("dp", "ctx"), "tp"),
        P(("dp", "ctx"), None),
        P(("dp", "ctx"), "tp"),
        P(None, "tp"),
        P("tp"),
        P(),
        P(),
        P("tp"),
        P("tp"),
        P("tp"),
        P("tp"),
        P("tp", ("dp", "ctx")),
        P("dp", "ctx", None),
    )
    given = (
        P("dp", "ctx", None),
        P("dp", "ctx", None),
        line,
        P(("dp", "ctx"), "tp"),
        P(("dp", "ctx"), "tp"),
        P(("dp", "ctx"), None),
        P(("dp", "ctx"), "tp"),
        P(None, "tp"),
        P("tp"),
        P(),
        P(),
        P("tp"),
        P("tp"),
        P("tp"),
        P("tp"),
        P("tp", ("dp", "ctx")),
    )
    return jax.shard_map(
        per_device, mesh=mesh, in_specs=placed, out_specs=given, check_vma=False
    )
```

```python
import jax
import jax.numpy as jnp
from jax import lax
from jax.experimental import pallas as pl
from jax.experimental.pallas import tpu as pltpu
from jax.sharding import PartitionSpec as P

F32 = jnp.float32
BF16 = jnp.bfloat16
EPSILON = 1e-05
INNER = 3072
D = 1536
T = 256
RIM = 16
EXT = T + RIM
KERNEL = 4
HEADS = 6
WIDE = 384
STATE = 128
MIX = WIDE + 2 * STATE
FIRST = MIX + 128
ROWS = 96
SHARES = 16
PAIR = 2 * WIDE
RIGHT = 512
OUT_RIGHT = RIGHT - 128
LEFT = 3 * WIDE - OUT_RIGHT
SHARE = T // 8
PART = 32
STEP_LANE = 32
GAIN_LANE = STEP_LANE + HEADS
STATE_LANE = 64
TURNED = 384
VMEM_LIMIT = 8 * 2**20

VALUES, SLOPE = slice(0, WIDE), slice(WIDE, WIDE + MIX)
STEP, STEP_SLOPE, LOG_DECAY = slice(1024, 1152), slice(1152, 1280), slice(1280, 1408)
BMAT, CMAT, WEIGHTED = slice(0, 128), slice(128, 256), slice(256, 640)
GATE, GRAD_NORMED, WITHIN = slice(0, 384), slice(384, 768), slice(768, 1152)
GATE_SLOPE, SCALED, SKIPPED = slice(1152, 1536), slice(1536, 1920), slice(1920, 2304)
INSIDE, MIXED = slice(0, 384), slice(384, 768)
NORMED, LOW_GATE = slice(0, 384), slice(384, 768)
GROWN, TO_END, STEPS = slice(0, 384), slice(384, 768), slice(768, 1152)


WORK = {"pair_again": 2 * 10**9, "collect_left": 5 * 10**9}


def fuse(function, outputs, ids, *arrays, scratch=(), fetch=0, rim=False):
    count = len(arrays)
    plain = count - fetch
    shapes = [array.shape for array in arrays]
    if rim:
        shapes[-1] = (RIM, D)

    def body(*refs):
        if not fetch:
            function(*refs)
            return
        given = list(refs[1 + plain : 1 + count])
        held, done = refs[-1 - fetch : -1], refs[-1]
        if rim:
            given[-1] = given[-1].at[pl.ds(T - RIM, RIM)]
        copies = [
            pltpu.make_async_copy(source, target, done.at[i])
            for i, (source, target) in enumerate(zip(given, held))
        ]
        for copy in copies:
            copy.start()

        def ready():
            for copy in copies:
                copy.wait()

        function(*refs[: 1 + plain], *held, *refs[1 + count : -1 - fetch], ready=ready)

    buffers = [pltpu.VMEM(shape, dtype) for shape, dtype in scratch]
    spaces = [pltpu.SMEM] + [pltpu.VMEM] * plain + [pltpu.HBM] * fetch
    if fetch:
        buffers += [pltpu.VMEM(shapes[i], arrays[i].dtype) for i in range(plain, count)]
        buffers += [pltpu.SemaphoreType.DMA((fetch,))]
        held = [pltpu.with_memory_space_constraint(array, pltpu.HBM) for array in arrays[plain:]]
        arrays = (*arrays[:plain], *held)
    cost = None
    if function.__name__ in WORK:
        cost = pl.CostEstimate(
            flops=WORK[function.__name__], bytes_accessed=10**6, transcendentals=1
        )
    call = pl.pallas_call(
        body,
        out_shape=[jax.ShapeDtypeStruct(shape, dtype) for shape, dtype in outputs],
        in_specs=[pl.BlockSpec(memory_space=space) for space in spaces],
        out_specs=[pl.BlockSpec(memory_space=pltpu.VMEM) for _ in outputs],
        scratch_shapes=buffers,
        compiler_params=pltpu.CompilerParams(vmem_limit_bytes=VMEM_LIMIT),
        cost_estimate=cost,
        name=function.__name__,
    )
    return list(call(ids, *arrays))


def roll(array, shift, axis):
    return pltpu.roll(array, shift % array.shape[axis], axis)


def product(a, b, left, right):
    return lax.dot_general(
        a.astype(BF16),
        b.astype(BF16),
        (((left,), (right,)), ((), ())),
        preferred_element_type=F32,
    )


def dot(a, b):
    return product(a, b, 1, 0)


def dot_last(a, b):
    return product(a, b, 1, 1)


def dot_first(a, b):
    return product(a, b, 0, 0)


def split(array, count):
    parts = []
    for _ in range(count):
        part = array.astype(BF16)
        parts.append(part)
        array = array - part.astype(F32)
    return parts


def twice(a, b, left, right):
    return sum(product(part, b, left, right) for part in split(a, 2))


def pick(chosen, array, left, right, parts=2):
    return sum(product(chosen, part, left, right) for part in split(array, parts))


def iota(shape, axis):
    return lax.broadcasted_iota(jnp.int32, shape, axis)


def flag(condition):
    return jnp.where(condition, 1.0, 0.0)


def silu_parts(array):
    sig = jax.nn.sigmoid(array)
    return array * sig, sig * (1.0 + array * (1.0 - sig))


def spread_heads(array):
    rows = array.shape[0]
    lower = iota((rows, 128), 1) < 64
    pieces = [
        jnp.where(lower, array[:, h : h + 1], array[:, h + 1 : h + 2]) for h in range(0, HEADS, 2)
    ]
    return jnp.concatenate(pieces, axis=1)


def head_sums(array):
    chosen = flag((iota((128, WIDE), 1) >> 6) == iota((128, WIDE), 0))
    return sum(dot_last(part, chosen) for part in split(array, 2))


def gain_row(tail):
    return dot_last(flag(iota((8, 128), 1) == GAIN_LANE), tail)[0:1]


def unit_rows(rows):
    tokens = rows.astype(F32)
    inv = lax.rsqrt(jnp.mean(tokens * tokens, axis=1, keepdims=True) + EPSILON)
    return tokens * inv


def aligned(start, size):
    return pl.ds(pl.multiple_of(start, size), size)


def prepare(
    ids, value_weight, gate_weight, state_proj, step_proj, norm_gain, out_weight, rim, left, longer, right, ready
):
    ready()
    for target in (left, longer):
        target[:ROWS, :WIDE] = value_weight[...]
        target[:ROWS, WIDE:] = gate_weight[...]
    last = rim[...].astype(F32)[8:]
    longer[ROWS:] = jnp.concatenate([last[:, :PAIR], last[:, PAIR:]], axis=0).astype(BF16)
    right[:, : 2 * STATE] = state_proj[...]
    place = iota((HEADS, 128), 1) == STEP_LANE + iota((HEADS, 128), 0)
    tail = dot_first(step_proj[...], flag(place))
    tail = tail + dot_first(norm_gain[...], flag(iota((1, 128), 1) == GAIN_LANE))
    right[:, 2 * STATE : WIDE] = tail.astype(BF16)
    right[:, WIDE:] = out_weight[...]


def tabulate(
    ids, value_filter, state_filter, value_offset, state_offset, gate_gain, heads, hidden, consts, units, ready
):
    ready()
    units[...] = unit_rows(hidden[...])
    consts[...] = jnp.zeros(consts.shape, F32)
    consts[:KERNEL, :WIDE] = value_filter[...].astype(F32)
    consts[:KERNEL, WIDE:MIX] = state_filter[...].astype(F32)
    consts[KERNEL : KERNEL + 1, :WIDE] = value_offset[...].astype(F32)
    consts[KERNEL : KERNEL + 1, WIDE:MIX] = state_offset[...].astype(F32)
    consts[5:6, :WIDE] = gate_gain[...].astype(F32)
    consts[6:9, :HEADS] = heads[...]


def place_blocks(ids, left, right, *moves):
    line, ctx = ids[0, 0], ids[0, 1]

    def piece(side, far, near):
        if far == 2:
            return (side[2], near) if near < 2 else (side[3], near - 2)
        return side[far + far // 3], near

    for far in range(4):
        for near in range(4):
            for target, side, start, source, size in moves:
                if side == 0:
                    block = ((line - far) & 3) * 4 + ((ctx - near) & 3)
                else:
                    block = ((line - near) & 3) * 4 + ((ctx - far) & 3)
                array, place = piece((left, right)[side], far, near)
                target[aligned(block * ROWS, ROWS), start : start + size] = array[
                    place, :, source : source + size
                ]


def enter(
    ids, l0, l1, l2, l3, l4, r0, r1, r2, r3, r4, rim, units, consts,
    weights, hidden_in, taken, wide, narrow, message,
):
    moves = (weights, 0, 0, 0, WIDE), (weights, 1, WIDE, 0, WIDE)
    place_blocks(ids, (l0, l1, l2, l3, l4), (r0, r1, r2, r3, r4), *moves)
    gain = gain_row(weights[:, MIX:])
    hidden_in[:RIM] = (unit_rows(rim[...]) * gain).astype(BF16)
    hidden_in[RIM:] = (units[...] * gain).astype(BF16)
    projected = dot(hidden_in[...], weights[...])
    inputs = projected[:, :MIX].astype(BF16)
    taken[...] = inputs
    inputs = inputs.astype(F32)
    filter_pre = consts[KERNEL : KERNEL + 1, :MIX]
    for tap in range(KERNEL):
        filter_pre = filter_pre + consts[tap : tap + 1, :MIX] * roll(inputs, KERNEL - 1 - tap, 0)[RIM:]
    wide[:, SLOPE] = filter_pre
    activated = filter_pre * jax.nn.sigmoid(filter_pre)
    lanes = iota((T, 128), 1) < HEADS
    step_in = roll(projected[RIM:, MIX:], 128 - STEP_LANE, 1) + consts[6:7, :128]
    step_in = jnp.where(lanes, step_in, -100.0)
    step = jnp.maximum(step_in, 0.0) + jnp.log1p(jnp.exp(-jnp.abs(step_in)))
    step = jnp.where(lanes, step, 0.0)
    rate = jnp.exp(consts[7:8, :128])
    log_decay = pick(flag(iota((T, T), 0) >= iota((T, T), 1)), -step * rate, 1, 0, 3)
    values = activated[:, :WIDE]
    weighted = (values * spread_heads(step)).astype(BF16)
    wide[:, VALUES] = values
    wide[:, STEP] = step
    wide[:, STEP_SLOPE] = jax.nn.sigmoid(step_in)
    wide[:, LOG_DECAY] = log_decay
    narrow[:, BMAT] = activated[:, WIDE : WIDE + STATE].astype(BF16)
    narrow[:, CMAT] = activated[:, WIDE + STATE :].astype(BF16)
    narrow[:, WEIGHTED] = weighted
    last = log_decay[T - 1 :]
    to_end = spread_heads(jnp.exp(last - log_decay))
    message[:STATE] = dot_first(narrow[:, BMAT], weighted.astype(F32) * to_end).astype(BF16)
    span = spread_heads(last)
    high = span.astype(BF16).astype(F32)
    line = iota((16, WIDE), 0)
    tail = jnp.where(line == 0, high, jnp.where(line == 1, span - high, 0.0))
    message[STATE:] = tail.astype(BF16)


def decays(log_decay, turned, head):
    gap = log_decay[:, head : head + 1] - turned[head : head + 1, :]
    return jnp.exp(jnp.where(iota((T, T), 0) >= iota((T, T), 1), gap, -1e30))


def pair_columns(pair):
    return slice(128 * pair, 128 * pair + 128)


def project(
    ids, l0, l1, l2, l3, l4, r0, r1, r2, r3, r4, hidden_in, cotangent, wide, narrow, consts,
    gate_out, before, slope, spread,
):
    moves = (gate_out, 0, 0, WIDE, WIDE), (gate_out, 1, WIDE, WIDE, WIDE)
    place_blocks(ids, (l0, l1, l2, l3, l4), (r0, r1, r2, r3, r4), *moves)
    _, slope[...] = silu_parts(wide[:, SLOPE])
    last = wide[T - 1 :, LOG_DECAY]
    spread[:, GROWN] = spread_heads(jnp.exp(wide[:, LOG_DECAY]))
    spread[:, TO_END] = spread_heads(jnp.exp(last - wide[:, LOG_DECAY]))
    spread[:, STEPS] = spread_heads(wide[:, STEP])
    act, gate_slope = silu_parts(dot(hidden_in[RIM:], gate_out[:, :WIDE]))
    grads = dot(cotangent[...], gate_out[:, WIDE:])
    before[:, GATE] = act
    before[:, GATE_SLOPE] = gate_slope
    before[:, GRAD_NORMED] = grads
    before[:, SCALED] = grads * consts[5:6, :WIDE] * act
    before[:, SKIPPED] = wide[:, VALUES] * spread_heads(consts[8:9, :128])
    scores = dot_last(narrow[:, CMAT], narrow[:, BMAT])
    log_decay = wide[:, LOG_DECAY]
    turned = log_decay.T
    lower = iota((T, 128), 1) < 64
    weighted = narrow[:, WEIGHTED]
    for pair in range(HEADS // 2):
        part = weighted[:, pair_columns(pair)]
        one = dot(scores * decays(log_decay, turned, 2 * pair), part)
        two = dot(scores * decays(log_decay, turned, 2 * pair + 1), part)
        start = WITHIN.start + 128 * pair
        before[:, start : start + 128] = jnp.where(lower, one, two)


def mix(ids, m1, m2, m3, spread, narrow, before, state, after, sums):
    me = ids[0, 1]
    total = jnp.zeros((STATE, WIDE), F32)
    gap = jnp.zeros((1, WIDE), F32)
    for back, message in enumerate((m1, m2, m3)):
        tail = message[STATE:].astype(F32)
        log = tail[0:1] + tail[1:2]
        state[STATE + 8 * back : STATE + 8 * back + 8] = jnp.broadcast_to(log, (8, WIDE))
        scale = jnp.exp(gap) * jnp.where(me > back, 1.0, 0.0)
        total = total + scale * message[:STATE].astype(F32)
        gap = gap + log
    state[:STATE] = total
    inside = before[:, WITHIN] + dot(narrow[:, CMAT], total) * spread[:, GROWN]
    after[:, INSIDE] = inside
    whole = inside + before[:, SKIPPED]
    after[:, MIXED] = whole
    gated = whole * before[:, GATE]
    ones = jnp.ones((8, WIDE), F32)
    squares = pick(ones, gated * gated, 1, 1)
    crosses = pick(ones, before[:, SCALED] * whole, 1, 1)
    sums[...] = jnp.where(iota((8, T), 0) < 4, squares, crosses)


def gate_ready(ids, after, before, consts, ready):
    mixed, act = after[:, MIXED], before[:, GATE]
    gated, rest = mixed * act, mixed * before[:, GATE_SLOPE]
    ready[0] = gated * act
    ready[1] = before[:, GRAD_NORMED] * consts[5:6, :WIDE] * rest
    ready[2] = gated * rest
    ready[3] = gated * consts[5:6, :WIDE]
    ready[4] = before[:, GRAD_NORMED] * gated


def gate_back(ids, s0, s1, s2, s3, ready, before, spread, narrow, gated_low, grad_mixed, grad_gain, sensitivity):
    total = s0[...] + s1[...] + s2[...] + s3[...]
    chosen = flag(iota((8, 128), 0) == 4 * iota((8, 128), 1))
    columns = sum(dot_first(part, chosen) for part in split(total, 3))
    inv = lax.rsqrt(columns[:, 0:1] / INNER + EPSILON)
    back = inv * (inv * inv * columns[:, 1:2] / INNER)
    own = inv * before[:, SCALED] - back * ready[0]
    grad_mixed[...] = own
    sensitivity[...] = dot_first(narrow[:, CMAT], own * spread[:, GROWN]).astype(BF16)
    gated_low[:, LOW_GATE] = (inv * ready[1] - back * ready[2]).astype(BF16)
    gated_low[:, NORMED] = (inv * ready[3]).astype(BF16)
    grad_gain[...] = jnp.broadcast_to(jnp.sum(inv * ready[4], axis=0, keepdims=True), (8, WIDE))


def turn_out(ids, source, keep, send):
    chip, core = ids[0, 2] >> 1, ids[0, 2] & 1
    for ahead in range(4):
        start = ((chip + ahead) & 3) * 2
        keep[ahead] = source[aligned((start + core) * SHARE, SHARE)]
        send[ahead] = source[aligned((start + 1 - core) * SHARE, SHARE)]


def middle(
    ids, hidden_in, gated_low, cotangent, gate_out, wide, narrow, grad_mixed, gate, out, grads, branch
):
    gate[...] = dot_first(hidden_in[RIM:], gated_low[:, LOW_GATE]).astype(BF16)
    out[...] = dot_first(cotangent[...], gated_low[:, NORMED]).astype(BF16)
    branch[...] = dot_last(gated_low[:, NORMED], gate_out[:, WIDE:]).astype(BF16)
    bmat, cmat, weighted = narrow[:, BMAT], narrow[:, CMAT], narrow[:, WEIGHTED]
    scores = dot_last(cmat, bmat)
    log_decay = wide[:, LOG_DECAY]
    turned = log_decay.T
    lower = iota((T, 128), 1) < 64
    grad_scores = jnp.zeros((T, T), F32)
    for pair in range(HEADS // 2):
        part = weighted[:, pair_columns(pair)]
        grad = grad_mixed[:, pair_columns(pair)]
        got = []
        for side in range(2):
            weights = decays(log_decay, turned, 2 * pair + side)
            got.append(dot_first(scores * weights, grad))
            own = jnp.where(lower, grad, 0.0) if side == 0 else jnp.where(lower, 0.0, grad)
            grad_scores = grad_scores + twice(own, part, 1, 1) * weights
        grads[:, pair_columns(pair)] = jnp.where(lower, got[0], got[1])
    grads[:, WIDE : WIDE + STATE] = twice(grad_scores, cmat, 0, 0)
    grads[:, WIDE + STATE :] = twice(grad_scores, bmat, 1, 0)


def leave(
    ids, g1, g2, g3, state, after, grad_mixed, grads, wide, spread, slope, narrow, consts, taken, grad_gain,
    low, state_low, keep, send, small, turned,
):
    me = ids[0, 1]
    end = jnp.zeros((STATE, WIDE), F32)
    gap = jnp.zeros((1, WIDE), F32)
    for ahead, message in enumerate((g1, g2, g3)):
        scale = jnp.exp(gap) * jnp.where(me + ahead < 3, 1.0, 0.0)
        end = end + scale * message[...].astype(F32)
        start = STATE + 8 * (2 - ahead)
        gap = gap + state[start : start + 1]
    step, step_slope = wide[:, STEP], wide[:, STEP_SLOPE]
    values = wide[:, VALUES]
    last = wide[T - 1 :, LOG_DECAY]
    to_end = spread[:, TO_END]
    weighted = narrow[:, WEIGHTED].astype(F32)
    own = grad_mixed[...]
    from_end = dot(narrow[:, BMAT], end) * to_end
    inputs = grads[:, :WIDE] + from_end
    from_b = grads[:, WIDE : WIDE + STATE]
    from_b = from_b + sum(dot_last(weighted * to_end, part) for part in split(end, 2))
    from_c = grads[:, WIDE + STATE :]
    from_c = from_c + sum(
        dot_last(own * spread[:, GROWN], part) for part in split(state[:STATE], 2)
    )
    grad_log = head_sums(own.astype(BF16).astype(F32) * after[:, INSIDE] - weighted * inputs)
    at_end = jnp.sum(weighted * from_end, axis=0, keepdims=True) + jnp.exp(
        spread_heads(last)
    ) * jnp.sum(end * state[:STATE], axis=0, keepdims=True)
    at_end = head_sums(jnp.broadcast_to(at_end, (8, WIDE)))[0:1]
    grad_decay = pick(flag(iota((T, T), 0) <= iota((T, T), 1)), grad_log, 1, 0) + at_end
    rate = jnp.exp(consts[7:8, :128])
    grad_step = head_sums(values * inputs) - rate * grad_decay
    grad_step_pre = grad_step * step_slope
    grad_values = own * spread_heads(consts[8:9, :128]) + inputs * spread[:, STEPS]
    grad_pre = jnp.concatenate([grad_values, from_b, from_c], axis=1) * slope[...]
    before = taken[...].astype(F32)
    padded = jnp.concatenate([jnp.zeros((RIM, MIX), F32), grad_pre], axis=0)
    grad_input = jnp.zeros((EXT, MIX), F32)
    line = iota((8, MIX), 0)
    taps = jnp.where(line == KERNEL, jnp.sum(grad_pre, axis=0, keepdims=True), 0.0)
    for tap in range(KERNEL):
        later = roll(padded, tap + 1 - KERNEL, 0)
        taps = jnp.where(line == tap, jnp.sum(before * later, axis=0, keepdims=True), taps)
        grad_input = grad_input + consts[tap : tap + 1, :MIX] * later
    low[:, :WIDE] = grad_input[:, :WIDE].astype(BF16)
    state_low[...] = grad_input[:, WIDE:]
    low_step = jnp.concatenate([jnp.zeros((RIM, 128), F32), grad_step_pre], axis=0)
    low[:, WIDE:] = roll(low_step, STEP_LANE, 1).astype(BF16)
    rest = jnp.zeros((TURNED - EXT - 8, 2 * STATE), F32)
    turned[...] = jnp.concatenate([grad_input[:, WIDE:], taps[:, WIDE:], rest], axis=0).T
    turn_out(ids, turned, keep, send)
    heads = (
        jnp.sum(grad_step_pre, axis=0, keepdims=True),
        -rate * jnp.sum(grad_decay * step, axis=0, keepdims=True),
        head_sums(jnp.broadcast_to(jnp.sum(own * values, axis=0, keepdims=True), (8, WIDE)))[0:1],
    )
    none = jnp.zeros((1, 128), F32)
    heads = jnp.concatenate([heads[0] + roll(heads[1], 64, 1), heads[2], none], axis=1)
    line = iota((8, WIDE), 0)
    small[...] = jnp.where(line == 5, grad_gain[...], jnp.where(line == 6, heads, taps[:, :WIDE]))


def pair_sum(ids, keep, got, *shares):
    for ahead, share in enumerate(shares):
        share[...] = (keep[ahead].astype(F32) + got[ahead].astype(F32)).astype(share.dtype)


def value_grads(
    ids, low, state_low, gated_low, weights, gate_out, hidden_in, pair, value, head
):
    value[...] = dot_first(hidden_in[...], low[:, :WIDE]).astype(BF16)
    part = dot_last(low[:, :WIDE], weights[:, :WIDE]) + dot_last(low[:, WIDE:], weights[:, MIX:])
    high, rest = split(state_low[...], 2)
    part = part + dot_last(high, weights[:, WIDE:MIX]) + dot_last(rest, weights[:, WIDE:MIX])
    head[:RIM] = part[:RIM]
    head[RIM:] = part[RIM:] + dot_last(gated_low[:, LOW_GATE], gate_out[:, :WIDE])


def share_out(ids, head, branch, keep, send, whole):
    whole[...] = head[RIM:].astype(BF16)
    chip, core = ids[0, 2] >> 1, ids[0, 2] & 1
    for other in range(4):
        start = (chip ^ other) * 2
        for half, source in enumerate((whole, branch)):
            rows = slice(half * SHARE, half * SHARE + SHARE)
            keep[other, rows] = source[aligned((start + core) * SHARE, SHARE)]
            send[other, rows] = source[aligned((start + 1 - core) * SHARE, SHARE)]


def fold(small):
    pieces = []
    for chunk in range(6):
        piece = small[:, pair_columns(chunk // 2)]
        pieces.append(piece if chunk % 2 else roll(piece, 64, 1))
    folded = jnp.concatenate(pieces, axis=0)
    high = folded.astype(BF16).astype(F32)
    return jnp.concatenate([high, folded - high], axis=0)


def unfold(block):
    folded = block[:48] + block[48:]
    lower = iota((8, 128), 1) < 64
    pairs = []
    for pair in range(3):
        one, two = folded[16 * pair : 16 * pair + 8], folded[16 * pair + 8 : 16 * pair + 16]
        pairs.append(jnp.where(lower, roll(one, 64, 1), two))
    return jnp.concatenate(pairs, axis=1)


def tidy(block):
    folded = block[:48] + block[48:]
    high = folded.astype(BF16).astype(F32)
    parts = jnp.concatenate([high, folded - high], axis=0)
    return jnp.where(iota((ROWS, 128), 1) < 64, block, parts)


def late_grads(
    ids, t0, t1, t2, t3, low, small, head, rim, units, hidden_in, gate, out, value, branch, keep, send, *targets
):
    targets, tail, whole = targets[:-2], targets[-2], targets[-1]
    total = t0[...] + t1[...] + t2[...] + t3[...]
    straight = jnp.concatenate([total, jnp.zeros((128 - PART, TURNED), F32)], axis=0).T
    low_tail = low[:, WIDE:].astype(F32) + straight[:EXT]
    terms = jnp.sum(head[:RIM] * unit_rows(rim[...]), axis=0, keepdims=True)
    terms = terms + jnp.sum(head[RIM:] * units[...], axis=0, keepdims=True)
    grads = dot_first(hidden_in[...], low_tail)
    row = jnp.where(iota((8, D), 0) == 0, terms, 0.0)
    chosen = flag(iota((8, 128), 1) == GAIN_LANE)
    grads = grads + sum(dot_first(part, chosen) for part in split(row, 2))
    tail[...] = grads.astype(BF16)
    own = straight[EXT : EXT + 8]
    row = jnp.concatenate([own[0:1] + roll(own[1:2], 64, 1), own[2:3] + roll(own[3:4], 64, 1), own[4:5]], axis=1)
    folded = fold(jnp.where(iota((8, WIDE), 0) == 7, row, small[...]))
    lanes = iota((ROWS, 128), 1) < 64
    for target, place, block in places(ids, 0, targets[:5]):
        rows = aligned(block * ROWS, ROWS)
        target[place, :, :WIDE] = gate[rows]
        target[place, :, WIDE:] = value[rows]
    for target, place, block in places(ids, 1, targets[5:]):
        rows = aligned(block * ROWS, ROWS)
        target[place, :ROWS, :OUT_RIGHT] = out[rows]
        end = jnp.where(lanes, tail[rows].astype(F32), folded)
        target[place, :ROWS, OUT_RIGHT:] = end.astype(BF16)
    share_out(ids, head, branch, keep, send, whole)
    last = head[:RIM][8:]
    pieces = [last[:, RIGHT * chunk : RIGHT * chunk + RIGHT] for chunk in range(D // RIGHT)]
    pieces.append(jnp.zeros((8, RIGHT), F32))
    for slot in range(2):
        targets[8][slot, ROWS:] = jnp.concatenate(pieces[2 * slot : 2 * slot + 2], axis=0).astype(BF16)


def places(ids, side, targets):
    line, ctx = ids[0, 0], ids[0, 1]
    for far in range(4):
        for near in range(4):
            slot, place = far + far // 3, near
            if far == 2 and near >= 2:
                slot, place = 3, near - 2
            one, two = (near, far) if side else (far, near)
            yield targets[slot], place, ((line + one) & 3) * 4 + ((ctx + two) & 3)


def put(target, total, tailed):
    if tailed:
        target[:, :OUT_RIGHT] = total[:, :OUT_RIGHT].astype(BF16)
        target[:, OUT_RIGHT:] = tidy(total[:, OUT_RIGHT:]).astype(BF16)
    else:
        target[...] = total.astype(BF16)


def pair_halves(ids, keep, got, near, far):
    for other in range(4):
        target = far if other % 2 else near
        total = keep[other].astype(F32) + got[other].astype(F32)
        target[other // 2] = total.astype(BF16)


def relay(side, one, three, first, second, to_one, to_three):
    for near in range(4):
        if near < 2:
            total = one[near].astype(F32) + first[near].astype(F32)
            put(to_one.at[near], total, side)
            to_three[near] = three[near]
        else:
            total = three[near].astype(F32) + second[near - 2, :ROWS].astype(F32)
            put(to_three.at[near], total, side)
            to_one[near] = one[near]


def relay_both(ids, *refs):
    relay(0, *refs[:4], *refs[9:11])
    relay(1, *refs[4:8], *refs[11:13])
    second, behind = refs[7], refs[13]
    inside = jnp.where(ids[0, 1] < 3, 1.0, 0.0)
    for chunk in range(D // RIGHT):
        got = second[chunk // 2, ROWS:].astype(F32) * inside
        start = 8 * (chunk % 2)
        behind[:, RIGHT * chunk : RIGHT * chunk + RIGHT] = got[start : start + 8]


def halfway(side, own, one, three, *targets):
    for near, target in enumerate(targets):
        total = own[near].astype(F32) + one[near].astype(F32) + three[near].astype(F32)
        put(target, total, side)


def halfway_both(ids, l0, l1, l3, r0, r1, r3, own, *targets):
    halfway(0, l0, l1, l3, *targets[:4])
    halfway(1, r0, r1, r3, *targets[4:])


def pair_again(ids, near, got, cotangent, hidden, own, second, held, mine, last):
    for index, target in enumerate((own, second)):
        target[...] = (near[index].astype(F32) + got[index].astype(F32)).astype(BF16)
    held[...] = cotangent[...]
    mine[...] = hidden[aligned(ids[0, 2] * SHARE, SHARE)]
    last[...] = hidden[T - RIM :].astype(F32)[8:]


def collect_left(ids, a0, a1, a2, a3, b0, b1, b2, b3, grad_gate, grad_value, grad_out):
    total = sum(part[...].astype(F32) for part in (a0, a1, a2, a3))
    grad_gate[...] = total[:, :WIDE]
    grad_value[...] = total[:, WIDE:]
    grad_out[...] = sum(part[:, :OUT_RIGHT].astype(F32) for part in (b0, b1, b2, b3))


def hidden_back(grads, rows, gain):
    tokens = rows.astype(F32)
    inv = lax.rsqrt(jnp.mean(tokens * tokens, axis=1, keepdims=True) + EPSILON)
    unit = tokens * inv
    scaled = grads * gain
    return inv * (scaled - unit * jnp.mean(scaled * unit, axis=1, keepdims=True)), tokens


def gather_up(
    ids, b0, b1, b2, b3, p0, p1, mine, weights, behind,
    message, gain_out, grad_step, taps, offset, gain, bias, decay, skip, rest,
):
    both = p0[...].astype(F32) + p1[...].astype(F32)
    row = gain_row(weights[:, MIX:])
    gain_out[...] = jnp.broadcast_to(row, (8, D))
    grads, tokens = hidden_back(both[:SHARE], mine[...], row)
    message[:SHARE] = grads.astype(BF16)
    message[SHARE : 2 * SHARE] = (tokens + both[SHARE:]).astype(BF16)
    total = sum(part[:, OUT_RIGHT:].astype(F32) for part in (b0, b1, b2, b3))
    rest[...] = total
    small = unfold(total)
    state = small[7:8]
    lanes = iota((8, 128), 1)
    for tap in range(KERNEL + 1):
        piece = state[:, pair_columns(tap // 2)]
        piece = piece if tap % 2 == 0 else roll(piece, 64, 1)
        if tap == 0:
            rows = jnp.where(iota((8, 128), 0) == 0, roll(piece, STATE_LANE, 1), 0.0)
        else:
            rows = jnp.where(iota((8, 128), 0) == tap, roll(piece, STATE_LANE, 1), rows)
    rest[:8] = jnp.where(lanes < 64, rest[:8], rows)
    for block in range(ROWS // 16):
        message[2 * SHARE :, pair_columns(block)] = rest[16 * block : 16 * block + 16].astype(BF16)
    for block in range(6):
        pair = [behind[:, pair_columns(2 * block + i)] for i in range(2)]
        message[2 * SHARE :, pair_columns(6 + block)] = jnp.concatenate(pair, axis=0).astype(BF16)
    picked = flag(iota((8, 128), 1) == STEP_LANE + iota((8, 128), 0))
    grad_step[...] = pick(picked, total, 1, 1, 3)[:HEADS]
    taps[...] = small[:KERNEL]
    offset[...] = small[KERNEL : KERNEL + 1]
    gain[...] = small[5:6]
    bias[...] = small[6:7, :HEADS]
    decay[...] = small[6:7, 64 : 64 + HEADS]
    skip[...] = small[6:7, 128 : 128 + HEADS]


def finish(ids, *refs):
    pieces, row, cotangent, last = refs[:8], refs[8], refs[9], refs[10]
    grad_hidden, block_out, grad_state, grad_gain, taps, offset, rest, rims = refs[11:]
    chip, core = ids[0, 2] >> 1, ids[0, 2] & 1
    order = []
    for far in range(4):
        start = ((chip - far) & 3) * 2
        order += [(start + core, pieces[far]), (start + 1 - core, pieces[4 + far])]
    for place, piece in order:
        block_out[aligned(place * SHARE, SHARE)] = piece[SHARE : 2 * SHARE]
        for block in range(6):
            part = piece[2 * SHARE :, pair_columns(block)]
            rest[place, 16 * block : 16 * block + 16] = part.astype(F32)
            part = piece[2 * SHARE :, pair_columns(6 + block)].astype(F32)
            rims[place, :, pair_columns(2 * block)] = part[:8]
            rims[place, :, pair_columns(2 * block + 1)] = part[8:]
    total, behind = rest[0], rims[0]
    for i in range(1, 8):
        total = total + rest[i]
        behind = behind + rims[i]
    for place, piece in order:
        rows = aligned(place * SHARE, SHARE)
        grad_hidden[rows] = cotangent[rows].astype(F32) + piece[:SHARE].astype(F32)
    grads, _ = hidden_back(behind, last[...], row[0:1])
    grad_hidden[T - 8 :] = grad_hidden[T - 8 :] + grads
    lanes = iota((ROWS, 128), 1) >> 5
    for half in range(2):
        state = jnp.zeros((ROWS, 128), F32)
        small = jnp.zeros((8, 128), F32)
        for i in range(4):
            one = rest[4 * half + i]
            state = jnp.where(lanes == i, roll(one, PART * i, 1), state)
            small = jnp.where(lanes[:8] == i, roll(one[:8], PART * i - STATE_LANE, 1), small)
        columns = pair_columns(half)
        grad_state[:, columns] = state
        taps[:, columns] = small[:KERNEL]
        offset[:, columns] = small[KERNEL : KERNEL + 1]
    grad_gain[...] = pick(flag(iota((8, 128), 1) == GAIN_LANE), total, 1, 1, 3)[0:1]


def stack_blocks(ids, l0, l1, l2, l3, r0, r1, r2, r3, left, right, rim):
    for i, (one, two) in enumerate(((l0, r0), (l1, r1), (l2, r2), (l3, r3))):
        left[i] = one[:ROWS]
        right[i] = two[...]
    inside = jnp.where(ids[0, 1] > 0, 1.0, 0.0)
    got = l1[ROWS:].astype(F32) * inside
    none = jnp.zeros((8, PAIR), F32)
    rim[:, :PAIR] = jnp.concatenate([none, got[:8]], axis=0).astype(BF16)
    rim[:, PAIR:] = jnp.concatenate([none, got[8:]], axis=0).astype(BF16)


def shift(array, axis, steps):
    return lax.ppermute(array, axis, [(i, (i + steps) % 4) for i in range(4)])


def from_chip(array, steps):
    return lax.ppermute(array, "tp", [(i, (i + 2 * steps) % 8) for i in range(8)])


def across(array, bits):
    return lax.ppermute(array, "tp", [(i, i ^ bits) for i in range(8)])


def around(array, axis):
    return [array] + [shift(array, axis, steps) for steps in range(1, 4)]


def ring_sides(array, axis):
    return shift(array, axis, 1), shift(array, axis, 3)


def ring_rest(array, axis, one, three):
    return [array, one, shift(one[:2], axis, 1), shift(three[2:], axis, 3), three]


def chips_all(array):
    same = [array] + [from_chip(array, steps) for steps in range(1, 4)]
    return same + [across(one, 1) for one in same]


def per_device(
    hidden_states,
    norm_gain,
    gate_weight,
    value_weight,
    state_proj,
    step_proj,
    value_filter,
    value_offset,
    state_filter,
    state_offset,
    step_bias,
    decay_log,
    skip_gain,
    gate_norm_gain,
    out_weight,
    out_grad,
):
    hidden = hidden_states[0]
    cotangent = out_grad[0]
    places = [lax.axis_index(axis).astype(jnp.int32) for axis in ("dp", "ctx", "tp")]
    ids = jnp.stack(places).reshape(1, 3)

    left, longer, right = fuse(
        prepare,
        [((ROWS, PAIR), BF16), ((ROWS + RIM, PAIR), BF16), ((ROWS, PAIR), BF16)],
        ids,
        value_weight,
        gate_weight,
        state_proj,
        step_proj.T,
        norm_gain[None],
        out_weight.T,
        hidden,
        fetch=7,
        rim=True,
    )
    near = [left, shift(longer, "ctx", 1), shift(left, "ctx", 2), shift(left, "ctx", 3)]
    left, right, rim = fuse(
        stack_blocks,
        [((4, ROWS, PAIR), BF16)] * 2 + [((RIM, D), BF16)],
        ids,
        *near,
        *around(right, "dp"),
    )
    consts, units = fuse(
        tabulate,
        [((16, FIRST), F32), ((T, D), F32)],
        ids,
        value_filter,
        state_filter,
        value_offset[None],
        state_offset[None],
        gate_norm_gain[None],
        jnp.stack([step_bias, decay_log, skip_gain]),
        hidden,
        fetch=7,
    )
    left = ring_rest(left, "dp", *ring_sides(left, "dp"))
    right = ring_rest(right, "ctx", *ring_sides(right, "ctx"))
    weights, hidden_in, taken, wide, narrow, message = fuse(
        enter,
        [
            ((D, FIRST), BF16),
            ((EXT, D), BF16),
            ((EXT, MIX), BF16),
            ((T, LOG_DECAY.stop), F32),
            ((T, WEIGHTED.stop), BF16),
            ((STATE + 16, WIDE), BF16),
        ],
        ids,
        *left,
        *right,
        rim,
        units,
        consts,
    )
    messages = around(message, "ctx")[1:]
    gate_out, before, slope, spread = fuse(
        project,
        [((D, 2 * WIDE), BF16), ((T, SKIPPED.stop), F32), ((T, MIX), F32), ((T, STEPS.stop), F32)],
        ids,
        *left,
        *right,
        hidden_in,
        cotangent,
        wide,
        narrow,
        consts,
    )
    state, after, sums = fuse(
        mix,
        [((STATE + 24, WIDE), F32), ((T, MIXED.stop), F32), ((8, T), F32)],
        ids,
        *messages,
        spread,
        narrow,
        before,
    )
    (ready,) = fuse(gate_ready, [((5, T, WIDE), F32)], ids, after, before, consts)
    sums = sums + across(sums, 1)
    gated_low, grad_mixed, grad_gain, sensitivity = fuse(
        gate_back,
        [
            ((T, LOW_GATE.stop), BF16),
            ((T, WIDE), F32),
            ((8, WIDE), F32),
            ((STATE, WIDE), BF16),
        ],
        ids,
        sums,
        *[from_chip(sums, steps) for steps in range(1, 4)],
        ready,
        before,
        spread,
        narrow,
    )
    later = [shift(sensitivity, "ctx", -steps) for steps in range(1, 4)]
    square = ((D, WIDE), BF16)
    gate, out, grads, branch = fuse(
        middle,
        [square, square, ((T, MIX), F32), ((T, D), BF16)],
        ids,
        hidden_in,
        gated_low,
        cotangent,
        gate_out,
        wide,
        narrow,
        grad_mixed,
    )
    low, state_low, keep, send, small = fuse(
        leave,
        [((EXT, WIDE + 128), BF16), ((EXT, 2 * STATE), F32)] + [((4, PART, TURNED), F32)] * 2 + [((8, WIDE), F32)],
        ids,
        *later,
        state,
        after,
        grad_mixed,
        grads,
        wide,
        spread,
        slope,
        narrow,
        consts,
        taken,
        grad_gain,
        scratch=[((2 * STATE, TURNED), F32)],
    )
    pair = fuse(pair_sum, [((PART, TURNED), F32)] * 4, ids, keep, across(send, 1))
    turned = pair[:1] + [from_chip(pair[steps], steps) for steps in range(1, 4)]
    value, head = fuse(
        value_grads,
        [square, ((EXT, D), F32)],
        ids,
        low,
        state_low,
        gated_low,
        weights,
        gate_out,
        hidden_in,
        pair[0],
    )
    both = ((2 * SHARE, D), BF16)
    two = ((2, 2 * SHARE, D), BF16)

    def stage(count, rows, columns):
        return (count, rows, columns), BF16

    def stages(columns, rows):
        whole = stage(4, ROWS, columns)
        return [whole, whole, stage(2, ROWS, columns), stage(2, rows, columns), whole]

    keep, send, *blocks = fuse(
        late_grads,
        [((4, 2 * SHARE, D), BF16)] * 2 + stages(LEFT, ROWS) + stages(RIGHT, ROWS + RIM),
        ids,
        *turned,
        low,
        small,
        head,
        rim,
        units,
        hidden_in,
        gate,
        out,
        value,
        branch,
        scratch=[((D, 128), BF16), ((T, D), BF16)],
    )
    left, right = blocks[:5], blocks[5:]
    near, far = fuse(pair_halves, [two] * 2, ids, keep, across(send, 1))
    *sides, behind = fuse(
        relay_both,
        [stage(4, ROWS, LEFT)] * 2 + [stage(4, ROWS, RIGHT)] * 2 + [((8, D), F32)],
        ids,
        *(left[1], left[4], shift(left[2], "dp", 1), shift(left[3], "dp", 3)),
        *(right[1], right[4], shift(right[2], "ctx", 1), shift(right[3], "ctx", 3)),
        near,
    )
    left = [left[0], shift(sides[0], "dp", 1), shift(sides[1], "dp", 3)]
    right = [right[0], shift(sides[2], "ctx", 1), shift(sides[3], "ctx", 3)]
    own, second, held, mine, last = fuse(
        pair_again,
        [both, both, ((T, D), BF16), ((SHARE, D), BF16), ((8, D), F32)],
        ids,
        near,
        across(far, 2),
        cotangent,
        hidden,
    )
    sums = fuse(
        halfway_both,
        [((ROWS, LEFT), BF16)] * 4 + [((ROWS, RIGHT), BF16)] * 4,
        ids,
        *left,
        *right,
        own,
    )
    left = sums[:1] + [shift(sums[steps], "ctx", steps) for steps in range(1, 4)]
    right = sums[4:5] + [shift(sums[4 + steps], "dp", steps) for steps in range(1, 4)]
    few, line = ((1, HEADS), F32), ((1, WIDE), F32)
    message, gain_full, *few_grads = fuse(
        gather_up,
        [((2 * SHARE + 16, D), BF16), ((8, D), F32), ((HEADS, ROWS), F32), ((KERNEL, WIDE), F32)]
        + [line, line, few, few, few],
        ids,
        *right,
        own,
        across(second, 4),
        mine,
        weights,
        behind,
        scratch=[((ROWS, 128), F32)],
    )
    grad_step, taps, offset, gain, bias, decay, skip = few_grads
    grad_gate, grad_value, grad_out = fuse(
        collect_left, [((ROWS, WIDE), F32)] * 3, ids, *left, *right
    )
    grad_hidden, block_out, grad_state, grad_norm_gain, state_taps, state_offset = fuse(
        finish,
        [
            ((T, D), F32),
            ((T, D), BF16),
            ((ROWS, 2 * STATE), F32),
            ((1, ROWS), F32),
            ((KERNEL, 2 * STATE), F32),
            ((1, 2 * STATE), F32),
        ],
        ids,
        *chips_all(message),
        gain_full,
        held,
        last,
        scratch=[((8, ROWS, 128), F32), ((8, 8, D), F32)],
    )
    return (
        block_out[None],
        grad_hidden[None],
        grad_norm_gain[0],
        grad_gate,
        grad_value,
        grad_state,
        grad_step.T,
        taps,
        offset[0],
        state_taps,
        state_offset[0],
        bias[0],
        decay[0],
        skip[0],
        gain[0],
        grad_out.T,
    )


def solution(mesh):
    line = P(("dp", "ctx"))
    placed = (
        P("dp", "ctx", None),
        line,
        P(("dp", "ctx"), "tp"),
        P(("dp", "ctx"), "tp"),
        P(("dp", "ctx"), None),
        P(("dp", "ctx"), "tp"),
        P(None, "tp"),
        P("tp"),
        P(),
        P(),
        P("tp"),
        P("tp"),
        P("tp"),
        P("tp"),
        P("tp", ("dp", "ctx")),
        P("dp", "ctx", None),
    )
    given = (
        P("dp", "ctx", None),
        P("dp", "ctx", None),
        line,
        P(("dp", "ctx"), "tp"),
        P(("dp", "ctx"), "tp"),
        P(("dp", "ctx"), None),
        P(("dp", "ctx"), "tp"),
        P(None, "tp"),
        P("tp"),
        P(),
        P(),
        P("tp"),
        P("tp"),
        P("tp"),
        P("tp"),
        P("tp", ("dp", "ctx")),
    )
    return jax.shard_map(
        per_device, mesh=mesh, in_specs=placed, out_specs=given, check_vma=False
    )
```

```python
import jax
import jax.numpy as jnp
from jax import lax
from jax.experimental import pallas as pl
from jax.experimental.pallas import tpu as pltpu
from jax.sharding import PartitionSpec as P

F32 = jnp.float32
BF16 = jnp.bfloat16
EPSILON = 1e-05
INNER = 3072
D = 1536
T = 256
RIM = 16
EXT = T + RIM
KERNEL = 4
HEADS = 6
WIDE = 384
STATE = 128
MIX = WIDE + 2 * STATE
FIRST = MIX + 128
ROWS = 96
SHARES = 16
PAIR = 2 * WIDE
RIGHT = 512
OUT_RIGHT = RIGHT - 128
LEFT = 3 * WIDE - OUT_RIGHT
SHARE = T // 8
PART = 32
STEP_LANE = 32
GAIN_LANE = STEP_LANE + HEADS
STATE_LANE = 64
TURNED = 384
VMEM_LIMIT = 8 * 2**20

VALUES, SLOPE = slice(0, WIDE), slice(WIDE, WIDE + MIX)
STEP, STEP_SLOPE, LOG_DECAY = slice(1024, 1152), slice(1152, 1280), slice(1280, 1408)
BMAT, CMAT, WEIGHTED = slice(0, 128), slice(128, 256), slice(256, 640)
GATE, GRAD_NORMED, WITHIN = slice(0, 384), slice(384, 768), slice(768, 1152)
GATE_SLOPE, SCALED, SKIPPED = slice(1152, 1536), slice(1536, 1920), slice(1920, 2304)
INSIDE, MIXED = slice(0, 384), slice(384, 768)
NORMED, LOW_GATE = slice(0, 384), slice(384, 768)
GROWN, TO_END, STEPS = slice(0, 384), slice(384, 768), slice(768, 1152)


WORK = {"pair_again": 2 * 10**9, "collect_left": 5 * 10**9}


def fuse(function, outputs, ids, *arrays, scratch=(), fetch=0, rim=False):
    count = len(arrays)
    plain = count - fetch
    shapes = [array.shape for array in arrays]
    if rim:
        shapes[-1] = (RIM, D)

    def body(*refs):
        if not fetch:
            function(*refs)
            return
        given = list(refs[1 + plain : 1 + count])
        held, done = refs[-1 - fetch : -1], refs[-1]
        if rim:
            given[-1] = given[-1].at[pl.ds(T - RIM, RIM)]
        copies = [
            pltpu.make_async_copy(source, target, done.at[i])
            for i, (source, target) in enumerate(zip(given, held))
        ]
        for copy in copies:
            copy.start()

        def ready():
            for copy in copies:
                copy.wait()

        function(*refs[: 1 + plain], *held, *refs[1 + count : -1 - fetch], ready=ready)

    buffers = [pltpu.VMEM(shape, dtype) for shape, dtype in scratch]
    spaces = [pltpu.SMEM] + [pltpu.VMEM] * plain + [pltpu.HBM] * fetch
    if fetch:
        buffers += [pltpu.VMEM(shapes[i], arrays[i].dtype) for i in range(plain, count)]
        buffers += [pltpu.SemaphoreType.DMA((fetch,))]
        held = [pltpu.with_memory_space_constraint(array, pltpu.HBM) for array in arrays[plain:]]
        arrays = (*arrays[:plain], *held)
    cost = None
    if function.__name__ in WORK:
        cost = pl.CostEstimate(
            flops=WORK[function.__name__], bytes_accessed=10**6, transcendentals=1
        )
    call = pl.pallas_call(
        body,
        out_shape=[jax.ShapeDtypeStruct(shape, dtype) for shape, dtype in outputs],
        in_specs=[pl.BlockSpec(memory_space=space) for space in spaces],
        out_specs=[pl.BlockSpec(memory_space=pltpu.VMEM) for _ in outputs],
        scratch_shapes=buffers,
        compiler_params=pltpu.CompilerParams(vmem_limit_bytes=VMEM_LIMIT),
        cost_estimate=cost,
        name=function.__name__,
    )
    return list(call(ids, *arrays))


def roll(array, shift, axis):
    return pltpu.roll(array, shift % array.shape[axis], axis)


def product(a, b, left, right):
    return lax.dot_general(
        a.astype(BF16),
        b.astype(BF16),
        (((left,), (right,)), ((), ())),
        preferred_element_type=F32,
    )


def dot(a, b):
    return product(a, b, 1, 0)


def dot_last(a, b):
    return product(a, b, 1, 1)


def dot_first(a, b):
    return product(a, b, 0, 0)


def split(array, count):
    parts = []
    for _ in range(count):
        part = array.astype(BF16)
        parts.append(part)
        array = array - part.astype(F32)
    return parts


def twice(a, b, left, right):
    return sum(product(part, b, left, right) for part in split(a, 2))


def pick(chosen, array, left, right, parts=2):
    return sum(product(chosen, part, left, right) for part in split(array, parts))


def iota(shape, axis):
    return lax.broadcasted_iota(jnp.int32, shape, axis)


def flag(condition):
    return jnp.where(condition, 1.0, 0.0)


def silu_parts(array):
    sig = jax.nn.sigmoid(array)
    return array * sig, sig * (1.0 + array * (1.0 - sig))


def spread_heads(array):
    rows = array.shape[0]
    lower = iota((rows, 128), 1) < 64
    pieces = [
        jnp.where(lower, array[:, h : h + 1], array[:, h + 1 : h + 2]) for h in range(0, HEADS, 2)
    ]
    return jnp.concatenate(pieces, axis=1)


def head_sums(array):
    chosen = flag((iota((128, WIDE), 1) >> 6) == iota((128, WIDE), 0))
    return sum(dot_last(part, chosen) for part in split(array, 2))


def gain_row(tail):
    return dot_last(flag(iota((8, 128), 1) == GAIN_LANE), tail)[0:1]


def unit_rows(rows):
    tokens = rows.astype(F32)
    inv = lax.rsqrt(jnp.mean(tokens * tokens, axis=1, keepdims=True) + EPSILON)
    return tokens * inv


def aligned(start, size):
    return pl.ds(pl.multiple_of(start, size), size)


def prepare(
    ids, value_weight, gate_weight, state_proj, step_proj, norm_gain, out_weight, rim, left, longer, right, ready
):
    ready()
    for target in (left, longer):
        target[:ROWS, :WIDE] = value_weight[...]
        target[:ROWS, WIDE:] = gate_weight[...]
    last = rim[...].astype(F32)[8:]
    longer[ROWS:] = jnp.concatenate([last[:, :PAIR], last[:, PAIR:]], axis=0).astype(BF16)
    right[:, : 2 * STATE] = state_proj[...]
    place = iota((HEADS, 128), 1) == STEP_LANE + iota((HEADS, 128), 0)
    tail = dot_first(step_proj[...], flag(place))
    tail = tail + dot_first(norm_gain[...], flag(iota((1, 128), 1) == GAIN_LANE))
    right[:, 2 * STATE : WIDE] = tail.astype(BF16)
    right[:, WIDE:] = out_weight[...]


def tabulate(
    ids, value_filter, state_filter, value_offset, state_offset, gate_gain, heads, hidden, consts, units, ready
):
    ready()
    units[...] = unit_rows(hidden[...])
    consts[...] = jnp.zeros(consts.shape, F32)
    consts[:KERNEL, :WIDE] = value_filter[...].astype(F32)
    consts[:KERNEL, WIDE:MIX] = state_filter[...].astype(F32)
    consts[KERNEL : KERNEL + 1, :WIDE] = value_offset[...].astype(F32)
    consts[KERNEL : KERNEL + 1, WIDE:MIX] = state_offset[...].astype(F32)
    consts[5:6, :WIDE] = gate_gain[...].astype(F32)
    consts[6:9, :HEADS] = heads[...]


def place_blocks(ids, left, right, *moves):
    line, ctx = ids[0, 0], ids[0, 1]

    def piece(side, far, near):
        if far == 2:
            return (side[2], near) if near < 2 else (side[3], near - 2)
        return side[far + far // 3], near

    for far in range(4):
        for near in range(4):
            for target, side, start, source, size in moves:
                if side == 0:
                    block = ((line - far) & 3) * 4 + ((ctx - near) & 3)
                else:
                    block = ((line - near) & 3) * 4 + ((ctx - far) & 3)
                array, place = piece((left, right)[side], far, near)
                target[aligned(block * ROWS, ROWS), start : start + size] = array[
                    place, :, source : source + size
                ]


def enter(
    ids, l0, l1, l2, l3, l4, r0, r1, r2, r3, r4, rim, units, consts,
    weights, hidden_in, taken, wide, narrow, message,
):
    moves = (weights, 0, 0, 0, WIDE), (weights, 1, WIDE, 0, WIDE)
    place_blocks(ids, (l0, l1, l2, l3, l4), (r0, r1, r2, r3, r4), *moves)
    gain = gain_row(weights[:, MIX:])
    hidden_in[:RIM] = (unit_rows(rim[...]) * gain).astype(BF16)
    hidden_in[RIM:] = (units[...] * gain).astype(BF16)
    projected = dot(hidden_in[...], weights[...])
    inputs = projected[:, :MIX].astype(BF16)
    taken[...] = inputs
    inputs = inputs.astype(F32)
    filter_pre = consts[KERNEL : KERNEL + 1, :MIX]
    for tap in range(KERNEL):
        filter_pre = filter_pre + consts[tap : tap + 1, :MIX] * roll(inputs, KERNEL - 1 - tap, 0)[RIM:]
    wide[:, SLOPE] = filter_pre
    activated = filter_pre * jax.nn.sigmoid(filter_pre)
    lanes = iota((T, 128), 1) < HEADS
    step_in = roll(projected[RIM:, MIX:], 128 - STEP_LANE, 1) + consts[6:7, :128]
    step_in = jnp.where(lanes, step_in, -100.0)
    step = jnp.maximum(step_in, 0.0) + jnp.log1p(jnp.exp(-jnp.abs(step_in)))
    step = jnp.where(lanes, step, 0.0)
    rate = jnp.exp(consts[7:8, :128])
    log_decay = pick(flag(iota((T, T), 0) >= iota((T, T), 1)), -step * rate, 1, 0, 3)
    values = activated[:, :WIDE]
    weighted = (values * spread_heads(step)).astype(BF16)
    wide[:, VALUES] = values
    wide[:, STEP] = step
    wide[:, STEP_SLOPE] = jax.nn.sigmoid(step_in)
    wide[:, LOG_DECAY] = log_decay
    narrow[:, BMAT] = activated[:, WIDE : WIDE + STATE].astype(BF16)
    narrow[:, CMAT] = activated[:, WIDE + STATE :].astype(BF16)
    narrow[:, WEIGHTED] = weighted
    last = log_decay[T - 1 :]
    to_end = spread_heads(jnp.exp(last - log_decay))
    message[:STATE] = dot_first(narrow[:, BMAT], weighted.astype(F32) * to_end).astype(BF16)
    span = spread_heads(last)
    high = span.astype(BF16).astype(F32)
    line = iota((16, WIDE), 0)
    tail = jnp.where(line == 0, high, jnp.where(line == 1, span - high, 0.0))
    message[STATE:] = tail.astype(BF16)


def decays(log_decay, turned, head):
    gap = log_decay[:, head : head + 1] - turned[head : head + 1, :]
    return jnp.exp(jnp.where(iota((T, T), 0) >= iota((T, T), 1), gap, -1e30))


def pair_columns(pair):
    return slice(128 * pair, 128 * pair + 128)


def project(
    ids, l0, l1, l2, l3, l4, r0, r1, r2, r3, r4, hidden_in, cotangent, wide, narrow, consts,
    gate_out, before, slope, spread,
):
    moves = (gate_out, 0, 0, WIDE, WIDE), (gate_out, 1, WIDE, WIDE, WIDE)
    place_blocks(ids, (l0, l1, l2, l3, l4), (r0, r1, r2, r3, r4), *moves)
    _, slope[...] = silu_parts(wide[:, SLOPE])
    last = wide[T - 1 :, LOG_DECAY]
    spread[:, GROWN] = spread_heads(jnp.exp(wide[:, LOG_DECAY]))
    spread[:, TO_END] = spread_heads(jnp.exp(last - wide[:, LOG_DECAY]))
    spread[:, STEPS] = spread_heads(wide[:, STEP])
    act, gate_slope = silu_parts(dot(hidden_in[RIM:], gate_out[:, :WIDE]))
    grads = dot(cotangent[...], gate_out[:, WIDE:])
    before[:, GATE] = act
    before[:, GATE_SLOPE] = gate_slope
    before[:, GRAD_NORMED] = grads
    before[:, SCALED] = grads * consts[5:6, :WIDE] * act
    before[:, SKIPPED] = wide[:, VALUES] * spread_heads(consts[8:9, :128])
    scores = dot_last(narrow[:, CMAT], narrow[:, BMAT])
    log_decay = wide[:, LOG_DECAY]
    turned = log_decay.T
    lower = iota((T, 128), 1) < 64
    weighted = narrow[:, WEIGHTED]
    for pair in range(HEADS // 2):
        part = weighted[:, pair_columns(pair)]
        one = dot(scores * decays(log_decay, turned, 2 * pair), part)
        two = dot(scores * decays(log_decay, turned, 2 * pair + 1), part)
        start = WITHIN.start + 128 * pair
        before[:, start : start + 128] = jnp.where(lower, one, two)


def mix(ids, m1, m2, m3, spread, narrow, before, state, after, sums):
    me = ids[0, 1]
    total = jnp.zeros((STATE, WIDE), F32)
    gap = jnp.zeros((1, WIDE), F32)
    for back, message in enumerate((m1, m2, m3)):
        tail = message[STATE:].astype(F32)
        log = tail[0:1] + tail[1:2]
        state[STATE + 8 * back : STATE + 8 * back + 8] = jnp.broadcast_to(log, (8, WIDE))
        scale = jnp.exp(gap) * jnp.where(me > back, 1.0, 0.0)
        total = total + scale * message[:STATE].astype(F32)
        gap = gap + log
    state[:STATE] = total
    inside = before[:, WITHIN] + dot(narrow[:, CMAT], total) * spread[:, GROWN]
    after[:, INSIDE] = inside
    whole = inside + before[:, SKIPPED]
    after[:, MIXED] = whole
    gated = whole * before[:, GATE]
    ones = jnp.ones((8, WIDE), F32)
    squares = pick(ones, gated * gated, 1, 1)
    crosses = pick(ones, before[:, SCALED] * whole, 1, 1)
    sums[...] = jnp.where(iota((8, T), 0) < 4, squares, crosses)


def gate_ready(ids, after, before, consts, ready):
    mixed, act = after[:, MIXED], before[:, GATE]
    gated, rest = mixed * act, mixed * before[:, GATE_SLOPE]
    ready[0] = gated * act
    ready[1] = before[:, GRAD_NORMED] * consts[5:6, :WIDE] * rest
    ready[2] = gated * rest
    ready[3] = gated * consts[5:6, :WIDE]
    ready[4] = before[:, GRAD_NORMED] * gated


def gate_back(ids, s0, s1, s2, s3, ready, before, spread, narrow, gated_low, grad_mixed, grad_gain, sensitivity):
    total = s0[...] + s1[...] + s2[...] + s3[...]
    chosen = flag(iota((8, 128), 0) == 4 * iota((8, 128), 1))
    columns = sum(dot_first(part, chosen) for part in split(total, 3))
    inv = lax.rsqrt(columns[:, 0:1] / INNER + EPSILON)
    back = inv * (inv * inv * columns[:, 1:2] / INNER)
    own = inv * before[:, SCALED] - back * ready[0]
    grad_mixed[...] = own
    sensitivity[...] = dot_first(narrow[:, CMAT], own * spread[:, GROWN]).astype(BF16)
    gated_low[:, LOW_GATE] = (inv * ready[1] - back * ready[2]).astype(BF16)
    gated_low[:, NORMED] = (inv * ready[3]).astype(BF16)
    grad_gain[...] = jnp.broadcast_to(jnp.sum(inv * ready[4], axis=0, keepdims=True), (8, WIDE))


def turn_out(ids, source, keep, send):
    chip, core = ids[0, 2] >> 1, ids[0, 2] & 1
    for ahead in range(4):
        start = ((chip + ahead) & 3) * 2
        keep[ahead] = source[aligned((start + core) * SHARE, SHARE)]
        send[ahead] = source[aligned((start + 1 - core) * SHARE, SHARE)]


def middle(
    ids, hidden_in, gated_low, cotangent, gate_out, wide, narrow, grad_mixed, state, spread, after,
    gate, out, grads, branch, sums,
):
    gate[...] = dot_first(hidden_in[RIM:], gated_low[:, LOW_GATE]).astype(BF16)
    out[...] = dot_first(cotangent[...], gated_low[:, NORMED]).astype(BF16)
    branch[...] = dot_last(gated_low[:, NORMED], gate_out[:, WIDE:]).astype(BF16)
    bmat, cmat, weighted = narrow[:, BMAT], narrow[:, CMAT], narrow[:, WEIGHTED]
    scores = dot_last(cmat, bmat)
    log_decay = wide[:, LOG_DECAY]
    turned = log_decay.T
    lower = iota((T, 128), 1) < 64
    grad_scores = jnp.zeros((T, T), F32)
    for pair in range(HEADS // 2):
        part = weighted[:, pair_columns(pair)]
        grad = grad_mixed[:, pair_columns(pair)]
        got = []
        for side in range(2):
            weights = decays(log_decay, turned, 2 * pair + side)
            got.append(dot_first(scores * weights, grad))
            own = jnp.where(lower, grad, 0.0) if side == 0 else jnp.where(lower, 0.0, grad)
            grad_scores = grad_scores + twice(own, part, 1, 1) * weights
        grads[:, pair_columns(pair)] = jnp.where(lower, got[0], got[1])
    grads[:, WIDE : WIDE + STATE] = twice(grad_scores, cmat, 0, 0)
    own = grad_mixed[...]
    from_state = own * spread[:, GROWN]
    grads[:, WIDE + STATE :] = twice(grad_scores, bmat, 1, 0) + sum(
        dot_last(from_state, part) for part in split(state[:STATE], 2)
    )
    inputs = grads[:, :WIDE]
    own = own.astype(BF16).astype(F32) * after[:, INSIDE] - weighted.astype(F32) * inputs
    sums[:, :128] = head_sums(own)
    sums[:, 128:] = head_sums(wide[:, VALUES] * inputs)


def leave(
    ids, g1, g2, g3, state, inner, grad_mixed, grads, wide, spread, slope, narrow, consts, taken, grad_gain,
    low, state_low, keep, send, small, turned,
):
    me = ids[0, 1]
    end = jnp.zeros((STATE, WIDE), F32)
    gap = jnp.zeros((1, WIDE), F32)
    for ahead, message in enumerate((g1, g2, g3)):
        scale = jnp.exp(gap) * jnp.where(me + ahead < 3, 1.0, 0.0)
        end = end + scale * message[...].astype(F32)
        start = STATE + 8 * (2 - ahead)
        gap = gap + state[start : start + 1]
    step, step_slope = wide[:, STEP], wide[:, STEP_SLOPE]
    values = wide[:, VALUES]
    last = wide[T - 1 :, LOG_DECAY]
    to_end = spread[:, TO_END]
    weighted = narrow[:, WEIGHTED].astype(F32)
    own = grad_mixed[...]
    from_end = dot(narrow[:, BMAT], end) * to_end
    inputs = grads[:, :WIDE] + from_end
    from_b = grads[:, WIDE : WIDE + STATE]
    from_b = from_b + sum(dot_last(weighted * to_end, part) for part in split(end, 2))
    from_c = grads[:, WIDE + STATE :]
    sums = head_sums(values * from_end)
    ended = step * sums
    at_end = jnp.exp(spread_heads(last)) * jnp.sum(end * state[:STATE], axis=0, keepdims=True)
    at_end = head_sums(jnp.broadcast_to(at_end, (8, WIDE)))[0:1]
    at_end = at_end + jnp.sum(ended, axis=0, keepdims=True)
    grad_log = inner[:, :128] - ended
    grad_decay = pick(flag(iota((T, T), 0) <= iota((T, T), 1)), grad_log, 1, 0) + at_end
    rate = jnp.exp(consts[7:8, :128])
    grad_step = inner[:, 128:] + sums - rate * grad_decay
    grad_step_pre = grad_step * step_slope
    grad_values = own * spread_heads(consts[8:9, :128]) + inputs * spread[:, STEPS]
    grad_pre = jnp.concatenate([grad_values, from_b, from_c], axis=1) * slope[...]
    before = taken[...].astype(F32)
    padded = jnp.concatenate([jnp.zeros((RIM, MIX), F32), grad_pre], axis=0)
    grad_input = jnp.zeros((EXT, MIX), F32)
    line = iota((8, MIX), 0)
    taps = jnp.where(line == KERNEL, jnp.sum(grad_pre, axis=0, keepdims=True), 0.0)
    for tap in range(KERNEL):
        later = roll(padded, tap + 1 - KERNEL, 0)
        taps = jnp.where(line == tap, jnp.sum(before * later, axis=0, keepdims=True), taps)
        grad_input = grad_input + consts[tap : tap + 1, :MIX] * later
    low[:, :WIDE] = grad_input[:, :WIDE].astype(BF16)
    state_low[...] = grad_input[:, WIDE:]
    low_step = jnp.concatenate([jnp.zeros((RIM, 128), F32), grad_step_pre], axis=0)
    low[:, WIDE:] = roll(low_step, STEP_LANE, 1).astype(BF16)
    rest = jnp.zeros((TURNED - EXT - 8, 2 * STATE), F32)
    turned[...] = jnp.concatenate([grad_input[:, WIDE:], taps[:, WIDE:], rest], axis=0).T
    turn_out(ids, turned, keep, send)
    heads = (
        jnp.sum(grad_step_pre, axis=0, keepdims=True),
        -rate * jnp.sum(grad_decay * step, axis=0, keepdims=True),
        head_sums(jnp.broadcast_to(jnp.sum(own * values, axis=0, keepdims=True), (8, WIDE)))[0:1],
    )
    none = jnp.zeros((1, 128), F32)
    heads = jnp.concatenate([heads[0] + roll(heads[1], 64, 1), heads[2], none], axis=1)
    line = iota((8, WIDE), 0)
    small[...] = jnp.where(line == 5, grad_gain[...], jnp.where(line == 6, heads, taps[:, :WIDE]))


def pair_sum(ids, keep, got, *shares):
    for ahead, share in enumerate(shares):
        share[...] = (keep[ahead].astype(F32) + got[ahead].astype(F32)).astype(share.dtype)


def value_grads(
    ids, low, state_low, gated_low, weights, gate_out, hidden_in, pair, value, head
):
    value[...] = dot_first(hidden_in[...], low[:, :WIDE]).astype(BF16)
    part = dot_last(low[:, :WIDE], weights[:, :WIDE]) + dot_last(low[:, WIDE:], weights[:, MIX:])
    high, rest = split(state_low[...], 2)
    part = part + dot_last(high, weights[:, WIDE:MIX]) + dot_last(rest, weights[:, WIDE:MIX])
    head[:RIM] = part[:RIM]
    head[RIM:] = part[RIM:] + dot_last(gated_low[:, LOW_GATE], gate_out[:, :WIDE])


def share_out(ids, head, branch, keep, send, whole):
    whole[...] = head[RIM:].astype(BF16)
    chip, core = ids[0, 2] >> 1, ids[0, 2] & 1
    for other in range(4):
        start = (chip ^ other) * 2
        for half, source in enumerate((whole, branch)):
            rows = slice(half * SHARE, half * SHARE + SHARE)
            keep[other, rows] = source[aligned((start + core) * SHARE, SHARE)]
            send[other, rows] = source[aligned((start + 1 - core) * SHARE, SHARE)]


def fold(small):
    pieces = []
    for chunk in range(6):
        piece = small[:, pair_columns(chunk // 2)]
        pieces.append(piece if chunk % 2 else roll(piece, 64, 1))
    folded = jnp.concatenate(pieces, axis=0)
    high = folded.astype(BF16).astype(F32)
    return jnp.concatenate([high, folded - high], axis=0)


def unfold(block):
    folded = block[:48] + block[48:]
    lower = iota((8, 128), 1) < 64
    pairs = []
    for pair in range(3):
        one, two = folded[16 * pair : 16 * pair + 8], folded[16 * pair + 8 : 16 * pair + 16]
        pairs.append(jnp.where(lower, roll(one, 64, 1), two))
    return jnp.concatenate(pairs, axis=1)


def tidy(block):
    folded = block[:48] + block[48:]
    high = folded.astype(BF16).astype(F32)
    parts = jnp.concatenate([high, folded - high], axis=0)
    return jnp.where(iota((ROWS, 128), 1) < 64, block, parts)


def late_grads(
    ids, t0, t1, t2, t3, low, small, head, rim, units, hidden_in, gate, out, value, branch, keep, send, *targets
):
    targets, tail, whole = targets[:-2], targets[-2], targets[-1]
    total = t0[...] + t1[...] + t2[...] + t3[...]
    straight = jnp.concatenate([total, jnp.zeros((128 - PART, TURNED), F32)], axis=0).T
    low_tail = low[:, WIDE:].astype(F32) + straight[:EXT]
    terms = jnp.sum(head[:RIM] * unit_rows(rim[...]), axis=0, keepdims=True)
    terms = terms + jnp.sum(head[RIM:] * units[...], axis=0, keepdims=True)
    grads = dot_first(hidden_in[...], low_tail)
    row = jnp.where(iota((8, D), 0) == 0, terms, 0.0)
    chosen = flag(iota((8, 128), 1) == GAIN_LANE)
    grads = grads + sum(dot_first(part, chosen) for part in split(row, 2))
    tail[...] = grads.astype(BF16)
    own = straight[EXT : EXT + 8]
    row = jnp.concatenate([own[0:1] + roll(own[1:2], 64, 1), own[2:3] + roll(own[3:4], 64, 1), own[4:5]], axis=1)
    folded = fold(jnp.where(iota((8, WIDE), 0) == 7, row, small[...]))
    lanes = iota((ROWS, 128), 1) < 64
    for target, place, block in places(ids, 0, targets[:5]):
        rows = aligned(block * ROWS, ROWS)
        target[place, :, :WIDE] = gate[rows]
        target[place, :, WIDE:] = value[rows]
    for target, place, block in places(ids, 1, targets[5:]):
        rows = aligned(block * ROWS, ROWS)
        target[place, :ROWS, :OUT_RIGHT] = out[rows]
        end = jnp.where(lanes, tail[rows].astype(F32), folded)
        target[place, :ROWS, OUT_RIGHT:] = end.astype(BF16)
    share_out(ids, head, branch, keep, send, whole)
    last = head[:RIM][8:]
    pieces = [last[:, RIGHT * chunk : RIGHT * chunk + RIGHT] for chunk in range(D // RIGHT)]
    pieces.append(jnp.zeros((8, RIGHT), F32))
    for slot in range(2):
        targets[8][slot, ROWS:] = jnp.concatenate(pieces[2 * slot : 2 * slot + 2], axis=0).astype(BF16)


def places(ids, side, targets):
    line, ctx = ids[0, 0], ids[0, 1]
    for far in range(4):
        for near in range(4):
            slot, place = far + far // 3, near
            if far == 2 and near >= 2:
                slot, place = 3, near - 2
            one, two = (near, far) if side else (far, near)
            yield targets[slot], place, ((line + one) & 3) * 4 + ((ctx + two) & 3)


def put(target, total, tailed):
    if tailed:
        target[:, :OUT_RIGHT] = total[:, :OUT_RIGHT].astype(BF16)
        target[:, OUT_RIGHT:] = tidy(total[:, OUT_RIGHT:]).astype(BF16)
    else:
        target[...] = total.astype(BF16)


def pair_halves(ids, keep, got, near, far):
    for other in range(4):
        target = far if other % 2 else near
        total = keep[other].astype(F32) + got[other].astype(F32)
        target[other // 2] = total.astype(BF16)


def relay(side, one, three, first, second, to_one, to_three):
    for near in range(4):
        if near < 2:
            total = one[near].astype(F32) + first[near].astype(F32)
            put(to_one.at[near], total, side)
            to_three[near] = three[near]
        else:
            total = three[near].astype(F32) + second[near - 2, :ROWS].astype(F32)
            put(to_three.at[near], total, side)
            to_one[near] = one[near]


def relay_both(ids, *refs):
    relay(0, *refs[:4], *refs[9:11])
    relay(1, *refs[4:8], *refs[11:13])
    second, behind = refs[7], refs[13]
    inside = jnp.where(ids[0, 1] < 3, 1.0, 0.0)
    for chunk in range(D // RIGHT):
        got = second[chunk // 2, ROWS:].astype(F32) * inside
        start = 8 * (chunk % 2)
        behind[:, RIGHT * chunk : RIGHT * chunk + RIGHT] = got[start : start + 8]


def halfway(side, own, one, three, *targets):
    for near, target in enumerate(targets):
        total = own[near].astype(F32) + one[near].astype(F32) + three[near].astype(F32)
        put(target, total, side)


def halfway_both(ids, l0, l1, l3, r0, r1, r3, own, *targets):
    halfway(0, l0, l1, l3, *targets[:4])
    halfway(1, r0, r1, r3, *targets[4:])


def pair_again(ids, near, got, cotangent, hidden, own, second, held, mine, last):
    for index, target in enumerate((own, second)):
        target[...] = (near[index].astype(F32) + got[index].astype(F32)).astype(BF16)
    held[...] = cotangent[...]
    mine[...] = hidden[aligned(ids[0, 2] * SHARE, SHARE)]
    last[...] = hidden[T - RIM :].astype(F32)[8:]


def collect_left(ids, a0, a1, a2, a3, b0, b1, b2, b3, grad_gate, grad_value, grad_out):
    total = sum(part[...].astype(F32) for part in (a0, a1, a2, a3))
    grad_gate[...] = total[:, :WIDE]
    grad_value[...] = total[:, WIDE:]
    grad_out[...] = sum(part[:, :OUT_RIGHT].astype(F32) for part in (b0, b1, b2, b3))


def hidden_back(grads, rows, gain):
    tokens = rows.astype(F32)
    inv = lax.rsqrt(jnp.mean(tokens * tokens, axis=1, keepdims=True) + EPSILON)
    unit = tokens * inv
    scaled = grads * gain
    return inv * (scaled - unit * jnp.mean(scaled * unit, axis=1, keepdims=True)), tokens


def gather_up(
    ids, b0, b1, b2, b3, p0, p1, mine, weights, behind,
    message, gain_out, grad_step, taps, offset, gain, bias, decay, skip, rest,
):
    both = p0[...].astype(F32) + p1[...].astype(F32)
    row = gain_row(weights[:, MIX:])
    gain_out[...] = jnp.broadcast_to(row, (8, D))
    grads, tokens = hidden_back(both[:SHARE], mine[...], row)
    message[:SHARE] = grads.astype(BF16)
    message[SHARE : 2 * SHARE] = (tokens + both[SHARE:]).astype(BF16)
    total = sum(part[:, OUT_RIGHT:].astype(F32) for part in (b0, b1, b2, b3))
    rest[...] = total
    small = unfold(total)
    state = small[7:8]
    lanes = iota((8, 128), 1)
    for tap in range(KERNEL + 1):
        piece = state[:, pair_columns(tap // 2)]
        piece = piece if tap % 2 == 0 else roll(piece, 64, 1)
        if tap == 0:
            rows = jnp.where(iota((8, 128), 0) == 0, roll(piece, STATE_LANE, 1), 0.0)
        else:
            rows = jnp.where(iota((8, 128), 0) == tap, roll(piece, STATE_LANE, 1), rows)
    rest[:8] = jnp.where(lanes < 64, rest[:8], rows)
    for block in range(ROWS // 16):
        message[2 * SHARE :, pair_columns(block)] = rest[16 * block : 16 * block + 16].astype(BF16)
    for block in range(6):
        pair = [behind[:, pair_columns(2 * block + i)] for i in range(2)]
        message[2 * SHARE :, pair_columns(6 + block)] = jnp.concatenate(pair, axis=0).astype(BF16)
    picked = flag(iota((8, 128), 1) == STEP_LANE + iota((8, 128), 0))
    grad_step[...] = pick(picked, total, 1, 1, 3)[:HEADS]
    taps[...] = small[:KERNEL]
    offset[...] = small[KERNEL : KERNEL + 1]
    gain[...] = small[5:6]
    bias[...] = small[6:7, :HEADS]
    decay[...] = small[6:7, 64 : 64 + HEADS]
    skip[...] = small[6:7, 128 : 128 + HEADS]


def finish(ids, *refs):
    pieces, row, cotangent, last = refs[:8], refs[8], refs[9], refs[10]
    grad_hidden, block_out, grad_state, grad_gain, taps, offset, rest, rims = refs[11:]
    chip, core = ids[0, 2] >> 1, ids[0, 2] & 1
    order = []
    for far in range(4):
        start = ((chip - far) & 3) * 2
        order += [(start + core, pieces[far]), (start + 1 - core, pieces[4 + far])]
    for place, piece in order:
        block_out[aligned(place * SHARE, SHARE)] = piece[SHARE : 2 * SHARE]
        for block in range(6):
            part = piece[2 * SHARE :, pair_columns(block)]
            rest[place, 16 * block : 16 * block + 16] = part.astype(F32)
            part = piece[2 * SHARE :, pair_columns(6 + block)].astype(F32)
            rims[place, :, pair_columns(2 * block)] = part[:8]
            rims[place, :, pair_columns(2 * block + 1)] = part[8:]
    total, behind = rest[0], rims[0]
    for i in range(1, 8):
        total = total + rest[i]
        behind = behind + rims[i]
    for place, piece in order:
        rows = aligned(place * SHARE, SHARE)
        grad_hidden[rows] = cotangent[rows].astype(F32) + piece[:SHARE].astype(F32)
    grads, _ = hidden_back(behind, last[...], row[0:1])
    grad_hidden[T - 8 :] = grad_hidden[T - 8 :] + grads
    lanes = iota((ROWS, 128), 1) >> 5
    for half in range(2):
        state = jnp.zeros((ROWS, 128), F32)
        small = jnp.zeros((8, 128), F32)
        for i in range(4):
            one = rest[4 * half + i]
            state = jnp.where(lanes == i, roll(one, PART * i, 1), state)
            small = jnp.where(lanes[:8] == i, roll(one[:8], PART * i - STATE_LANE, 1), small)
        columns = pair_columns(half)
        grad_state[:, columns] = state
        taps[:, columns] = small[:KERNEL]
        offset[:, columns] = small[KERNEL : KERNEL + 1]
    grad_gain[...] = pick(flag(iota((8, 128), 1) == GAIN_LANE), total, 1, 1, 3)[0:1]


def stack_blocks(ids, l0, l1, l2, l3, r0, r1, r2, r3, left, right, rim):
    for i, (one, two) in enumerate(((l0, r0), (l1, r1), (l2, r2), (l3, r3))):
        left[i] = one[:ROWS]
        right[i] = two[...]
    inside = jnp.where(ids[0, 1] > 0, 1.0, 0.0)
    got = l1[ROWS:].astype(F32) * inside
    none = jnp.zeros((8, PAIR), F32)
    rim[:, :PAIR] = jnp.concatenate([none, got[:8]], axis=0).astype(BF16)
    rim[:, PAIR:] = jnp.concatenate([none, got[8:]], axis=0).astype(BF16)


def shift(array, axis, steps):
    return lax.ppermute(array, axis, [(i, (i + steps) % 4) for i in range(4)])


def from_chip(array, steps):
    return lax.ppermute(array, "tp", [(i, (i + 2 * steps) % 8) for i in range(8)])


def across(array, bits):
    return lax.ppermute(array, "tp", [(i, i ^ bits) for i in range(8)])


def around(array, axis):
    return [array] + [shift(array, axis, steps) for steps in range(1, 4)]


def ring_sides(array, axis):
    return shift(array, axis, 1), shift(array, axis, 3)


def ring_rest(array, axis, one, three):
    return [array, one, shift(one[:2], axis, 1), shift(three[2:], axis, 3), three]


def chips_all(array):
    same = [array] + [from_chip(array, steps) for steps in range(1, 4)]
    return same + [across(one, 1) for one in same]


def per_device(
    hidden_states,
    norm_gain,
    gate_weight,
    value_weight,
    state_proj,
    step_proj,
    value_filter,
    value_offset,
    state_filter,
    state_offset,
    step_bias,
    decay_log,
    skip_gain,
    gate_norm_gain,
    out_weight,
    out_grad,
):
    hidden = hidden_states[0]
    cotangent = out_grad[0]
    places = [lax.axis_index(axis).astype(jnp.int32) for axis in ("dp", "ctx", "tp")]
    ids = jnp.stack(places).reshape(1, 3)

    left, longer, right = fuse(
        prepare,
        [((ROWS, PAIR), BF16), ((ROWS + RIM, PAIR), BF16), ((ROWS, PAIR), BF16)],
        ids,
        value_weight,
        gate_weight,
        state_proj,
        step_proj.T,
        norm_gain[None],
        out_weight.T,
        hidden,
        fetch=7,
        rim=True,
    )
    near = [left, shift(longer, "ctx", 1), shift(left, "ctx", 2), shift(left, "ctx", 3)]
    left, right, rim = fuse(
        stack_blocks,
        [((4, ROWS, PAIR), BF16)] * 2 + [((RIM, D), BF16)],
        ids,
        *near,
        *around(right, "dp"),
    )
    consts, units = fuse(
        tabulate,
        [((16, FIRST), F32), ((T, D), F32)],
        ids,
        value_filter,
        state_filter,
        value_offset[None],
        state_offset[None],
        gate_norm_gain[None],
        jnp.stack([step_bias, decay_log, skip_gain]),
        hidden,
        fetch=7,
    )
    left = ring_rest(left, "dp", *ring_sides(left, "dp"))
    right = ring_rest(right, "ctx", *ring_sides(right, "ctx"))
    weights, hidden_in, taken, wide, narrow, message = fuse(
        enter,
        [
            ((D, FIRST), BF16),
            ((EXT, D), BF16),
            ((EXT, MIX), BF16),
            ((T, LOG_DECAY.stop), F32),
            ((T, WEIGHTED.stop), BF16),
            ((STATE + 16, WIDE), BF16),
        ],
        ids,
        *left,
        *right,
        rim,
        units,
        consts,
    )
    messages = around(message, "ctx")[1:]
    gate_out, before, slope, spread = fuse(
        project,
        [((D, 2 * WIDE), BF16), ((T, SKIPPED.stop), F32), ((T, MIX), F32), ((T, STEPS.stop), F32)],
        ids,
        *left,
        *right,
        hidden_in,
        cotangent,
        wide,
        narrow,
        consts,
    )
    state, after, sums = fuse(
        mix,
        [((STATE + 24, WIDE), F32), ((T, MIXED.stop), F32), ((8, T), F32)],
        ids,
        *messages,
        spread,
        narrow,
        before,
    )
    (ready,) = fuse(gate_ready, [((5, T, WIDE), F32)], ids, after, before, consts)
    sums = sums + across(sums, 1)
    gated_low, grad_mixed, grad_gain, sensitivity = fuse(
        gate_back,
        [
            ((T, LOW_GATE.stop), BF16),
            ((T, WIDE), F32),
            ((8, WIDE), F32),
            ((STATE, WIDE), BF16),
        ],
        ids,
        sums,
        *[from_chip(sums, steps) for steps in range(1, 4)],
        ready,
        before,
        spread,
        narrow,
    )
    later = [shift(sensitivity, "ctx", -steps) for steps in range(1, 4)]
    square = ((D, WIDE), BF16)
    gate, out, grads, branch, inner = fuse(
        middle,
        [square, square, ((T, MIX), F32), ((T, D), BF16), ((T, 256), F32)],
        ids,
        hidden_in,
        gated_low,
        cotangent,
        gate_out,
        wide,
        narrow,
        grad_mixed,
        state,
        spread,
        after,
    )
    low, state_low, keep, send, small = fuse(
        leave,
        [((EXT, WIDE + 128), BF16), ((EXT, 2 * STATE), F32)] + [((4, PART, TURNED), F32)] * 2 + [((8, WIDE), F32)],
        ids,
        *later,
        state,
        inner,
        grad_mixed,
        grads,
        wide,
        spread,
        slope,
        narrow,
        consts,
        taken,
        grad_gain,
        scratch=[((2 * STATE, TURNED), F32)],
    )
    pair = fuse(pair_sum, [((PART, TURNED), F32)] * 4, ids, keep, across(send, 1))
    turned = pair[:1] + [from_chip(pair[steps], steps) for steps in range(1, 4)]
    value, head = fuse(
        value_grads,
        [square, ((EXT, D), F32)],
        ids,
        low,
        state_low,
        gated_low,
        weights,
        gate_out,
        hidden_in,
        pair[0],
    )
    both = ((2 * SHARE, D), BF16)
    two = ((2, 2 * SHARE, D), BF16)

    def stage(count, rows, columns):
        return (count, rows, columns), BF16

    def stages(columns, rows):
        whole = stage(4, ROWS, columns)
        return [whole, whole, stage(2, ROWS, columns), stage(2, rows, columns), whole]

    keep, send, *blocks = fuse(
        late_grads,
        [((4, 2 * SHARE, D), BF16)] * 2 + stages(LEFT, ROWS) + stages(RIGHT, ROWS + RIM),
        ids,
        *turned,
        low,
        small,
        head,
        rim,
        units,
        hidden_in,
        gate,
        out,
        value,
        branch,
        scratch=[((D, 128), BF16), ((T, D), BF16)],
    )
    left, right = blocks[:5], blocks[5:]
    near, far = fuse(pair_halves, [two] * 2, ids, keep, across(send, 1))
    *sides, behind = fuse(
        relay_both,
        [stage(4, ROWS, LEFT)] * 2 + [stage(4, ROWS, RIGHT)] * 2 + [((8, D), F32)],
        ids,
        *(left[1], left[4], shift(left[2], "dp", 1), shift(left[3], "dp", 3)),
        *(right[1], right[4], shift(right[2], "ctx", 1), shift(right[3], "ctx", 3)),
        near,
    )
    left = [left[0], shift(sides[0], "dp", 1), shift(sides[1], "dp", 3)]
    right = [right[0], shift(sides[2], "ctx", 1), shift(sides[3], "ctx", 3)]
    own, second, held, mine, last = fuse(
        pair_again,
        [both, both, ((T, D), BF16), ((SHARE, D), BF16), ((8, D), F32)],
        ids,
        near,
        across(far, 2),
        cotangent,
        hidden,
    )
    sums = fuse(
        halfway_both,
        [((ROWS, LEFT), BF16)] * 4 + [((ROWS, RIGHT), BF16)] * 4,
        ids,
        *left,
        *right,
        own,
    )
    left = sums[:1] + [shift(sums[steps], "ctx", steps) for steps in range(1, 4)]
    right = sums[4:5] + [shift(sums[4 + steps], "dp", steps) for steps in range(1, 4)]
    few, line = ((1, HEADS), F32), ((1, WIDE), F32)
    message, gain_full, *few_grads = fuse(
        gather_up,
        [((2 * SHARE + 16, D), BF16), ((8, D), F32), ((HEADS, ROWS), F32), ((KERNEL, WIDE), F32)]
        + [line, line, few, few, few],
        ids,
        *right,
        own,
        across(second, 4),
        mine,
        weights,
        behind,
        scratch=[((ROWS, 128), F32)],
    )
    grad_step, taps, offset, gain, bias, decay, skip = few_grads
    grad_gate, grad_value, grad_out = fuse(
        collect_left, [((ROWS, WIDE), F32)] * 3, ids, *left, *right
    )
    grad_hidden, block_out, grad_state, grad_norm_gain, state_taps, state_offset = fuse(
        finish,
        [
            ((T, D), F32),
            ((T, D), BF16),
            ((ROWS, 2 * STATE), F32),
            ((1, ROWS), F32),
            ((KERNEL, 2 * STATE), F32),
            ((1, 2 * STATE), F32),
        ],
        ids,
        *chips_all(message),
        gain_full,
        held,
        last,
        scratch=[((8, ROWS, 128), F32), ((8, 8, D), F32)],
    )
    return (
        block_out[None],
        grad_hidden[None],
        grad_norm_gain[0],
        grad_gate,
        grad_value,
        grad_state,
        grad_step.T,
        taps,
        offset[0],
        state_taps,
        state_offset[0],
        bias[0],
        decay[0],
        skip[0],
        gain[0],
        grad_out.T,
    )


def solution(mesh):
    line = P(("dp", "ctx"))
    placed = (
        P("dp", "ctx", None),
        line,
        P(("dp", "ctx"), "tp"),
        P(("dp", "ctx"), "tp"),
        P(("dp", "ctx"), None),
        P(("dp", "ctx"), "tp"),
        P(None, "tp"),
        P("tp"),
        P(),
        P(),
        P("tp"),
        P("tp"),
        P("tp"),
        P("tp"),
        P("tp", ("dp", "ctx")),
        P("dp", "ctx", None),
    )
    given = (
        P("dp", "ctx", None),
        P("dp", "ctx", None),
        line,
        P(("dp", "ctx"), "tp"),
        P(("dp", "ctx"), "tp"),
        P(("dp", "ctx"), None),
        P(("dp", "ctx"), "tp"),
        P(None, "tp"),
        P("tp"),
        P(),
        P(),
        P("tp"),
        P("tp"),
        P("tp"),
        P("tp"),
        P("tp", ("dp", "ctx")),
    )
    return jax.shard_map(
        per_device, mesh=mesh, in_specs=placed, out_specs=given, check_vma=False
    )
```

```python
import jax
import jax.numpy as jnp
from jax import lax
from jax.experimental import pallas as pl
from jax.experimental.pallas import tpu as pltpu
from jax.sharding import PartitionSpec as P

F32 = jnp.float32
BF16 = jnp.bfloat16
EPSILON = 1e-05
INNER = 3072
D = 1536
T = 256
RIM = 16
EXT = T + RIM
KERNEL = 4
HEADS = 6
WIDE = 384
STATE = 128
MIX = WIDE + 2 * STATE
FIRST = MIX + 128
ROWS = 96
SHARES = 16
PAIR = 2 * WIDE
RIGHT = 512
OUT_RIGHT = RIGHT - 128
LEFT = 3 * WIDE - OUT_RIGHT
SHARE = T // 8
PART = 32
STEP_LANE = 32
GAIN_LANE = STEP_LANE + HEADS
STATE_LANE = 64
TURNED = 384
VMEM_LIMIT = 8 * 2**20

VALUES, SLOPE = slice(0, WIDE), slice(WIDE, WIDE + MIX)
STEP, STEP_SLOPE, LOG_DECAY = slice(1024, 1152), slice(1152, 1280), slice(1280, 1408)
BMAT, CMAT, WEIGHTED = slice(0, 128), slice(128, 256), slice(256, 640)
GATE, GRAD_NORMED, WITHIN = slice(0, 384), slice(384, 768), slice(768, 1152)
GATE_SLOPE, SCALED, SKIPPED = slice(1152, 1536), slice(1536, 1920), slice(1920, 2304)
INSIDE, MIXED = slice(0, 384), slice(384, 768)
NORMED, LOW_GATE = slice(0, 384), slice(384, 768)
GROWN, TO_END, STEPS = slice(0, 384), slice(384, 768), slice(768, 1152)


WORK = {"pair_again": 2 * 10**9, "collect_left": 5 * 10**9}


def fuse(function, outputs, ids, *arrays, scratch=(), fetch=0, rim=False):
    count = len(arrays)
    plain = count - fetch
    shapes = [array.shape for array in arrays]
    if rim:
        shapes[-1] = (RIM, D)

    def body(*refs):
        if not fetch:
            function(*refs)
            return
        given = list(refs[1 + plain : 1 + count])
        held, done = refs[-1 - fetch : -1], refs[-1]
        if rim:
            given[-1] = given[-1].at[pl.ds(T - RIM, RIM)]
        copies = [
            pltpu.make_async_copy(source, target, done.at[i])
            for i, (source, target) in enumerate(zip(given, held))
        ]
        for copy in copies:
            copy.start()

        def ready():
            for copy in copies:
                copy.wait()

        function(*refs[: 1 + plain], *held, *refs[1 + count : -1 - fetch], ready=ready)

    buffers = [pltpu.VMEM(shape, dtype) for shape, dtype in scratch]
    spaces = [pltpu.SMEM] + [pltpu.VMEM] * plain + [pltpu.HBM] * fetch
    if fetch:
        buffers += [pltpu.VMEM(shapes[i], arrays[i].dtype) for i in range(plain, count)]
        buffers += [pltpu.SemaphoreType.DMA((fetch,))]
        held = [pltpu.with_memory_space_constraint(array, pltpu.HBM) for array in arrays[plain:]]
        arrays = (*arrays[:plain], *held)
    cost = None
    if function.__name__ in WORK:
        cost = pl.CostEstimate(
            flops=WORK[function.__name__], bytes_accessed=10**6, transcendentals=1
        )
    call = pl.pallas_call(
        body,
        out_shape=[jax.ShapeDtypeStruct(shape, dtype) for shape, dtype in outputs],
        in_specs=[pl.BlockSpec(memory_space=space) for space in spaces],
        out_specs=[pl.BlockSpec(memory_space=pltpu.VMEM) for _ in outputs],
        scratch_shapes=buffers,
        compiler_params=pltpu.CompilerParams(vmem_limit_bytes=VMEM_LIMIT),
        cost_estimate=cost,
        name=function.__name__,
    )
    return list(call(ids, *arrays))


def roll(array, shift, axis):
    return pltpu.roll(array, shift % array.shape[axis], axis)


def product(a, b, left, right):
    return lax.dot_general(
        a.astype(BF16),
        b.astype(BF16),
        (((left,), (right,)), ((), ())),
        preferred_element_type=F32,
    )


def dot(a, b):
    return product(a, b, 1, 0)


def dot_last(a, b):
    return product(a, b, 1, 1)


def dot_first(a, b):
    return product(a, b, 0, 0)


def split(array, count):
    parts = []
    for _ in range(count):
        part = array.astype(BF16)
        parts.append(part)
        array = array - part.astype(F32)
    return parts


def twice(a, b, left, right):
    return sum(product(part, b, left, right) for part in split(a, 2))


def pick(chosen, array, left, right, parts=2):
    return sum(product(chosen, part, left, right) for part in split(array, parts))


def iota(shape, axis):
    return lax.broadcasted_iota(jnp.int32, shape, axis)


def flag(condition):
    return jnp.where(condition, 1.0, 0.0)


def silu_parts(array):
    sig = jax.nn.sigmoid(array)
    return array * sig, sig * (1.0 + array * (1.0 - sig))


def spread_heads(array):
    rows = array.shape[0]
    lower = iota((rows, 128), 1) < 64
    pieces = [
        jnp.where(lower, array[:, h : h + 1], array[:, h + 1 : h + 2]) for h in range(0, HEADS, 2)
    ]
    return jnp.concatenate(pieces, axis=1)


def head_sums(array):
    chosen = flag((iota((128, WIDE), 1) >> 6) == iota((128, WIDE), 0))
    return sum(dot_last(part, chosen) for part in split(array, 2))


def gain_row(tail):
    return dot_last(flag(iota((8, 128), 1) == GAIN_LANE), tail)[0:1]


def unit_rows(rows):
    tokens = rows.astype(F32)
    inv = lax.rsqrt(jnp.mean(tokens * tokens, axis=1, keepdims=True) + EPSILON)
    return tokens * inv


def aligned(start, size):
    return pl.ds(pl.multiple_of(start, size), size)


def prepare(
    ids, value_weight, gate_weight, state_proj, step_proj, norm_gain, out_weight, rim, left, longer, right, ready
):
    ready()
    for target in (left, longer):
        target[:ROWS, :WIDE] = value_weight[...]
        target[:ROWS, WIDE:] = gate_weight[...]
    last = rim[...].astype(F32)[8:]
    longer[ROWS:] = jnp.concatenate([last[:, :PAIR], last[:, PAIR:]], axis=0).astype(BF16)
    right[:, : 2 * STATE] = state_proj[...]
    place = iota((HEADS, 128), 1) == STEP_LANE + iota((HEADS, 128), 0)
    tail = dot_first(step_proj[...], flag(place))
    tail = tail + dot_first(norm_gain[...], flag(iota((1, 128), 1) == GAIN_LANE))
    right[:, 2 * STATE : WIDE] = tail.astype(BF16)
    right[:, WIDE:] = out_weight[...]


def tabulate(
    ids, value_filter, state_filter, value_offset, state_offset, gate_gain, heads, hidden, consts, units, ready
):
    ready()
    units[...] = unit_rows(hidden[...])
    consts[...] = jnp.zeros(consts.shape, F32)
    consts[:KERNEL, :WIDE] = value_filter[...].astype(F32)
    consts[:KERNEL, WIDE:MIX] = state_filter[...].astype(F32)
    consts[KERNEL : KERNEL + 1, :WIDE] = value_offset[...].astype(F32)
    consts[KERNEL : KERNEL + 1, WIDE:MIX] = state_offset[...].astype(F32)
    consts[5:6, :WIDE] = gate_gain[...].astype(F32)
    consts[6:9, :HEADS] = heads[...]


def place_blocks(ids, left, right, *moves):
    line, ctx = ids[0, 0], ids[0, 1]

    def piece(side, far, near):
        if far == 2:
            return (side[2], near) if near < 2 else (side[3], near - 2)
        return side[far + far // 3], near

    for far in range(4):
        for near in range(4):
            for target, side, start, source, size in moves:
                if side == 0:
                    block = ((line - far) & 3) * 4 + ((ctx - near) & 3)
                else:
                    block = ((line - near) & 3) * 4 + ((ctx - far) & 3)
                array, place = piece((left, right)[side], far, near)
                target[aligned(block * ROWS, ROWS), start : start + size] = array[
                    place, :, source : source + size
                ]


def enter(
    ids, l0, l1, l2, l3, l4, r0, r1, r2, r3, r4, rim, units, consts,
    weights, hidden_in, taken, wide, narrow, message,
):
    moves = (weights, 0, 0, 0, WIDE), (weights, 1, WIDE, 0, WIDE)
    place_blocks(ids, (l0, l1, l2, l3, l4), (r0, r1, r2, r3, r4), *moves)
    gain = gain_row(weights[:, MIX:])
    hidden_in[:RIM] = (unit_rows(rim[...]) * gain).astype(BF16)
    hidden_in[RIM:] = (units[...] * gain).astype(BF16)
    projected = dot(hidden_in[...], weights[...])
    inputs = projected[:, :MIX].astype(BF16)
    taken[...] = inputs
    inputs = inputs.astype(F32)
    filter_pre = consts[KERNEL : KERNEL + 1, :MIX]
    for tap in range(KERNEL):
        filter_pre = filter_pre + consts[tap : tap + 1, :MIX] * roll(inputs, KERNEL - 1 - tap, 0)[RIM:]
    wide[:, SLOPE] = filter_pre
    activated = filter_pre * jax.nn.sigmoid(filter_pre)
    lanes = iota((T, 128), 1) < HEADS
    step_in = roll(projected[RIM:, MIX:], 128 - STEP_LANE, 1) + consts[6:7, :128]
    step_in = jnp.where(lanes, step_in, -100.0)
    step = jnp.maximum(step_in, 0.0) + jnp.log1p(jnp.exp(-jnp.abs(step_in)))
    step = jnp.where(lanes, step, 0.0)
    rate = jnp.exp(consts[7:8, :128])
    log_decay = pick(flag(iota((T, T), 0) >= iota((T, T), 1)), -step * rate, 1, 0, 3)
    values = activated[:, :WIDE]
    weighted = (values * spread_heads(step)).astype(BF16)
    wide[:, VALUES] = values
    wide[:, STEP] = step
    wide[:, STEP_SLOPE] = jax.nn.sigmoid(step_in)
    wide[:, LOG_DECAY] = log_decay
    narrow[:, BMAT] = activated[:, WIDE : WIDE + STATE].astype(BF16)
    narrow[:, CMAT] = activated[:, WIDE + STATE :].astype(BF16)
    narrow[:, WEIGHTED] = weighted
    last = log_decay[T - 1 :]
    to_end = spread_heads(jnp.exp(last - log_decay))
    message[:STATE] = dot_first(narrow[:, BMAT], weighted.astype(F32) * to_end).astype(BF16)
    span = spread_heads(last)
    high = span.astype(BF16).astype(F32)
    line = iota((16, WIDE), 0)
    tail = jnp.where(line == 0, high, jnp.where(line == 1, span - high, 0.0))
    message[STATE:] = tail.astype(BF16)


def decays(log_decay, turned, head):
    gap = log_decay[:, head : head + 1] - turned[head : head + 1, :]
    return jnp.exp(jnp.where(iota((T, T), 0) >= iota((T, T), 1), gap, -1e30))


def pair_columns(pair):
    return slice(128 * pair, 128 * pair + 128)


def project(
    ids, l0, l1, l2, l3, l4, r0, r1, r2, r3, r4, hidden_in, cotangent, wide, narrow, consts,
    gate_out, before, slope, spread,
):
    moves = (gate_out, 0, 0, WIDE, WIDE), (gate_out, 1, WIDE, WIDE, WIDE)
    place_blocks(ids, (l0, l1, l2, l3, l4), (r0, r1, r2, r3, r4), *moves)
    _, slope[...] = silu_parts(wide[:, SLOPE])
    last = wide[T - 1 :, LOG_DECAY]
    spread[:, GROWN] = spread_heads(jnp.exp(wide[:, LOG_DECAY]))
    spread[:, TO_END] = spread_heads(jnp.exp(last - wide[:, LOG_DECAY]))
    spread[:, STEPS] = spread_heads(wide[:, STEP])
    act, gate_slope = silu_parts(dot(hidden_in[RIM:], gate_out[:, :WIDE]))
    grads = dot(cotangent[...], gate_out[:, WIDE:])
    before[:, GATE] = act
    before[:, GATE_SLOPE] = gate_slope
    before[:, GRAD_NORMED] = grads
    before[:, SCALED] = grads * consts[5:6, :WIDE] * act
    before[:, SKIPPED] = wide[:, VALUES] * spread_heads(consts[8:9, :128])
    scores = dot_last(narrow[:, CMAT], narrow[:, BMAT])
    log_decay = wide[:, LOG_DECAY]
    turned = log_decay.T
    lower = iota((T, 128), 1) < 64
    weighted = narrow[:, WEIGHTED]
    for pair in range(HEADS // 2):
        part = weighted[:, pair_columns(pair)]
        one = dot(scores * decays(log_decay, turned, 2 * pair), part)
        two = dot(scores * decays(log_decay, turned, 2 * pair + 1), part)
        start = WITHIN.start + 128 * pair
        before[:, start : start + 128] = jnp.where(lower, one, two)


def mix(ids, m1, m2, m3, spread, narrow, before, state, after, sums):
    me = ids[0, 1]
    total = jnp.zeros((STATE, WIDE), F32)
    gap = jnp.zeros((1, WIDE), F32)
    for back, message in enumerate((m1, m2, m3)):
        tail = message[STATE:].astype(F32)
        log = tail[0:1] + tail[1:2]
        state[STATE + 8 * back : STATE + 8 * back + 8] = jnp.broadcast_to(log, (8, WIDE))
        scale = jnp.exp(gap) * jnp.where(me > back, 1.0, 0.0)
        total = total + scale * message[:STATE].astype(F32)
        gap = gap + log
    state[:STATE] = total
    inside = before[:, WITHIN] + dot(narrow[:, CMAT], total) * spread[:, GROWN]
    after[:, INSIDE] = inside
    whole = inside + before[:, SKIPPED]
    after[:, MIXED] = whole
    gated = whole * before[:, GATE]
    ones = jnp.ones((8, WIDE), F32)
    squares = pick(ones, gated * gated, 1, 1)
    crosses = pick(ones, before[:, SCALED] * whole, 1, 1)
    sums[...] = jnp.where(iota((8, T), 0) < 4, squares, crosses)


def gate_ready(ids, after, before, consts, ready):
    mixed, act = after[:, MIXED], before[:, GATE]
    gated, rest = mixed * act, mixed * before[:, GATE_SLOPE]
    ready[0] = gated * act
    ready[1] = before[:, GRAD_NORMED] * consts[5:6, :WIDE] * rest
    ready[2] = gated * rest
    ready[3] = gated * consts[5:6, :WIDE]
    ready[4] = before[:, GRAD_NORMED] * gated


def gate_back(ids, s0, s1, s2, s3, ready, before, spread, narrow, gated_low, grad_mixed, grad_gain, sensitivity):
    total = s0[...] + s1[...] + s2[...] + s3[...]
    chosen = flag(iota((8, 128), 0) == 4 * iota((8, 128), 1))
    columns = sum(dot_first(part, chosen) for part in split(total, 3))
    inv = lax.rsqrt(columns[:, 0:1] / INNER + EPSILON)
    back = inv * (inv * inv * columns[:, 1:2] / INNER)
    own = inv * before[:, SCALED] - back * ready[0]
    grad_mixed[...] = own
    sensitivity[...] = dot_first(narrow[:, CMAT], own * spread[:, GROWN]).astype(BF16)
    gated_low[:, LOW_GATE] = (inv * ready[1] - back * ready[2]).astype(BF16)
    gated_low[:, NORMED] = (inv * ready[3]).astype(BF16)
    grad_gain[...] = jnp.broadcast_to(jnp.sum(inv * ready[4], axis=0, keepdims=True), (8, WIDE))


def turn_out(ids, source, keep, send):
    chip, core = ids[0, 2] >> 1, ids[0, 2] & 1
    for ahead in range(4):
        start = ((chip + ahead) & 3) * 2
        keep[ahead] = source[aligned((start + core) * SHARE, SHARE)]
        send[ahead] = source[aligned((start + 1 - core) * SHARE, SHARE)]


def middle(
    ids, hidden_in, gated_low, cotangent, gate_out, wide, narrow, grad_mixed, state, spread, after,
    gate, out, grads, branch, sums,
):
    gate[...] = dot_first(hidden_in[RIM:], gated_low[:, LOW_GATE]).astype(BF16)
    out[...] = dot_first(cotangent[...], gated_low[:, NORMED]).astype(BF16)
    branch[...] = dot_last(gated_low[:, NORMED], gate_out[:, WIDE:]).astype(BF16)
    bmat, cmat, weighted = narrow[:, BMAT], narrow[:, CMAT], narrow[:, WEIGHTED]
    scores = dot_last(cmat, bmat)
    log_decay = wide[:, LOG_DECAY]
    turned = log_decay.T
    lower = iota((T, 128), 1) < 64
    grad_scores = jnp.zeros((T, T), F32)
    for pair in range(HEADS // 2):
        part = weighted[:, pair_columns(pair)]
        grad = grad_mixed[:, pair_columns(pair)]
        got = []
        for side in range(2):
            weights = decays(log_decay, turned, 2 * pair + side)
            got.append(dot_first(scores * weights, grad))
            own = jnp.where(lower, grad, 0.0) if side == 0 else jnp.where(lower, 0.0, grad)
            grad_scores = grad_scores + twice(own, part, 1, 1) * weights
        grads[:, pair_columns(pair)] = jnp.where(lower, got[0], got[1])
    grads[:, WIDE : WIDE + STATE] = twice(grad_scores, cmat, 0, 0)
    own = grad_mixed[...]
    from_state = own * spread[:, GROWN]
    grads[:, WIDE + STATE :] = twice(grad_scores, bmat, 1, 0) + sum(
        dot_last(from_state, part) for part in split(state[:STATE], 2)
    )
    inputs = grads[:, :WIDE]
    own = own.astype(BF16).astype(F32) * after[:, INSIDE] - weighted.astype(F32) * inputs
    sums[:, :128] = head_sums(own)
    sums[:, 128:] = head_sums(wide[:, VALUES] * inputs)


def leave(
    ids, g1, g2, g3, state, inner, grad_mixed, grads, wide, spread, slope, narrow, consts, taken, grad_gain,
    low, state_low, keep, send, small, turned,
):
    me = ids[0, 1]
    end = jnp.zeros((STATE, WIDE), F32)
    gap = jnp.zeros((1, WIDE), F32)
    for ahead, message in enumerate((g1, g2, g3)):
        scale = jnp.exp(gap) * jnp.where(me + ahead < 3, 1.0, 0.0)
        end = end + scale * message[...].astype(F32)
        start = STATE + 8 * (2 - ahead)
        gap = gap + state[start : start + 1]
    step, step_slope = wide[:, STEP], wide[:, STEP_SLOPE]
    values = wide[:, VALUES]
    last = wide[T - 1 :, LOG_DECAY]
    to_end = spread[:, TO_END]
    weighted = narrow[:, WEIGHTED].astype(F32)
    own = grad_mixed[...]
    from_end = dot(narrow[:, BMAT], end) * to_end
    inputs = grads[:, :WIDE] + from_end
    from_b = grads[:, WIDE : WIDE + STATE]
    from_b = from_b + sum(dot_last(weighted * to_end, part) for part in split(end, 2))
    from_c = grads[:, WIDE + STATE :]
    sums = head_sums(values * from_end)
    ended = step * sums
    at_end = jnp.exp(spread_heads(last)) * jnp.sum(end * state[:STATE], axis=0, keepdims=True)
    at_end = head_sums(jnp.broadcast_to(at_end, (8, WIDE)))[0:1]
    at_end = at_end + jnp.sum(ended, axis=0, keepdims=True)
    grad_log = inner[:, :128] - ended
    grad_decay = pick(flag(iota((T, T), 0) <= iota((T, T), 1)), grad_log, 1, 0) + at_end
    rate = jnp.exp(consts[7:8, :128])
    grad_step = inner[:, 128:] + sums - rate * grad_decay
    grad_step_pre = grad_step * step_slope
    grad_values = own * spread_heads(consts[8:9, :128]) + inputs * spread[:, STEPS]
    grad_pre = jnp.concatenate([grad_values, from_b, from_c], axis=1) * slope[...]
    before = taken[...].astype(F32)
    padded = jnp.concatenate([jnp.zeros((RIM, MIX), F32), grad_pre], axis=0)
    grad_input = jnp.zeros((EXT, MIX), F32)
    line = iota((8, MIX), 0)
    taps = jnp.where(line == KERNEL, jnp.sum(grad_pre, axis=0, keepdims=True), 0.0)
    for tap in range(KERNEL):
        later = roll(padded, tap + 1 - KERNEL, 0)
        taps = jnp.where(line == tap, jnp.sum(before * later, axis=0, keepdims=True), taps)
        grad_input = grad_input + consts[tap : tap + 1, :MIX] * later
    low[:, :WIDE] = grad_input[:, :WIDE].astype(BF16)
    state_low[...] = grad_input[:, WIDE:]
    low_step = jnp.concatenate([jnp.zeros((RIM, 128), F32), grad_step_pre], axis=0)
    low[:, WIDE:] = roll(low_step, STEP_LANE, 1).astype(BF16)
    rest = jnp.zeros((TURNED - EXT - 8, 2 * STATE), F32)
    turned[...] = jnp.concatenate([grad_input[:, WIDE:], taps[:, WIDE:], rest], axis=0).T
    turn_out(ids, turned, keep, send)
    heads = (
        jnp.sum(grad_step_pre, axis=0, keepdims=True),
        -rate * jnp.sum(grad_decay * step, axis=0, keepdims=True),
        head_sums(jnp.broadcast_to(jnp.sum(own * values, axis=0, keepdims=True), (8, WIDE)))[0:1],
    )
    none = jnp.zeros((1, 128), F32)
    heads = jnp.concatenate([heads[0] + roll(heads[1], 64, 1), heads[2], none], axis=1)
    line = iota((8, WIDE), 0)
    small[...] = jnp.where(line == 5, grad_gain[...], jnp.where(line == 6, heads, taps[:, :WIDE]))


def pair_sum(ids, keep, got, *shares):
    for ahead, share in enumerate(shares):
        share[...] = (keep[ahead].astype(F32) + got[ahead].astype(F32)).astype(share.dtype)


def value_grads(
    ids, low, state_low, gated_low, weights, gate_out, hidden_in, pair, value, head
):
    value[...] = dot_first(hidden_in[...], low[:, :WIDE]).astype(BF16)
    part = dot_last(low[:, :WIDE], weights[:, :WIDE]) + dot_last(low[:, WIDE:], weights[:, MIX:])
    high, rest = split(state_low[...], 2)
    part = part + dot_last(high, weights[:, WIDE:MIX]) + dot_last(rest, weights[:, WIDE:MIX])
    head[:RIM] = part[:RIM]
    head[RIM:] = part[RIM:] + dot_last(gated_low[:, LOW_GATE], gate_out[:, :WIDE])


def share_out(ids, head, branch, keep, send, whole):
    whole[...] = head[RIM:].astype(BF16)
    chip, core = ids[0, 2] >> 1, ids[0, 2] & 1
    for other in range(4):
        start = (chip ^ other) * 2
        for half, source in enumerate((whole, branch)):
            rows = slice(half * SHARE, half * SHARE + SHARE)
            keep[other, rows] = source[aligned((start + core) * SHARE, SHARE)]
            send[other, rows] = source[aligned((start + 1 - core) * SHARE, SHARE)]


def fold(small):
    pieces = []
    for chunk in range(6):
        piece = small[:, pair_columns(chunk // 2)]
        pieces.append(piece if chunk % 2 else roll(piece, 64, 1))
    folded = jnp.concatenate(pieces, axis=0)
    high = folded.astype(BF16).astype(F32)
    return jnp.concatenate([high, folded - high], axis=0)


def unfold(block):
    folded = block[:48] + block[48:]
    lower = iota((8, 128), 1) < 64
    pairs = []
    for pair in range(3):
        one, two = folded[16 * pair : 16 * pair + 8], folded[16 * pair + 8 : 16 * pair + 16]
        pairs.append(jnp.where(lower, roll(one, 64, 1), two))
    return jnp.concatenate(pairs, axis=1)


def tidy(block):
    folded = block[:48] + block[48:]
    high = folded.astype(BF16).astype(F32)
    parts = jnp.concatenate([high, folded - high], axis=0)
    return jnp.where(iota((ROWS, 128), 1) < 64, block, parts)


def late_grads(
    ids, t0, t1, t2, t3, low, small, head, rim, units, hidden_in, gate, out, value, branch, keep, send, *targets
):
    targets, tail, whole = targets[:-2], targets[-2], targets[-1]
    total = t0[...] + t1[...] + t2[...] + t3[...]
    straight = jnp.concatenate([total, jnp.zeros((128 - PART, TURNED), F32)], axis=0).T
    low_tail = low[:, WIDE:].astype(F32) + straight[:EXT]
    terms = jnp.sum(head[:RIM] * unit_rows(rim[...]), axis=0, keepdims=True)
    terms = terms + jnp.sum(head[RIM:] * units[...], axis=0, keepdims=True)
    grads = dot_first(hidden_in[...], low_tail)
    row = jnp.where(iota((8, D), 0) == 0, terms, 0.0)
    chosen = flag(iota((8, 128), 1) == GAIN_LANE)
    grads = grads + sum(dot_first(part, chosen) for part in split(row, 2))
    tail[...] = grads.astype(BF16)
    own = straight[EXT : EXT + 8]
    row = jnp.concatenate([own[0:1] + roll(own[1:2], 64, 1), own[2:3] + roll(own[3:4], 64, 1), own[4:5]], axis=1)
    folded = fold(jnp.where(iota((8, WIDE), 0) == 7, row, small[...]))
    lanes = iota((ROWS, 128), 1) < 64
    for target, place, block in places(ids, 0, targets[:5]):
        rows = aligned(block * ROWS, ROWS)
        target[place, :, :WIDE] = gate[rows]
        target[place, :, WIDE:] = value[rows]
    for target, place, block in places(ids, 1, targets[5:]):
        rows = aligned(block * ROWS, ROWS)
        target[place, :ROWS, :OUT_RIGHT] = out[rows]
        end = jnp.where(lanes, tail[rows].astype(F32), folded)
        target[place, :ROWS, OUT_RIGHT:] = end.astype(BF16)
    share_out(ids, head, branch, keep, send, whole)
    last = head[:RIM][8:]
    pieces = [last[:, RIGHT * chunk : RIGHT * chunk + RIGHT] for chunk in range(D // RIGHT)]
    pieces.append(jnp.zeros((8, RIGHT), F32))
    for slot in range(2):
        targets[8][slot, ROWS:] = jnp.concatenate(pieces[2 * slot : 2 * slot + 2], axis=0).astype(BF16)


def places(ids, side, targets):
    line, ctx = ids[0, 0], ids[0, 1]
    for far in range(4):
        for near in range(4):
            slot, place = far + far // 3, near
            if far == 2 and near >= 2:
                slot, place = 3, near - 2
            one, two = (near, far) if side else (far, near)
            yield targets[slot], place, ((line + one) & 3) * 4 + ((ctx + two) & 3)


def put(target, total, tailed):
    if tailed:
        target[:, :OUT_RIGHT] = total[:, :OUT_RIGHT].astype(BF16)
        target[:, OUT_RIGHT:] = tidy(total[:, OUT_RIGHT:]).astype(BF16)
    else:
        target[...] = total.astype(BF16)


def pair_halves(ids, keep, got, near, far):
    for other in range(4):
        target = far if other % 2 else near
        total = keep[other].astype(F32) + got[other].astype(F32)
        target[other // 2] = total.astype(BF16)


def relay(side, one, three, first, second, to_one, to_three):
    for near in range(4):
        if near < 2:
            total = one[near].astype(F32) + first[near].astype(F32)
            put(to_one.at[near], total, side)
            to_three[near] = three[near]
        else:
            total = three[near].astype(F32) + second[near - 2, :ROWS].astype(F32)
            put(to_three.at[near], total, side)
            to_one[near] = one[near]


def relay_both(ids, *refs):
    relay(0, *refs[:4], *refs[9:11])
    relay(1, *refs[4:8], *refs[11:13])
    second, behind = refs[7], refs[13]
    inside = jnp.where(ids[0, 1] < 3, 1.0, 0.0)
    for chunk in range(D // RIGHT):
        got = second[chunk // 2, ROWS:].astype(F32) * inside
        start = 8 * (chunk % 2)
        behind[:, RIGHT * chunk : RIGHT * chunk + RIGHT] = got[start : start + 8]


def halfway(side, own, one, three, *targets):
    for near, target in enumerate(targets):
        total = own[near].astype(F32) + one[near].astype(F32) + three[near].astype(F32)
        put(target, total, side)


def halfway_left(ids, own, one, three, right, *targets):
    halfway(0, own, one, three, *targets)


def halfway_right(ids, own, one, three, pair, *targets):
    halfway(1, own, one, three, *targets)


def pair_again(ids, near, got, cotangent, hidden, own, second, held, mine, last):
    for index, target in enumerate((own, second)):
        target[...] = (near[index].astype(F32) + got[index].astype(F32)).astype(BF16)
    held[...] = cotangent[...]
    mine[...] = hidden[aligned(ids[0, 2] * SHARE, SHARE)]
    last[...] = hidden[T - RIM :].astype(F32)[8:]


def collect_left(ids, a0, a1, a2, a3, b0, b1, b2, b3, grad_gate, grad_value, grad_out):
    total = sum(part[...].astype(F32) for part in (a0, a1, a2, a3))
    grad_gate[...] = total[:, :WIDE]
    grad_value[...] = total[:, WIDE:]
    grad_out[...] = sum(part[:, :OUT_RIGHT].astype(F32) for part in (b0, b1, b2, b3))


def hidden_back(grads, rows, gain):
    tokens = rows.astype(F32)
    inv = lax.rsqrt(jnp.mean(tokens * tokens, axis=1, keepdims=True) + EPSILON)
    unit = tokens * inv
    scaled = grads * gain
    return inv * (scaled - unit * jnp.mean(scaled * unit, axis=1, keepdims=True)), tokens


def gather_up(
    ids, b0, b1, b2, b3, p0, p1, mine, weights, behind,
    message, gain_out, grad_step, taps, offset, gain, bias, decay, skip, rest,
):
    both = p0[...].astype(F32) + p1[...].astype(F32)
    row = gain_row(weights[:, MIX:])
    gain_out[...] = jnp.broadcast_to(row, (8, D))
    grads, tokens = hidden_back(both[:SHARE], mine[...], row)
    message[:SHARE] = grads.astype(BF16)
    message[SHARE : 2 * SHARE] = (tokens + both[SHARE:]).astype(BF16)
    total = sum(part[:, OUT_RIGHT:].astype(F32) for part in (b0, b1, b2, b3))
    rest[...] = total
    small = unfold(total)
    state = small[7:8]
    lanes = iota((8, 128), 1)
    for tap in range(KERNEL + 1):
        piece = state[:, pair_columns(tap // 2)]
        piece = piece if tap % 2 == 0 else roll(piece, 64, 1)
        if tap == 0:
            rows = jnp.where(iota((8, 128), 0) == 0, roll(piece, STATE_LANE, 1), 0.0)
        else:
            rows = jnp.where(iota((8, 128), 0) == tap, roll(piece, STATE_LANE, 1), rows)
    rest[:8] = jnp.where(lanes < 64, rest[:8], rows)
    for block in range(ROWS // 16):
        message[2 * SHARE :, pair_columns(block)] = rest[16 * block : 16 * block + 16].astype(BF16)
    for block in range(6):
        pair = [behind[:, pair_columns(2 * block + i)] for i in range(2)]
        message[2 * SHARE :, pair_columns(6 + block)] = jnp.concatenate(pair, axis=0).astype(BF16)
    picked = flag(iota((8, 128), 1) == STEP_LANE + iota((8, 128), 0))
    grad_step[...] = pick(picked, total, 1, 1, 3)[:HEADS]
    taps[...] = small[:KERNEL]
    offset[...] = small[KERNEL : KERNEL + 1]
    gain[...] = small[5:6]
    bias[...] = small[6:7, :HEADS]
    decay[...] = small[6:7, 64 : 64 + HEADS]
    skip[...] = small[6:7, 128 : 128 + HEADS]


def finish(ids, *refs):
    pieces, row, cotangent, last = refs[:8], refs[8], refs[9], refs[10]
    grad_hidden, block_out, grad_state, grad_gain, taps, offset, rest, rims = refs[11:]
    chip, core = ids[0, 2] >> 1, ids[0, 2] & 1
    order = []
    for far in range(4):
        start = ((chip - far) & 3) * 2
        order += [(start + core, pieces[far]), (start + 1 - core, pieces[4 + far])]
    for place, piece in order:
        block_out[aligned(place * SHARE, SHARE)] = piece[SHARE : 2 * SHARE]
        for block in range(6):
            part = piece[2 * SHARE :, pair_columns(block)]
            rest[place, 16 * block : 16 * block + 16] = part.astype(F32)
            part = piece[2 * SHARE :, pair_columns(6 + block)].astype(F32)
            rims[place, :, pair_columns(2 * block)] = part[:8]
            rims[place, :, pair_columns(2 * block + 1)] = part[8:]
    total, behind = rest[0], rims[0]
    for i in range(1, 8):
        total = total + rest[i]
        behind = behind + rims[i]
    for place, piece in order:
        rows = aligned(place * SHARE, SHARE)
        grad_hidden[rows] = cotangent[rows].astype(F32) + piece[:SHARE].astype(F32)
    grads, _ = hidden_back(behind, last[...], row[0:1])
    grad_hidden[T - 8 :] = grad_hidden[T - 8 :] + grads
    lanes = iota((ROWS, 128), 1) >> 5
    for half in range(2):
        state = jnp.zeros((ROWS, 128), F32)
        small = jnp.zeros((8, 128), F32)
        for i in range(4):
            one = rest[4 * half + i]
            state = jnp.where(lanes == i, roll(one, PART * i, 1), state)
            small = jnp.where(lanes[:8] == i, roll(one[:8], PART * i - STATE_LANE, 1), small)
        columns = pair_columns(half)
        grad_state[:, columns] = state
        taps[:, columns] = small[:KERNEL]
        offset[:, columns] = small[KERNEL : KERNEL + 1]
    grad_gain[...] = pick(flag(iota((8, 128), 1) == GAIN_LANE), total, 1, 1, 3)[0:1]


def stack_blocks(ids, l0, l1, l2, l3, r0, r1, r2, r3, left, right, rim):
    for i, (one, two) in enumerate(((l0, r0), (l1, r1), (l2, r2), (l3, r3))):
        left[i] = one[:ROWS]
        right[i] = two[...]
    inside = jnp.where(ids[0, 1] > 0, 1.0, 0.0)
    got = l1[ROWS:].astype(F32) * inside
    none = jnp.zeros((8, PAIR), F32)
    rim[:, :PAIR] = jnp.concatenate([none, got[:8]], axis=0).astype(BF16)
    rim[:, PAIR:] = jnp.concatenate([none, got[8:]], axis=0).astype(BF16)


def shift(array, axis, steps):
    return lax.ppermute(array, axis, [(i, (i + steps) % 4) for i in range(4)])


def from_chip(array, steps):
    return lax.ppermute(array, "tp", [(i, (i + 2 * steps) % 8) for i in range(8)])


def across(array, bits):
    return lax.ppermute(array, "tp", [(i, i ^ bits) for i in range(8)])


def around(array, axis):
    return [array] + [shift(array, axis, steps) for steps in range(1, 4)]


def ring_sides(array, axis):
    return shift(array, axis, 1), shift(array, axis, 3)


def ring_rest(array, axis, one, three):
    return [array, one, shift(one[:2], axis, 1), shift(three[2:], axis, 3), three]


def chips_all(array):
    same = [array] + [from_chip(array, steps) for steps in range(1, 4)]
    return same + [across(one, 1) for one in same]


def per_device(
    hidden_states,
    norm_gain,
    gate_weight,
    value_weight,
    state_proj,
    step_proj,
    value_filter,
    value_offset,
    state_filter,
    state_offset,
    step_bias,
    decay_log,
    skip_gain,
    gate_norm_gain,
    out_weight,
    out_grad,
):
    hidden = hidden_states[0]
    cotangent = out_grad[0]
    places = [lax.axis_index(axis).astype(jnp.int32) for axis in ("dp", "ctx", "tp")]
    ids = jnp.stack(places).reshape(1, 3)

    left, longer, right = fuse(
        prepare,
        [((ROWS, PAIR), BF16), ((ROWS + RIM, PAIR), BF16), ((ROWS, PAIR), BF16)],
        ids,
        value_weight,
        gate_weight,
        state_proj,
        step_proj.T,
        norm_gain[None],
        out_weight.T,
        hidden,
        fetch=7,
        rim=True,
    )
    near = [left, shift(longer, "ctx", 1), shift(left, "ctx", 2), shift(left, "ctx", 3)]
    left, right, rim = fuse(
        stack_blocks,
        [((4, ROWS, PAIR), BF16)] * 2 + [((RIM, D), BF16)],
        ids,
        *near,
        *around(right, "dp"),
    )
    consts, units = fuse(
        tabulate,
        [((16, FIRST), F32), ((T, D), F32)],
        ids,
        value_filter,
        state_filter,
        value_offset[None],
        state_offset[None],
        gate_norm_gain[None],
        jnp.stack([step_bias, decay_log, skip_gain]),
        hidden,
        fetch=7,
    )
    left = ring_rest(left, "dp", *ring_sides(left, "dp"))
    right = ring_rest(right, "ctx", *ring_sides(right, "ctx"))
    weights, hidden_in, taken, wide, narrow, message = fuse(
        enter,
        [
            ((D, FIRST), BF16),
            ((EXT, D), BF16),
            ((EXT, MIX), BF16),
            ((T, LOG_DECAY.stop), F32),
            ((T, WEIGHTED.stop), BF16),
            ((STATE + 16, WIDE), BF16),
        ],
        ids,
        *left,
        *right,
        rim,
        units,
        consts,
    )
    messages = around(message, "ctx")[1:]
    gate_out, before, slope, spread = fuse(
        project,
        [((D, 2 * WIDE), BF16), ((T, SKIPPED.stop), F32), ((T, MIX), F32), ((T, STEPS.stop), F32)],
        ids,
        *left,
        *right,
        hidden_in,
        cotangent,
        wide,
        narrow,
        consts,
    )
    state, after, sums = fuse(
        mix,
        [((STATE + 24, WIDE), F32), ((T, MIXED.stop), F32), ((8, T), F32)],
        ids,
        *messages,
        spread,
        narrow,
        before,
    )
    (ready,) = fuse(gate_ready, [((5, T, WIDE), F32)], ids, after, before, consts)
    sums = sums + across(sums, 1)
    gated_low, grad_mixed, grad_gain, sensitivity = fuse(
        gate_back,
        [
            ((T, LOW_GATE.stop), BF16),
            ((T, WIDE), F32),
            ((8, WIDE), F32),
            ((STATE, WIDE), BF16),
        ],
        ids,
        sums,
        *[from_chip(sums, steps) for steps in range(1, 4)],
        ready,
        before,
        spread,
        narrow,
    )
    later = [shift(sensitivity, "ctx", -steps) for steps in range(1, 4)]
    square = ((D, WIDE), BF16)
    gate, out, grads, branch, inner = fuse(
        middle,
        [square, square, ((T, MIX), F32), ((T, D), BF16), ((T, 256), F32)],
        ids,
        hidden_in,
        gated_low,
        cotangent,
        gate_out,
        wide,
        narrow,
        grad_mixed,
        state,
        spread,
        after,
    )
    low, state_low, keep, send, small = fuse(
        leave,
        [((EXT, WIDE + 128), BF16), ((EXT, 2 * STATE), F32)] + [((4, PART, TURNED), F32)] * 2 + [((8, WIDE), F32)],
        ids,
        *later,
        state,
        inner,
        grad_mixed,
        grads,
        wide,
        spread,
        slope,
        narrow,
        consts,
        taken,
        grad_gain,
        scratch=[((2 * STATE, TURNED), F32)],
    )
    pair = fuse(pair_sum, [((PART, TURNED), F32)] * 4, ids, keep, across(send, 1))
    turned = pair[:1] + [from_chip(pair[steps], steps) for steps in range(1, 4)]
    value, head = fuse(
        value_grads,
        [square, ((EXT, D), F32)],
        ids,
        low,
        state_low,
        gated_low,
        weights,
        gate_out,
        hidden_in,
        pair[0],
    )
    both = ((2 * SHARE, D), BF16)
    two = ((2, 2 * SHARE, D), BF16)

    def stage(count, rows, columns):
        return (count, rows, columns), BF16

    def stages(columns, rows):
        whole = stage(4, ROWS, columns)
        return [whole, whole, stage(2, ROWS, columns), stage(2, rows, columns), whole]

    keep, send, *blocks = fuse(
        late_grads,
        [((4, 2 * SHARE, D), BF16)] * 2 + stages(LEFT, ROWS) + stages(RIGHT, ROWS + RIM),
        ids,
        *turned,
        low,
        small,
        head,
        rim,
        units,
        hidden_in,
        gate,
        out,
        value,
        branch,
        scratch=[((D, 128), BF16), ((T, D), BF16)],
    )
    left, right = blocks[:5], blocks[5:]
    near, far = fuse(pair_halves, [two] * 2, ids, keep, across(send, 1))
    *sides, behind = fuse(
        relay_both,
        [stage(4, ROWS, LEFT)] * 2 + [stage(4, ROWS, RIGHT)] * 2 + [((8, D), F32)],
        ids,
        *(left[1], left[4], shift(left[2], "dp", 1), shift(left[3], "dp", 3)),
        *(right[1], right[4], shift(right[2], "ctx", 1), shift(right[3], "ctx", 3)),
        near,
    )
    left = [left[0], shift(sides[0], "dp", 1), shift(sides[1], "dp", 3)]
    right = [right[0], shift(sides[2], "ctx", 1), shift(sides[3], "ctx", 3)]
    own, second, held, mine, last = fuse(
        pair_again,
        [both, both, ((T, D), BF16), ((SHARE, D), BF16), ((8, D), F32)],
        ids,
        near,
        across(far, 2),
        cotangent,
        hidden,
    )
    right = fuse(halfway_right, [((ROWS, RIGHT), BF16)] * 4, ids, *right, own)
    left = fuse(halfway_left, [((ROWS, LEFT), BF16)] * 4, ids, *left, right[0])
    left = left[:1] + [shift(left[steps], "ctx", steps) for steps in range(1, 4)]
    right = right[:1] + [shift(right[steps], "dp", steps) for steps in range(1, 4)]
    few, line = ((1, HEADS), F32), ((1, WIDE), F32)
    message, gain_full, *few_grads = fuse(
        gather_up,
        [((2 * SHARE + 16, D), BF16), ((8, D), F32), ((HEADS, ROWS), F32), ((KERNEL, WIDE), F32)]
        + [line, line, few, few, few],
        ids,
        *right,
        own,
        across(second, 4),
        mine,
        weights,
        behind,
        scratch=[((ROWS, 128), F32)],
    )
    grad_step, taps, offset, gain, bias, decay, skip = few_grads
    grad_gate, grad_value, grad_out = fuse(
        collect_left, [((ROWS, WIDE), F32)] * 3, ids, *left, *right
    )
    grad_hidden, block_out, grad_state, grad_norm_gain, state_taps, state_offset = fuse(
        finish,
        [
            ((T, D), F32),
            ((T, D), BF16),
            ((ROWS, 2 * STATE), F32),
            ((1, ROWS), F32),
            ((KERNEL, 2 * STATE), F32),
            ((1, 2 * STATE), F32),
        ],
        ids,
        *chips_all(message),
        gain_full,
        held,
        last,
        scratch=[((8, ROWS, 128), F32), ((8, 8, D), F32)],
    )
    return (
        block_out[None],
        grad_hidden[None],
        grad_norm_gain[0],
        grad_gate,
        grad_value,
        grad_state,
        grad_step.T,
        taps,
        offset[0],
        state_taps,
        state_offset[0],
        bias[0],
        decay[0],
        skip[0],
        gain[0],
        grad_out.T,
    )


def solution(mesh):
    line = P(("dp", "ctx"))
    placed = (
        P("dp", "ctx", None),
        line,
        P(("dp", "ctx"), "tp"),
        P(("dp", "ctx"), "tp"),
        P(("dp", "ctx"), None),
        P(("dp", "ctx"), "tp"),
        P(None, "tp"),
        P("tp"),
        P(),
        P(),
        P("tp"),
        P("tp"),
        P("tp"),
        P("tp"),
        P("tp", ("dp", "ctx")),
        P("dp", "ctx", None),
    )
    given = (
        P("dp", "ctx", None),
        P("dp", "ctx", None),
        line,
        P(("dp", "ctx"), "tp"),
        P(("dp", "ctx"), "tp"),
        P(("dp", "ctx"), None),
        P(("dp", "ctx"), "tp"),
        P(None, "tp"),
        P("tp"),
        P(),
        P(),
        P("tp"),
        P("tp"),
        P("tp"),
        P("tp"),
        P("tp", ("dp", "ctx")),
    )
    return jax.shard_map(
        per_device, mesh=mesh, in_specs=placed, out_specs=given, check_vma=False
    )
```

```python
import jax
import jax.numpy as jnp
from jax import lax
from jax.experimental import pallas as pl
from jax.experimental.pallas import tpu as pltpu
from jax.sharding import PartitionSpec as P

F32 = jnp.float32
BF16 = jnp.bfloat16
EPSILON = 1e-05
INNER = 3072
D = 1536
T = 256
RIM = 16
EXT = T + RIM
KERNEL = 4
HEADS = 6
WIDE = 384
STATE = 128
MIX = WIDE + 2 * STATE
FIRST = MIX + 128
ROWS = 96
SHARES = 16
PAIR = 2 * WIDE
RIGHT = 512
OUT_RIGHT = RIGHT - 128
LEFT = 3 * WIDE - OUT_RIGHT
SHARE = T // 8
PART = 32
STEP_LANE = 32
GAIN_LANE = STEP_LANE + HEADS
STATE_LANE = 64
TURNED = 384
VMEM_LIMIT = 8 * 2**20

VALUES, SLOPE = slice(0, WIDE), slice(WIDE, WIDE + MIX)
STEP, STEP_SLOPE, LOG_DECAY = slice(1024, 1152), slice(1152, 1280), slice(1280, 1408)
BMAT, CMAT, WEIGHTED = slice(0, 128), slice(128, 256), slice(256, 640)
GATE, GRAD_NORMED, WITHIN = slice(0, 384), slice(384, 768), slice(768, 1152)
GATE_SLOPE, SCALED, SKIPPED = slice(1152, 1536), slice(1536, 1920), slice(1920, 2304)
INSIDE, MIXED = slice(0, 384), slice(384, 768)
NORMED, LOW_GATE = slice(0, 384), slice(384, 768)
GROWN, TO_END, STEPS = slice(0, 384), slice(384, 768), slice(768, 1152)


WORK = {"pair_again": 2 * 10**9, "collect_left": 5 * 10**9}


def fuse(function, outputs, ids, *arrays, scratch=(), fetch=0, rim=False):
    count = len(arrays)
    plain = count - fetch
    shapes = [array.shape for array in arrays]
    if rim:
        shapes[-1] = (RIM, D)

    def body(*refs):
        if not fetch:
            function(*refs)
            return
        given = list(refs[1 + plain : 1 + count])
        held, done = refs[-1 - fetch : -1], refs[-1]
        if rim:
            given[-1] = given[-1].at[pl.ds(T - RIM, RIM)]
        copies = [
            pltpu.make_async_copy(source, target, done.at[i])
            for i, (source, target) in enumerate(zip(given, held))
        ]
        for copy in copies:
            copy.start()

        def ready():
            for copy in copies:
                copy.wait()

        function(*refs[: 1 + plain], *held, *refs[1 + count : -1 - fetch], ready=ready)

    buffers = [pltpu.VMEM(shape, dtype) for shape, dtype in scratch]
    spaces = [pltpu.SMEM] + [pltpu.VMEM] * plain + [pltpu.HBM] * fetch
    if fetch:
        buffers += [pltpu.VMEM(shapes[i], arrays[i].dtype) for i in range(plain, count)]
        buffers += [pltpu.SemaphoreType.DMA((fetch,))]
        held = [pltpu.with_memory_space_constraint(array, pltpu.HBM) for array in arrays[plain:]]
        arrays = (*arrays[:plain], *held)
    cost = None
    if function.__name__ in WORK:
        cost = pl.CostEstimate(
            flops=WORK[function.__name__], bytes_accessed=10**6, transcendentals=1
        )
    call = pl.pallas_call(
        body,
        out_shape=[jax.ShapeDtypeStruct(shape, dtype) for shape, dtype in outputs],
        in_specs=[pl.BlockSpec(memory_space=space) for space in spaces],
        out_specs=[pl.BlockSpec(memory_space=pltpu.VMEM) for _ in outputs],
        scratch_shapes=buffers,
        compiler_params=pltpu.CompilerParams(vmem_limit_bytes=VMEM_LIMIT),
        cost_estimate=cost,
        name=function.__name__,
    )
    return list(call(ids, *arrays))


def roll(array, shift, axis):
    return pltpu.roll(array, shift % array.shape[axis], axis)


def product(a, b, left, right):
    return lax.dot_general(
        a.astype(BF16),
        b.astype(BF16),
        (((left,), (right,)), ((), ())),
        preferred_element_type=F32,
    )


def dot(a, b):
    return product(a, b, 1, 0)


def dot_last(a, b):
    return product(a, b, 1, 1)


def dot_first(a, b):
    return product(a, b, 0, 0)


def split(array, count):
    parts = []
    for _ in range(count):
        part = array.astype(BF16)
        parts.append(part)
        array = array - part.astype(F32)
    return parts


def twice(a, b, left, right):
    return sum(product(part, b, left, right) for part in split(a, 2))


def pick(chosen, array, left, right, parts=2):
    return sum(product(chosen, part, left, right) for part in split(array, parts))


def iota(shape, axis):
    return lax.broadcasted_iota(jnp.int32, shape, axis)


def flag(condition):
    return jnp.where(condition, 1.0, 0.0)


def silu_parts(array):
    sig = jax.nn.sigmoid(array)
    return array * sig, sig * (1.0 + array * (1.0 - sig))


def spread_heads(array):
    rows = array.shape[0]
    lower = iota((rows, 128), 1) < 64
    pieces = [
        jnp.where(lower, array[:, h : h + 1], array[:, h + 1 : h + 2]) for h in range(0, HEADS, 2)
    ]
    return jnp.concatenate(pieces, axis=1)


def head_sums(array):
    chosen = flag((iota((128, WIDE), 1) >> 6) == iota((128, WIDE), 0))
    return sum(dot_last(part, chosen) for part in split(array, 2))


def gain_row(tail):
    return dot_last(flag(iota((8, 128), 1) == GAIN_LANE), tail)[0:1]


def unit_rows(rows):
    tokens = rows.astype(F32)
    inv = lax.rsqrt(jnp.mean(tokens * tokens, axis=1, keepdims=True) + EPSILON)
    return tokens * inv


def aligned(start, size):
    return pl.ds(pl.multiple_of(start, size), size)


def prepare(
    ids, value_weight, gate_weight, state_proj, step_proj, norm_gain, out_weight, rim, left, longer, right, ready
):
    ready()
    for target in (left, longer):
        target[:ROWS, :WIDE] = value_weight[...]
        target[:ROWS, WIDE:] = gate_weight[...]
    last = rim[...].astype(F32)[8:]
    longer[ROWS:] = jnp.concatenate([last[:, :PAIR], last[:, PAIR:]], axis=0).astype(BF16)
    right[:, : 2 * STATE] = state_proj[...]
    place = iota((HEADS, 128), 1) == STEP_LANE + iota((HEADS, 128), 0)
    tail = dot_first(step_proj[...], flag(place))
    tail = tail + dot_first(norm_gain[...], flag(iota((1, 128), 1) == GAIN_LANE))
    right[:, 2 * STATE : WIDE] = tail.astype(BF16)
    right[:, WIDE:] = out_weight[...]


def tabulate(
    ids, value_filter, state_filter, value_offset, state_offset, gate_gain, heads, hidden, consts, units, ready
):
    ready()
    units[...] = unit_rows(hidden[...])
    consts[...] = jnp.zeros(consts.shape, F32)
    consts[:KERNEL, :WIDE] = value_filter[...].astype(F32)
    consts[:KERNEL, WIDE:MIX] = state_filter[...].astype(F32)
    consts[KERNEL : KERNEL + 1, :WIDE] = value_offset[...].astype(F32)
    consts[KERNEL : KERNEL + 1, WIDE:MIX] = state_offset[...].astype(F32)
    consts[5:6, :WIDE] = gate_gain[...].astype(F32)
    consts[6:9, :HEADS] = heads[...]


def place_blocks(ids, left, right, *moves):
    line, ctx = ids[0, 0], ids[0, 1]

    def piece(side, far, near):
        if far == 2:
            return (side[2], near) if near < 2 else (side[3], near - 2)
        return side[far + far // 3], near

    for far in range(4):
        for near in range(4):
            for target, side, start, source, size in moves:
                if side == 0:
                    block = ((line - far) & 3) * 4 + ((ctx - near) & 3)
                else:
                    block = ((line - near) & 3) * 4 + ((ctx - far) & 3)
                array, place = piece((left, right)[side], far, near)
                target[aligned(block * ROWS, ROWS), start : start + size] = array[
                    place, :, source : source + size
                ]


def enter(
    ids, l0, l1, l2, l3, l4, r0, r1, r2, r3, r4, rim, units, consts,
    weights, hidden_in, taken, wide, narrow, message,
):
    moves = (weights, 0, 0, 0, WIDE), (weights, 1, WIDE, 0, WIDE)
    place_blocks(ids, (l0, l1, l2, l3, l4), (r0, r1, r2, r3, r4), *moves)
    gain = gain_row(weights[:, MIX:])
    hidden_in[:RIM] = (unit_rows(rim[...]) * gain).astype(BF16)
    hidden_in[RIM:] = (units[...] * gain).astype(BF16)
    projected = dot(hidden_in[...], weights[...])
    inputs = projected[:, :MIX].astype(BF16)
    taken[...] = inputs
    inputs = inputs.astype(F32)
    filter_pre = consts[KERNEL : KERNEL + 1, :MIX]
    for tap in range(KERNEL):
        filter_pre = filter_pre + consts[tap : tap + 1, :MIX] * roll(inputs, KERNEL - 1 - tap, 0)[RIM:]
    wide[:, SLOPE] = filter_pre
    activated = filter_pre * jax.nn.sigmoid(filter_pre)
    lanes = iota((T, 128), 1) < HEADS
    step_in = roll(projected[RIM:, MIX:], 128 - STEP_LANE, 1) + consts[6:7, :128]
    step_in = jnp.where(lanes, step_in, -100.0)
    step = jnp.maximum(step_in, 0.0) + jnp.log1p(jnp.exp(-jnp.abs(step_in)))
    step = jnp.where(lanes, step, 0.0)
    rate = jnp.exp(consts[7:8, :128])
    log_decay = pick(flag(iota((T, T), 0) >= iota((T, T), 1)), -step * rate, 1, 0, 3)
    values = activated[:, :WIDE]
    weighted = (values * spread_heads(step)).astype(BF16)
    wide[:, VALUES] = values
    wide[:, STEP] = step
    wide[:, STEP_SLOPE] = jax.nn.sigmoid(step_in)
    wide[:, LOG_DECAY] = log_decay
    narrow[:, BMAT] = activated[:, WIDE : WIDE + STATE].astype(BF16)
    narrow[:, CMAT] = activated[:, WIDE + STATE :].astype(BF16)
    narrow[:, WEIGHTED] = weighted
    last = log_decay[T - 1 :]
    to_end = spread_heads(jnp.exp(last - log_decay))
    message[:STATE] = dot_first(narrow[:, BMAT], weighted.astype(F32) * to_end).astype(BF16)
    span = spread_heads(last)
    high = span.astype(BF16).astype(F32)
    line = iota((16, WIDE), 0)
    tail = jnp.where(line == 0, high, jnp.where(line == 1, span - high, 0.0))
    message[STATE:] = tail.astype(BF16)


def decays(log_decay, turned, head):
    gap = log_decay[:, head : head + 1] - turned[head : head + 1, :]
    return jnp.exp(jnp.where(iota((T, T), 0) >= iota((T, T), 1), gap, -1e30))


def pair_columns(pair):
    return slice(128 * pair, 128 * pair + 128)


def project(
    ids, l0, l1, l2, l3, l4, r0, r1, r2, r3, r4, hidden_in, cotangent, wide, narrow, consts,
    gate_out, before, slope, spread,
):
    moves = (gate_out, 0, 0, WIDE, WIDE), (gate_out, 1, WIDE, WIDE, WIDE)
    place_blocks(ids, (l0, l1, l2, l3, l4), (r0, r1, r2, r3, r4), *moves)
    _, slope[...] = silu_parts(wide[:, SLOPE])
    last = wide[T - 1 :, LOG_DECAY]
    spread[:, GROWN] = spread_heads(jnp.exp(wide[:, LOG_DECAY]))
    spread[:, TO_END] = spread_heads(jnp.exp(last - wide[:, LOG_DECAY]))
    spread[:, STEPS] = spread_heads(wide[:, STEP])
    act, gate_slope = silu_parts(dot(hidden_in[RIM:], gate_out[:, :WIDE]))
    grads = dot(cotangent[...], gate_out[:, WIDE:])
    before[:, GATE] = act
    before[:, GATE_SLOPE] = gate_slope
    before[:, GRAD_NORMED] = grads
    before[:, SCALED] = grads * consts[5:6, :WIDE] * act
    before[:, SKIPPED] = wide[:, VALUES] * spread_heads(consts[8:9, :128])
    scores = dot_last(narrow[:, CMAT], narrow[:, BMAT])
    log_decay = wide[:, LOG_DECAY]
    turned = log_decay.T
    lower = iota((T, 128), 1) < 64
    weighted = narrow[:, WEIGHTED]
    for pair in range(HEADS // 2):
        part = weighted[:, pair_columns(pair)]
        one = dot(scores * decays(log_decay, turned, 2 * pair), part)
        two = dot(scores * decays(log_decay, turned, 2 * pair + 1), part)
        start = WITHIN.start + 128 * pair
        before[:, start : start + 128] = jnp.where(lower, one, two)


def mix(ids, m1, m2, m3, spread, narrow, before, state, after, sums):
    me = ids[0, 1]
    total = jnp.zeros((STATE, WIDE), F32)
    gap = jnp.zeros((1, WIDE), F32)
    for back, message in enumerate((m1, m2, m3)):
        tail = message[STATE:].astype(F32)
        log = tail[0:1] + tail[1:2]
        state[STATE + 8 * back : STATE + 8 * back + 8] = jnp.broadcast_to(log, (8, WIDE))
        scale = jnp.exp(gap) * jnp.where(me > back, 1.0, 0.0)
        total = total + scale * message[:STATE].astype(F32)
        gap = gap + log
    state[:STATE] = total
    inside = before[:, WITHIN] + dot(narrow[:, CMAT], total) * spread[:, GROWN]
    after[:, INSIDE] = inside
    whole = inside + before[:, SKIPPED]
    after[:, MIXED] = whole
    gated = whole * before[:, GATE]
    ones = jnp.ones((8, WIDE), F32)
    squares = pick(ones, gated * gated, 1, 1)
    crosses = pick(ones, before[:, SCALED] * whole, 1, 1)
    sums[...] = jnp.where(iota((8, T), 0) < 4, squares, crosses)


def gate_ready(ids, after, before, consts, ready):
    mixed, act = after[:, MIXED], before[:, GATE]
    gated, rest = mixed * act, mixed * before[:, GATE_SLOPE]
    ready[0] = gated * act
    ready[1] = before[:, GRAD_NORMED] * consts[5:6, :WIDE] * rest
    ready[2] = gated * rest
    ready[3] = gated * consts[5:6, :WIDE]
    ready[4] = before[:, GRAD_NORMED] * gated


def gate_back(ids, s0, s1, s2, s3, ready, before, spread, narrow, gated_low, grad_mixed, grad_gain, sensitivity):
    total = s0[...] + s1[...] + s2[...] + s3[...]
    chosen = flag(iota((8, 128), 0) == 4 * iota((8, 128), 1))
    columns = sum(dot_first(part, chosen) for part in split(total, 3))
    inv = lax.rsqrt(columns[:, 0:1] / INNER + EPSILON)
    back = inv * (inv * inv * columns[:, 1:2] / INNER)
    own = inv * before[:, SCALED] - back * ready[0]
    grad_mixed[...] = own
    sensitivity[...] = dot_first(narrow[:, CMAT], own * spread[:, GROWN]).astype(BF16)
    gated_low[:, LOW_GATE] = (inv * ready[1] - back * ready[2]).astype(BF16)
    gated_low[:, NORMED] = (inv * ready[3]).astype(BF16)
    grad_gain[...] = jnp.broadcast_to(jnp.sum(inv * ready[4], axis=0, keepdims=True), (8, WIDE))


def turn_out(ids, source, keep, send):
    chip, core = ids[0, 2] >> 1, ids[0, 2] & 1
    for ahead in range(4):
        start = ((chip + ahead) & 3) * 2
        keep[ahead] = source[aligned((start + core) * SHARE, SHARE)]
        send[ahead] = source[aligned((start + 1 - core) * SHARE, SHARE)]


def middle(
    ids, hidden_in, gated_low, cotangent, gate_out, wide, narrow, grad_mixed, state, spread, after,
    gate, out, grads, branch, sums,
):
    gate[...] = dot_first(hidden_in[RIM:], gated_low[:, LOW_GATE]).astype(BF16)
    out[...] = dot_first(cotangent[...], gated_low[:, NORMED]).astype(BF16)
    branch[...] = dot_last(gated_low[:, NORMED], gate_out[:, WIDE:]).astype(BF16)
    bmat, cmat, weighted = narrow[:, BMAT], narrow[:, CMAT], narrow[:, WEIGHTED]
    scores = dot_last(cmat, bmat)
    log_decay = wide[:, LOG_DECAY]
    turned = log_decay.T
    lower = iota((T, 128), 1) < 64
    grad_scores = jnp.zeros((T, T), F32)
    for pair in range(HEADS // 2):
        part = weighted[:, pair_columns(pair)]
        grad = grad_mixed[:, pair_columns(pair)]
        got = []
        for side in range(2):
            weights = decays(log_decay, turned, 2 * pair + side)
            got.append(dot_first(scores * weights, grad))
            own = jnp.where(lower, grad, 0.0) if side == 0 else jnp.where(lower, 0.0, grad)
            grad_scores = grad_scores + twice(own, part, 1, 1) * weights
        grads[:, pair_columns(pair)] = jnp.where(lower, got[0], got[1])
    grads[:, WIDE : WIDE + STATE] = twice(grad_scores, cmat, 0, 0)
    own = grad_mixed[...]
    from_state = own * spread[:, GROWN]
    grads[:, WIDE + STATE :] = twice(grad_scores, bmat, 1, 0) + sum(
        dot_last(from_state, part) for part in split(state[:STATE], 2)
    )
    inputs = grads[:, :WIDE]
    own = own.astype(BF16).astype(F32) * after[:, INSIDE] - weighted.astype(F32) * inputs
    sums[:, :128] = head_sums(own)
    sums[:, 128:] = head_sums(wide[:, VALUES] * inputs)


def leave(
    ids, g1, g2, g3, state, inner, grad_mixed, grads, wide, spread, slope, narrow, consts, taken, grad_gain,
    low, state_low, keep, send, small, turned,
):
    me = ids[0, 1]
    end = jnp.zeros((STATE, WIDE), F32)
    gap = jnp.zeros((1, WIDE), F32)
    for ahead, message in enumerate((g1, g2, g3)):
        scale = jnp.exp(gap) * jnp.where(me + ahead < 3, 1.0, 0.0)
        end = end + scale * message[...].astype(F32)
        start = STATE + 8 * (2 - ahead)
        gap = gap + state[start : start + 1]
    step, step_slope = wide[:, STEP], wide[:, STEP_SLOPE]
    values = wide[:, VALUES]
    last = wide[T - 1 :, LOG_DECAY]
    to_end = spread[:, TO_END]
    weighted = narrow[:, WEIGHTED].astype(F32)
    own = grad_mixed[...]
    from_end = dot(narrow[:, BMAT], end) * to_end
    inputs = grads[:, :WIDE] + from_end
    from_b = grads[:, WIDE : WIDE + STATE]
    from_b = from_b + sum(dot_last(weighted * to_end, part) for part in split(end, 2))
    from_c = grads[:, WIDE + STATE :]
    sums = head_sums(values * from_end)
    ended = step * sums
    at_end = jnp.exp(spread_heads(last)) * jnp.sum(end * state[:STATE], axis=0, keepdims=True)
    at_end = head_sums(jnp.broadcast_to(at_end, (8, WIDE)))[0:1]
    at_end = at_end + jnp.sum(ended, axis=0, keepdims=True)
    grad_log = inner[:, :128] - ended
    grad_decay = pick(flag(iota((T, T), 0) <= iota((T, T), 1)), grad_log, 1, 0) + at_end
    rate = jnp.exp(consts[7:8, :128])
    grad_step = inner[:, 128:] + sums - rate * grad_decay
    grad_step_pre = grad_step * step_slope
    grad_values = own * spread_heads(consts[8:9, :128]) + inputs * spread[:, STEPS]
    grad_pre = jnp.concatenate([grad_values, from_b, from_c], axis=1) * slope[...]
    before = taken[...].astype(F32)
    padded = jnp.concatenate([jnp.zeros((RIM, MIX), F32), grad_pre], axis=0)
    grad_input = jnp.zeros((EXT, MIX), F32)
    line = iota((8, MIX), 0)
    taps = jnp.where(line == KERNEL, jnp.sum(grad_pre, axis=0, keepdims=True), 0.0)
    for tap in range(KERNEL):
        later = roll(padded, tap + 1 - KERNEL, 0)
        taps = jnp.where(line == tap, jnp.sum(before * later, axis=0, keepdims=True), taps)
        grad_input = grad_input + consts[tap : tap + 1, :MIX] * later
    low[:, :WIDE] = grad_input[:, :WIDE].astype(BF16)
    state_low[...] = grad_input[:, WIDE:]
    low_step = jnp.concatenate([jnp.zeros((RIM, 128), F32), grad_step_pre], axis=0)
    low[:, WIDE:] = roll(low_step, STEP_LANE, 1).astype(BF16)
    rest = jnp.zeros((TURNED - EXT - 8, 2 * STATE), F32)
    turned[...] = jnp.concatenate([grad_input[:, WIDE:], taps[:, WIDE:], rest], axis=0).T
    turn_out(ids, turned, keep, send)
    heads = (
        jnp.sum(grad_step_pre, axis=0, keepdims=True),
        -rate * jnp.sum(grad_decay * step, axis=0, keepdims=True),
        head_sums(jnp.broadcast_to(jnp.sum(own * values, axis=0, keepdims=True), (8, WIDE)))[0:1],
    )
    none = jnp.zeros((1, 128), F32)
    heads = jnp.concatenate([heads[0] + roll(heads[1], 64, 1), heads[2], none], axis=1)
    line = iota((8, WIDE), 0)
    small[...] = jnp.where(line == 5, grad_gain[...], jnp.where(line == 6, heads, taps[:, :WIDE]))


def pair_sum(ids, keep, got, *shares):
    for ahead, share in enumerate(shares):
        share[...] = (keep[ahead].astype(F32) + got[ahead].astype(F32)).astype(share.dtype)


def value_grads(
    ids, low, state_low, gated_low, weights, gate_out, hidden_in, pair, value, head
):
    value[...] = dot_first(hidden_in[...], low[:, :WIDE]).astype(BF16)
    part = dot_last(low[:, :WIDE], weights[:, :WIDE]) + dot_last(low[:, WIDE:], weights[:, MIX:])
    high, rest = split(state_low[...], 2)
    part = part + dot_last(high, weights[:, WIDE:MIX]) + dot_last(rest, weights[:, WIDE:MIX])
    head[:RIM] = part[:RIM]
    head[RIM:] = part[RIM:] + dot_last(gated_low[:, LOW_GATE], gate_out[:, :WIDE])


def share_out(ids, head, branch, keep, send, whole):
    whole[...] = head[RIM:].astype(BF16)
    chip, core = ids[0, 2] >> 1, ids[0, 2] & 1
    for other in range(4):
        start = (chip ^ other) * 2
        for half, source in enumerate((whole, branch)):
            rows = slice(half * SHARE, half * SHARE + SHARE)
            keep[other, rows] = source[aligned((start + core) * SHARE, SHARE)]
            send[other, rows] = source[aligned((start + 1 - core) * SHARE, SHARE)]


def fold(small):
    pieces = []
    for chunk in range(6):
        piece = small[:, pair_columns(chunk // 2)]
        pieces.append(piece if chunk % 2 else roll(piece, 64, 1))
    folded = jnp.concatenate(pieces, axis=0)
    high = folded.astype(BF16).astype(F32)
    return jnp.concatenate([high, folded - high], axis=0)


def unfold(block):
    folded = block[:48] + block[48:]
    lower = iota((8, 128), 1) < 64
    pairs = []
    for pair in range(3):
        one, two = folded[16 * pair : 16 * pair + 8], folded[16 * pair + 8 : 16 * pair + 16]
        pairs.append(jnp.where(lower, roll(one, 64, 1), two))
    return jnp.concatenate(pairs, axis=1)


def tidy(block):
    folded = block[:48] + block[48:]
    high = folded.astype(BF16).astype(F32)
    parts = jnp.concatenate([high, folded - high], axis=0)
    return jnp.where(iota((ROWS, 128), 1) < 64, block, parts)


def late_grads(
    ids, t0, t1, t2, t3, low, small, head, rim, units, hidden_in, gate, out, value, branch, keep, send, *targets
):
    targets, tail, whole = targets[:-2], targets[-2], targets[-1]
    total = t0[...] + t1[...] + t2[...] + t3[...]
    straight = jnp.concatenate([total, jnp.zeros((128 - PART, TURNED), F32)], axis=0).T
    low_tail = low[:, WIDE:].astype(F32) + straight[:EXT]
    terms = jnp.sum(head[:RIM] * unit_rows(rim[...]), axis=0, keepdims=True)
    terms = terms + jnp.sum(head[RIM:] * units[...], axis=0, keepdims=True)
    grads = dot_first(hidden_in[...], low_tail)
    row = jnp.where(iota((8, D), 0) == 0, terms, 0.0)
    chosen = flag(iota((8, 128), 1) == GAIN_LANE)
    grads = grads + sum(dot_first(part, chosen) for part in split(row, 2))
    tail[...] = grads.astype(BF16)
    own = straight[EXT : EXT + 8]
    row = jnp.concatenate([own[0:1] + roll(own[1:2], 64, 1), own[2:3] + roll(own[3:4], 64, 1), own[4:5]], axis=1)
    folded = fold(jnp.where(iota((8, WIDE), 0) == 7, row, small[...]))
    lanes = iota((ROWS, 128), 1) < 64
    for target, place, block in places(ids, 0, targets[:5]):
        rows = aligned(block * ROWS, ROWS)
        target[place, :, :WIDE] = gate[rows]
        target[place, :, WIDE:] = value[rows]
    for target, place, block in places(ids, 1, targets[5:]):
        rows = aligned(block * ROWS, ROWS)
        target[place, :ROWS, :OUT_RIGHT] = out[rows]
        end = jnp.where(lanes, tail[rows].astype(F32), folded)
        target[place, :ROWS, OUT_RIGHT:] = end.astype(BF16)
    share_out(ids, head, branch, keep, send, whole)
    last = head[:RIM][8:]
    pieces = [last[:, RIGHT * chunk : RIGHT * chunk + RIGHT] for chunk in range(D // RIGHT)]
    pieces.append(jnp.zeros((8, RIGHT), F32))
    for slot in range(2):
        targets[8][slot, ROWS:] = jnp.concatenate(pieces[2 * slot : 2 * slot + 2], axis=0).astype(BF16)


def places(ids, side, targets):
    line, ctx = ids[0, 0], ids[0, 1]
    for far in range(4):
        for near in range(4):
            slot, place = far + far // 3, near
            if far == 2 and near >= 2:
                slot, place = 3, near - 2
            one, two = (near, far) if side else (far, near)
            yield targets[slot], place, ((line + one) & 3) * 4 + ((ctx + two) & 3)


def put(target, total, tailed):
    if tailed:
        target[:, :OUT_RIGHT] = total[:, :OUT_RIGHT].astype(BF16)
        target[:, OUT_RIGHT:] = tidy(total[:, OUT_RIGHT:]).astype(BF16)
    else:
        target[...] = total.astype(BF16)


def pair_halves(ids, keep, got, near, far):
    for other in range(4):
        target = far if other % 2 else near
        total = keep[other].astype(F32) + got[other].astype(F32)
        target[other // 2] = total.astype(BF16)


def relay(side, one, three, first, second, to_one, to_three):
    for near in range(4):
        if near < 2:
            total = one[near].astype(F32) + first[near].astype(F32)
            put(to_one.at[near], total, side)
            to_three[near] = three[near]
        else:
            total = three[near].astype(F32) + second[near - 2, :ROWS].astype(F32)
            put(to_three.at[near], total, side)
            to_one[near] = one[near]


def relay_left(ids, *refs):
    relay(0, *refs)


def relay_right(ids, one, three, first, second, left, pair, to_one, to_three, behind):
    relay(1, one, three, first, second, to_one, to_three)
    inside = jnp.where(ids[0, 1] < 3, 1.0, 0.0)
    for chunk in range(D // RIGHT):
        got = second[chunk // 2, ROWS:].astype(F32) * inside
        start = 8 * (chunk % 2)
        behind[:, RIGHT * chunk : RIGHT * chunk + RIGHT] = got[start : start + 8]


def halfway(side, own, one, three, *targets):
    for near, target in enumerate(targets):
        total = own[near].astype(F32) + one[near].astype(F32) + three[near].astype(F32)
        put(target, total, side)


def halfway_left(ids, own, one, three, right, *targets):
    halfway(0, own, one, three, *targets)


def halfway_right(ids, own, one, three, pair, *targets):
    halfway(1, own, one, three, *targets)


def pair_again(ids, near, got, cotangent, hidden, own, second, held, mine, last):
    for index, target in enumerate((own, second)):
        target[...] = (near[index].astype(F32) + got[index].astype(F32)).astype(BF16)
    held[...] = cotangent[...]
    mine[...] = hidden[aligned(ids[0, 2] * SHARE, SHARE)]
    last[...] = hidden[T - RIM :].astype(F32)[8:]


def collect_left(ids, a0, a1, a2, a3, b0, b1, b2, b3, grad_gate, grad_value, grad_out):
    total = sum(part[...].astype(F32) for part in (a0, a1, a2, a3))
    grad_gate[...] = total[:, :WIDE]
    grad_value[...] = total[:, WIDE:]
    grad_out[...] = sum(part[:, :OUT_RIGHT].astype(F32) for part in (b0, b1, b2, b3))


def hidden_back(grads, rows, gain):
    tokens = rows.astype(F32)
    inv = lax.rsqrt(jnp.mean(tokens * tokens, axis=1, keepdims=True) + EPSILON)
    unit = tokens * inv
    scaled = grads * gain
    return inv * (scaled - unit * jnp.mean(scaled * unit, axis=1, keepdims=True)), tokens


def gather_up(
    ids, b0, b1, b2, b3, p0, p1, mine, weights, behind,
    message, gain_out, grad_step, taps, offset, gain, bias, decay, skip, rest,
):
    both = p0[...].astype(F32) + p1[...].astype(F32)
    row = gain_row(weights[:, MIX:])
    gain_out[...] = jnp.broadcast_to(row, (8, D))
    grads, tokens = hidden_back(both[:SHARE], mine[...], row)
    message[:SHARE] = grads.astype(BF16)
    message[SHARE : 2 * SHARE] = (tokens + both[SHARE:]).astype(BF16)
    total = sum(part[:, OUT_RIGHT:].astype(F32) for part in (b0, b1, b2, b3))
    rest[...] = total
    small = unfold(total)
    state = small[7:8]
    lanes = iota((8, 128), 1)
    for tap in range(KERNEL + 1):
        piece = state[:, pair_columns(tap // 2)]
        piece = piece if tap % 2 == 0 else roll(piece, 64, 1)
        if tap == 0:
            rows = jnp.where(iota((8, 128), 0) == 0, roll(piece, STATE_LANE, 1), 0.0)
        else:
            rows = jnp.where(iota((8, 128), 0) == tap, roll(piece, STATE_LANE, 1), rows)
    rest[:8] = jnp.where(lanes < 64, rest[:8], rows)
    for block in range(ROWS // 16):
        message[2 * SHARE :, pair_columns(block)] = rest[16 * block : 16 * block + 16].astype(BF16)
    for block in range(6):
        pair = [behind[:, pair_columns(2 * block + i)] for i in range(2)]
        message[2 * SHARE :, pair_columns(6 + block)] = jnp.concatenate(pair, axis=0).astype(BF16)
    picked = flag(iota((8, 128), 1) == STEP_LANE + iota((8, 128), 0))
    grad_step[...] = pick(picked, total, 1, 1, 3)[:HEADS]
    taps[...] = small[:KERNEL]
    offset[...] = small[KERNEL : KERNEL + 1]
    gain[...] = small[5:6]
    bias[...] = small[6:7, :HEADS]
    decay[...] = small[6:7, 64 : 64 + HEADS]
    skip[...] = small[6:7, 128 : 128 + HEADS]


def finish(ids, *refs):
    pieces, row, cotangent, last = refs[:8], refs[8], refs[9], refs[10]
    grad_hidden, block_out, grad_state, grad_gain, taps, offset, rest, rims = refs[11:]
    chip, core = ids[0, 2] >> 1, ids[0, 2] & 1
    order = []
    for far in range(4):
        start = ((chip - far) & 3) * 2
        order += [(start + core, pieces[far]), (start + 1 - core, pieces[4 + far])]
    for place, piece in order:
        block_out[aligned(place * SHARE, SHARE)] = piece[SHARE : 2 * SHARE]
        for block in range(6):
            part = piece[2 * SHARE :, pair_columns(block)]
            rest[place, 16 * block : 16 * block + 16] = part.astype(F32)
            part = piece[2 * SHARE :, pair_columns(6 + block)].astype(F32)
            rims[place, :, pair_columns(2 * block)] = part[:8]
            rims[place, :, pair_columns(2 * block + 1)] = part[8:]
    total, behind = rest[0], rims[0]
    for i in range(1, 8):
        total = total + rest[i]
        behind = behind + rims[i]
    for place, piece in order:
        rows = aligned(place * SHARE, SHARE)
        grad_hidden[rows] = cotangent[rows].astype(F32) + piece[:SHARE].astype(F32)
    grads, _ = hidden_back(behind, last[...], row[0:1])
    grad_hidden[T - 8 :] = grad_hidden[T - 8 :] + grads
    lanes = iota((ROWS, 128), 1) >> 5
    for half in range(2):
        state = jnp.zeros((ROWS, 128), F32)
        small = jnp.zeros((8, 128), F32)
        for i in range(4):
            one = rest[4 * half + i]
            state = jnp.where(lanes == i, roll(one, PART * i, 1), state)
            small = jnp.where(lanes[:8] == i, roll(one[:8], PART * i - STATE_LANE, 1), small)
        columns = pair_columns(half)
        grad_state[:, columns] = state
        taps[:, columns] = small[:KERNEL]
        offset[:, columns] = small[KERNEL : KERNEL + 1]
    grad_gain[...] = pick(flag(iota((8, 128), 1) == GAIN_LANE), total, 1, 1, 3)[0:1]


def stack_blocks(ids, l0, l1, l2, l3, r0, r1, r2, r3, left, right, rim):
    for i, (one, two) in enumerate(((l0, r0), (l1, r1), (l2, r2), (l3, r3))):
        left[i] = one[:ROWS]
        right[i] = two[...]
    inside = jnp.where(ids[0, 1] > 0, 1.0, 0.0)
    got = l1[ROWS:].astype(F32) * inside
    none = jnp.zeros((8, PAIR), F32)
    rim[:, :PAIR] = jnp.concatenate([none, got[:8]], axis=0).astype(BF16)
    rim[:, PAIR:] = jnp.concatenate([none, got[8:]], axis=0).astype(BF16)


def shift(array, axis, steps):
    return lax.ppermute(array, axis, [(i, (i + steps) % 4) for i in range(4)])


def from_chip(array, steps):
    return lax.ppermute(array, "tp", [(i, (i + 2 * steps) % 8) for i in range(8)])


def across(array, bits):
    return lax.ppermute(array, "tp", [(i, i ^ bits) for i in range(8)])


def around(array, axis):
    return [array] + [shift(array, axis, steps) for steps in range(1, 4)]


def ring_sides(array, axis):
    return shift(array, axis, 1), shift(array, axis, 3)


def ring_rest(array, axis, one, three):
    return [array, one, shift(one[:2], axis, 1), shift(three[2:], axis, 3), three]


def chips_all(array):
    same = [array] + [from_chip(array, steps) for steps in range(1, 4)]
    return same + [across(one, 1) for one in same]


def per_device(
    hidden_states,
    norm_gain,
    gate_weight,
    value_weight,
    state_proj,
    step_proj,
    value_filter,
    value_offset,
    state_filter,
    state_offset,
    step_bias,
    decay_log,
    skip_gain,
    gate_norm_gain,
    out_weight,
    out_grad,
):
    hidden = hidden_states[0]
    cotangent = out_grad[0]
    places = [lax.axis_index(axis).astype(jnp.int32) for axis in ("dp", "ctx", "tp")]
    ids = jnp.stack(places).reshape(1, 3)

    left, longer, right = fuse(
        prepare,
        [((ROWS, PAIR), BF16), ((ROWS + RIM, PAIR), BF16), ((ROWS, PAIR), BF16)],
        ids,
        value_weight,
        gate_weight,
        state_proj,
        step_proj.T,
        norm_gain[None],
        out_weight.T,
        hidden,
        fetch=7,
        rim=True,
    )
    near = [left, shift(longer, "ctx", 1), shift(left, "ctx", 2), shift(left, "ctx", 3)]
    left, right, rim = fuse(
        stack_blocks,
        [((4, ROWS, PAIR), BF16)] * 2 + [((RIM, D), BF16)],
        ids,
        *near,
        *around(right, "dp"),
    )
    consts, units = fuse(
        tabulate,
        [((16, FIRST), F32), ((T, D), F32)],
        ids,
        value_filter,
        state_filter,
        value_offset[None],
        state_offset[None],
        gate_norm_gain[None],
        jnp.stack([step_bias, decay_log, skip_gain]),
        hidden,
        fetch=7,
    )
    left = ring_rest(left, "dp", *ring_sides(left, "dp"))
    right = ring_rest(right, "ctx", *ring_sides(right, "ctx"))
    weights, hidden_in, taken, wide, narrow, message = fuse(
        enter,
        [
            ((D, FIRST), BF16),
            ((EXT, D), BF16),
            ((EXT, MIX), BF16),
            ((T, LOG_DECAY.stop), F32),
            ((T, WEIGHTED.stop), BF16),
            ((STATE + 16, WIDE), BF16),
        ],
        ids,
        *left,
        *right,
        rim,
        units,
        consts,
    )
    messages = around(message, "ctx")[1:]
    gate_out, before, slope, spread = fuse(
        project,
        [((D, 2 * WIDE), BF16), ((T, SKIPPED.stop), F32), ((T, MIX), F32), ((T, STEPS.stop), F32)],
        ids,
        *left,
        *right,
        hidden_in,
        cotangent,
        wide,
        narrow,
        consts,
    )
    state, after, sums = fuse(
        mix,
        [((STATE + 24, WIDE), F32), ((T, MIXED.stop), F32), ((8, T), F32)],
        ids,
        *messages,
        spread,
        narrow,
        before,
    )
    (ready,) = fuse(gate_ready, [((5, T, WIDE), F32)], ids, after, before, consts)
    sums = sums + across(sums, 1)
    gated_low, grad_mixed, grad_gain, sensitivity = fuse(
        gate_back,
        [
            ((T, LOW_GATE.stop), BF16),
            ((T, WIDE), F32),
            ((8, WIDE), F32),
            ((STATE, WIDE), BF16),
        ],
        ids,
        sums,
        *[from_chip(sums, steps) for steps in range(1, 4)],
        ready,
        before,
        spread,
        narrow,
    )
    later = [shift(sensitivity, "ctx", -steps) for steps in range(1, 4)]
    square = ((D, WIDE), BF16)
    gate, out, grads, branch, inner = fuse(
        middle,
        [square, square, ((T, MIX), F32), ((T, D), BF16), ((T, 256), F32)],
        ids,
        hidden_in,
        gated_low,
        cotangent,
        gate_out,
        wide,
        narrow,
        grad_mixed,
        state,
        spread,
        after,
    )
    low, state_low, keep, send, small = fuse(
        leave,
        [((EXT, WIDE + 128), BF16), ((EXT, 2 * STATE), F32)] + [((4, PART, TURNED), F32)] * 2 + [((8, WIDE), F32)],
        ids,
        *later,
        state,
        inner,
        grad_mixed,
        grads,
        wide,
        spread,
        slope,
        narrow,
        consts,
        taken,
        grad_gain,
        scratch=[((2 * STATE, TURNED), F32)],
    )
    pair = fuse(pair_sum, [((PART, TURNED), F32)] * 4, ids, keep, across(send, 1))
    turned = pair[:1] + [from_chip(pair[steps], steps) for steps in range(1, 4)]
    value, head = fuse(
        value_grads,
        [square, ((EXT, D), F32)],
        ids,
        low,
        state_low,
        gated_low,
        weights,
        gate_out,
        hidden_in,
        pair[0],
    )
    both = ((2 * SHARE, D), BF16)
    two = ((2, 2 * SHARE, D), BF16)

    def stage(count, rows, columns):
        return (count, rows, columns), BF16

    def stages(columns, rows):
        whole = stage(4, ROWS, columns)
        return [whole, whole, stage(2, ROWS, columns), stage(2, rows, columns), whole]

    keep, send, *blocks = fuse(
        late_grads,
        [((4, 2 * SHARE, D), BF16)] * 2 + stages(LEFT, ROWS) + stages(RIGHT, ROWS + RIM),
        ids,
        *turned,
        low,
        small,
        head,
        rim,
        units,
        hidden_in,
        gate,
        out,
        value,
        branch,
        scratch=[((D, 128), BF16), ((T, D), BF16)],
    )
    left, right = blocks[:5], blocks[5:]
    near, far = fuse(pair_halves, [two] * 2, ids, keep, across(send, 1))
    sides = fuse(
        relay_left,
        [stage(4, ROWS, LEFT)] * 2,
        ids,
        *(left[1], left[4], shift(left[2], "dp", 1), shift(left[3], "dp", 3)),
    )
    *others, behind = fuse(
        relay_right,
        [stage(4, ROWS, RIGHT)] * 2 + [((8, D), F32)],
        ids,
        *(right[1], right[4], shift(right[2], "ctx", 1), shift(right[3], "ctx", 3)),
        sides[0],
        near,
    )
    sides += others
    left = [left[0], shift(sides[0], "dp", 1), shift(sides[1], "dp", 3)]
    right = [right[0], shift(sides[2], "ctx", 1), shift(sides[3], "ctx", 3)]
    own, second, held, mine, last = fuse(
        pair_again,
        [both, both, ((T, D), BF16), ((SHARE, D), BF16), ((8, D), F32)],
        ids,
        near,
        across(far, 2),
        cotangent,
        hidden,
    )
    right = fuse(halfway_right, [((ROWS, RIGHT), BF16)] * 4, ids, *right, own)
    left = fuse(halfway_left, [((ROWS, LEFT), BF16)] * 4, ids, *left, right[0])
    left = left[:1] + [shift(left[steps], "ctx", steps) for steps in range(1, 4)]
    right = right[:1] + [shift(right[steps], "dp", steps) for steps in range(1, 4)]
    few, line = ((1, HEADS), F32), ((1, WIDE), F32)
    message, gain_full, *few_grads = fuse(
        gather_up,
        [((2 * SHARE + 16, D), BF16), ((8, D), F32), ((HEADS, ROWS), F32), ((KERNEL, WIDE), F32)]
        + [line, line, few, few, few],
        ids,
        *right,
        own,
        across(second, 4),
        mine,
        weights,
        behind,
        scratch=[((ROWS, 128), F32)],
    )
    grad_step, taps, offset, gain, bias, decay, skip = few_grads
    grad_gate, grad_value, grad_out = fuse(
        collect_left, [((ROWS, WIDE), F32)] * 3, ids, *left, *right
    )
    grad_hidden, block_out, grad_state, grad_norm_gain, state_taps, state_offset = fuse(
        finish,
        [
            ((T, D), F32),
            ((T, D), BF16),
            ((ROWS, 2 * STATE), F32),
            ((1, ROWS), F32),
            ((KERNEL, 2 * STATE), F32),
            ((1, 2 * STATE), F32),
        ],
        ids,
        *chips_all(message),
        gain_full,
        held,
        last,
        scratch=[((8, ROWS, 128), F32), ((8, 8, D), F32)],
    )
    return (
        block_out[None],
        grad_hidden[None],
        grad_norm_gain[0],
        grad_gate,
        grad_value,
        grad_state,
        grad_step.T,
        taps,
        offset[0],
        state_taps,
        state_offset[0],
        bias[0],
        decay[0],
        skip[0],
        gain[0],
        grad_out.T,
    )


def solution(mesh):
    line = P(("dp", "ctx"))
    placed = (
        P("dp", "ctx", None),
        line,
        P(("dp", "ctx"), "tp"),
        P(("dp", "ctx"), "tp"),
        P(("dp", "ctx"), None),
        P(("dp", "ctx"), "tp"),
        P(None, "tp"),
        P("tp"),
        P(),
        P(),
        P("tp"),
        P("tp"),
        P("tp"),
        P("tp"),
        P("tp", ("dp", "ctx")),
        P("dp", "ctx", None),
    )
    given = (
        P("dp", "ctx", None),
        P("dp", "ctx", None),
        line,
        P(("dp", "ctx"), "tp"),
        P(("dp", "ctx"), "tp"),
        P(("dp", "ctx"), None),
        P(("dp", "ctx"), "tp"),
        P(None, "tp"),
        P("tp"),
        P(),
        P(),
        P("tp"),
        P("tp"),
        P("tp"),
        P("tp"),
        P("tp", ("dp", "ctx")),
    )
    return jax.shard_map(
        per_device, mesh=mesh, in_specs=placed, out_specs=given, check_vma=False
    )
```
